32 devices in a mesh: dp: 4 (over y, core), expert: 8 (over z, x).
Axes of the slice: x: 2, y: 2, z: 4, core: 2. Of those that a mesh axis runs over, the one named last changes fastest.
Arguments:
- tokens: bfloat16 [128, 4096], P('dp'), may hold values from -6 to 6
- cotangent: bfloat16 [128, 4096], P('dp'), may hold values from -0.29882812 to 0.29882812
- logits: float32 [128, 32], P('dp'), may hold values from 0 to 320
- routes: int32 [128, 8], P('dp'), may hold values from 0 to 31, as said below
- gate_weight: bfloat16 [32, 1536, 4096], P('expert', 'dp'), may hold values from -0.09375 to 0.09375
- up_weight: bfloat16 [32, 1536, 4096], P('expert', 'dp'), may hold values from -0.09375 to 0.09375
- down_weight: bfloat16 [32, 1536, 4096], P('expert', 'dp'), may hold values from -0.15625 to 0.15625
Outputs:
- logit_grad: float32 [128, 32], P('dp')
- router_grad: float32 [4096, 32], P('dp')
The draws below stay inside these ranges and needn't reach their ends.
Inputs may be any that keep to these rules, and one draw needn't show every extreme that they name: `routes`: each row names 8 different experts.
All inputs are finite; a program needn't handle non-finite values.
Results may differ from the reference program's by a relative error of at most 0.0028.
Values may be sent and summed in bfloat16 or wider, within the bound.
No kernel may reach another device: no remote copies, remote signals or barrier semaphores. Data moves between devices by JAX's collectives and lax.ppermute only.
A program may use at most 128 MiB of HBM per device.

```python
import jax
import jax.numpy as jnp
from jax import lax

D = 4096
FF = 1536
TOP = 8
EXPERTS = 32
TOKENS = 128


def pick_routes(key):
    ranks = jax.random.randint(key, (TOKENS, EXPERTS), 0, 65536) * EXPERTS
    ranks = ranks + jnp.arange(EXPERTS, dtype=jnp.int32)[None, :]
    return lax_top(ranks)


def lax_top(ranks):
    return jax.lax.top_k(ranks, TOP)[1].astype(jnp.int32)


def draw_routes(key, part):
    return pick_routes(key)


def draw_logits(key, part):
    picked = pick_routes(key)
    key = jax.random.fold_in(key, 7)
    experts_range = jnp.arange(EXPERTS, dtype=jnp.int32)
    chosen = jnp.sum((picked[:, :, None] == experts_range[None, None, :]).astype(jnp.float32), axis=1)
    base = jnp.clip(0.5 * jax.random.normal(key, (TOKENS, EXPERTS), jnp.float32), -1.0, 1.0)
    return 1.5 + base + 2.0 * chosen


def levels(stream_key, dims, cuts, smallest, high):
    gain = 1.0
    for position, parts in cuts:
        heights = jax.random.uniform(jax.random.fold_in(jax.random.fold_in(stream_key, 6), position), (parts,), jnp.float32, smallest / len(cuts), high / len(cuts))
        gain = gain * jnp.repeat(jnp.exp(heights), dims[position] // parts).reshape((-1,) + (1,) * (len(dims) - 1 - position))
    return gain


def scatter_about(own_key, shape, scale, limit, cuts=(), kind=jnp.bfloat16):
    drawn = jax.random.normal(own_key, shape, jnp.float32) * scale
    if len(cuts) > 0:
        drawn = levels(own_key, shape, cuts, -0.22, 0.18) * drawn
    return jnp.clip(drawn, min=-limit, max=limit).astype(kind)


def setup_inputs(seed: int = 0) -> dict:
    streams_of = jax.random.split(jax.random.key(seed), 8)
    tokens = scatter_about(streams_of[0], (TOKENS, D), 1.0, 6.0, ((0, 4),))
    cotangent = scatter_about(streams_of[1], (TOKENS, D), 0.05, 0.29882812, ((0, 4),))
    logits = draw_logits(jax.random.fold_in(streams_of[7], 71), 0)
    routes = draw_routes(jax.random.fold_in(streams_of[7], 71), 0)
    gate_weight = scatter_about(streams_of[4], (EXPERTS, FF, D), D ** -0.5, 0.09375, ((0, 8), (1, 4)))
    up_weight = scatter_about(streams_of[5], (EXPERTS, FF, D), D ** -0.5, 0.09375, ((0, 8), (1, 4)))
    down_weight = scatter_about(streams_of[6], (EXPERTS, FF, D), FF ** -0.5, 0.15625, ((0, 8), (1, 4)))
    return dict(tokens=tokens, cotangent=cotangent, logits=logits, routes=routes, gate_weight=gate_weight, up_weight=up_weight, down_weight=down_weight)


def expert_scores(tokens, cotangent, weights):
    gate_rows, up_rows, down_rows = weights
    gate_pre = jnp.dot(tokens, gate_rows.T, preferred_element_type=jnp.float32)
    up_pre = jnp.dot(tokens, up_rows.T, preferred_element_type=jnp.float32)
    hidden = jax.nn.silu(gate_pre) * up_pre
    paired = jnp.dot(cotangent, down_rows.T, preferred_element_type=jnp.float32)
    return jnp.sum(hidden * paired, axis=1)


def reference(tokens, cotangent, logits, routes, gate_weight, up_weight, down_weight):
    scores = lax.map(lambda weights: expert_scores(tokens, cotangent, weights), (gate_weight, up_weight, down_weight)).T
    shifted = logits - jnp.max(logits, axis=1, keepdims=True)
    raised = jnp.exp(shifted)
    probs = raised / jnp.sum(raised, axis=1, keepdims=True)
    experts_range = jnp.arange(EXPERTS, dtype=jnp.int32)
    chosen = jnp.sum((routes[:, :, None] == experts_range[None, None, :]).astype(jnp.float32), axis=1)
    mass = jnp.sum(probs * chosen, axis=1, keepdims=True)
    weighted = jnp.sum(probs * chosen * scores, axis=1, keepdims=True)
    prob_grad = scores / mass - chosen * weighted / (mass * mass)
    logit_grad = probs * (prob_grad - jnp.sum(probs * prob_grad, axis=1, keepdims=True))
    grad_bf = logit_grad.astype(jnp.bfloat16)
    router_grad = jnp.dot(tokens.T, grad_bf, preferred_element_type=jnp.float32)
    return logit_grad, router_grad
```

```python
import functools

import jax
import jax.numpy as jnp
from jax import lax
from jax.experimental import pallas as pl
from jax.experimental.pallas import tpu as pltpu
from jax.sharding import PartitionSpec as P

CORES = 2


def dot_rows(a, b):
    return lax.dot_general(a, b, (((1,), (1,)), ((), ())), preferred_element_type=jnp.float32)


def place_rows(pieces, distances, rows):
    me = lax.axis_index("dp")
    tok_dev = pieces[0].shape[0]
    for piece, distance in zip(pieces, distances):
        start = pl.multiple_of(jnp.bitwise_xor(me, distance) * tok_dev, tok_dev)
        rows[pl.ds(start, tok_dev), :] = piece[...]


def start_loads(plan, sources, nears, sems):
    copies, number = [], 0
    for (first, last), source, near in zip(plan, sources, nears):
        for chunk in range(first, last):
            copies.append(pltpu.make_async_copy(source.at[chunk], near.at[chunk - first], sems.at[number]))
            number += 1
    for copy in copies:
        copy.start()
    return copies


def load_kernel(plan, source, after, near, sems):
    for copy in start_loads(plan, [source], [near], sems):
        copy.wait()


def pack_load_kernel(plan, logits, routes, cotangent, source, after, packed, near, *scratch):
    logits_near, routes_near, columns, pack_sems, sems = scratch
    model_width = cotangent.shape[1]
    copies = [
        pltpu.make_async_copy(logits, logits_near, pack_sems.at[0]),
        pltpu.make_async_copy(routes, routes_near, pack_sems.at[1]),
        pltpu.make_async_copy(cotangent, packed.at[:, :model_width], pack_sems.at[2]),
    ]
    for copy in copies:
        copy.start()
    loads = start_loads(plan, [source], [near], sems)
    columns[...] = jnp.zeros(columns.shape, jnp.float32)
    copies[0].wait()
    left = logits_near[...]
    experts_all = left.shape[1]
    for term in range(3):
        rounded = left.astype(jnp.bfloat16).astype(jnp.float32)
        columns[:, term * experts_all : (term + 1) * experts_all] = rounded
        left = left - rounded
    copies[1].wait()
    columns[:, 3 * experts_all : 3 * experts_all + routes.shape[0]] = routes_near[...].astype(jnp.float32).T
    packed[:, model_width:] = columns[...].astype(jnp.bfloat16)
    copies[2].wait()
    for copy in loads:
        copy.wait()


def find_chunk(parts, chunk):
    for first, buffer in reversed(parts):
        if chunk >= first:
            return buffer[chunk - first]


def hidden_chunk(rows, gate_rows, up_rows):
    gate_pre = dot_rows(rows[...], gate_rows)
    up_pre = dot_rows(rows[...], up_rows)
    return gate_pre / (1.0 + jnp.exp(-gate_pre)) * up_pre


def first_hidden_kernel(distances, plan, *refs):
    count = len(distances)
    pieces, refs = refs[:count], refs[count:]
    gate, up, up_far, down_far, hidden, mine, rows, up_near, down_near, sems, mine_sem = refs
    loads = start_loads(plan, [up_far, down_far], [up_near, down_near], sems)
    place_rows(pieces, distances, rows)
    width = mine.shape[1]
    start = pl.multiple_of(lax.axis_index("dp") * width, width)
    own = pltpu.make_async_copy(rows.at[:, pl.ds(start, width)], mine, mine_sem)
    own.start()
    for chunk in range(hidden.shape[0]):
        hidden[chunk] = hidden_chunk(rows, gate[chunk], up[chunk])
    own.wait()
    for copy in loads:
        copy.wait()


def second_hidden_kernel(up_starts, plan, rows, gate, up_0, up_1, down_far, after, hidden, down_near, sems):
    loads = start_loads(plan, [down_far], [down_near], sems)
    up_parts = list(zip(up_starts, (up_0, up_1)))
    for number in range(hidden.shape[0]):
        chunk = plan[0][0] + number
        hidden[number] = hidden_chunk(rows, gate[chunk], find_chunk(up_parts, chunk))
    for copy in loads:
        copy.wait()


def score_kernel(distances, top, *refs):
    count = len(distances)
    pieces, refs = refs[:count], refs[count:]
    hidden, down, partial, probs, chosen, rows, total = refs[:2], refs[2:4], *refs[4:]
    model_width = down[0].shape[2]
    experts_all = probs.shape[0]
    place_rows(pieces, distances, rows)
    packed = rows[:, model_width:].astype(jnp.float32).T
    terms = [packed[term * experts_all : (term + 1) * experts_all] for term in range(3)]
    logits = terms[0] + terms[1] + terms[2]
    raised = jnp.exp(logits - jnp.max(logits, axis=0, keepdims=True))
    probs[...] = raised / jnp.sum(raised, axis=0, keepdims=True)
    number = lax.broadcasted_iota(jnp.int32, logits.shape, 0).astype(jnp.float32)
    named = jnp.zeros(logits.shape, jnp.float32)
    for slot in range(3 * experts_all, 3 * experts_all + top):
        named = named + (packed[slot : slot + 1] == number).astype(jnp.float32)
    chosen[...] = named
    local_experts, _, unit = total.shape
    half, chunks = down[0].shape[0], down[0].shape[0] + down[1].shape[0]
    per_chunk = down[0].shape[1] // unit
    per_expert = chunks * per_chunk // local_experts
    sums = [None] * local_experts
    for chunk in range(chunks):
        side, at = chunk // half, chunk % half
        product = hidden[side][at] * dot_rows(rows[:, :model_width], down[side][at])
        for part in range(per_chunk):
            expert = (chunk * per_chunk + part) // per_expert
            term = product[:, part * unit : (part + 1) * unit]
            sums[expert] = term if sums[expert] is None else sums[expert] + term
    for expert in range(local_experts):
        total[expert] = sums[expert]
        partial[:, expert : expert + 1, :] = jnp.broadcast_to(
            jnp.sum(total[expert].T, axis=0, keepdims=True)[None], (partial.shape[0], 1, partial.shape[2])
        )


def gradient_kernel(data_count, blocks, probs_ref, chosen_ref, mine, logit_grad, router_grad, grads):
    experts_all, total_tokens = probs_ref.shape
    scores = jnp.sum(blocks[...].reshape((data_count, experts_all, total_tokens)), axis=0)
    probs, chosen = probs_ref[...], chosen_ref[...]
    mass = jnp.sum(probs * chosen, axis=0, keepdims=True)
    weighted = jnp.sum(probs * chosen * scores, axis=0, keepdims=True)
    prob_grad = scores / mass - chosen * weighted / (mass * mass)
    grad = probs * (prob_grad - jnp.sum(probs * prob_grad, axis=0, keepdims=True))
    router_grad[...] = jnp.dot(grad.astype(jnp.bfloat16), mine[...], preferred_element_type=jnp.float32)
    grads[...] = grad.T
    tok_dev = logit_grad.shape[0]
    logit_grad[...] = grads[pl.ds(pl.multiple_of(lax.axis_index("dp") * tok_dev, tok_dev), tok_dev), :]


def swap(value, axis, distance):
    return lax.ppermute(value, axis, [(index, index ^ distance) for index in range(lax.axis_size(axis))])


def per_device(tokens, cotangent, logits, routes, gate_weight, up_weight, down_weight):
    data_count = lax.axis_size("dp")
    expert_count = lax.axis_size("expert")
    tok_dev, model_width = tokens.shape
    local_experts, ff_dev = gate_weight.shape[:2]
    total_tokens = tok_dev * data_count
    experts_all = local_experts * expert_count
    top = routes.shape[1]
    unit = 128 if ff_dev % 128 == 0 else ff_dev
    units = local_experts * ff_dev // unit
    chunk_rows = unit * (2 if unit == 128 and units % 2 == 0 else 1)
    chunks = local_experts * ff_dev // chunk_rows
    extra = -(-(3 * experts_all + top) // 128) * 128
    chips = data_count // CORES
    distances = [chip * CORES + core for chip in range(chips) for core in range(CORES)]
    half = chunks // 2
    up_cut = 5 * chunks // 6

    vmem = pl.BlockSpec(memory_space=pltpu.VMEM)
    hbm = pl.BlockSpec(memory_space=pltpu.HBM)
    anywhere = pl.BlockSpec(memory_space=pl.ANY)
    row_bytes = total_tokens * model_width * 2
    chunk_bytes = chunk_rows * model_width * 2
    chunk_flops = 2 * chunk_rows * model_width * total_tokens

    def keep_far(value):
        return pltpu.with_memory_space_constraint(value, pltpu.HBM)

    def near(first, last):
        return pltpu.VMEM((last - first, chunk_rows, model_width), jnp.bfloat16)

    def cost(loads, dots):
        return pl.CostEstimate(flops=dots * chunk_flops, bytes_accessed=loads * chunk_bytes, transcendentals=0)

    def scoped(size):
        return pltpu.CompilerParams(vmem_limit_bytes=size + (2 << 20))

    def load(part, source, after):
        return pl.pallas_call(
            functools.partial(load_kernel, [part]),
            out_shape=near(*part),
            in_specs=[hbm, anywhere],
            out_specs=vmem,
            scratch_shapes=[pltpu.SemaphoreType.DMA((part[1] - part[0],))],
            compiler_params=scoped(0),
            cost_estimate=cost(part[1] - part[0], 0),
            name="load_up",
        )(source, after)

    cut = (chunks, chunk_rows, model_width)
    gate, up, down = (keep_far(weight.reshape(cut)) for weight in (gate_weight, up_weight, down_weight))

    tokens_beside = swap(tokens, "dp", 1)
    tokens_far = [swap(tokens, "dp", chip * CORES) for chip in range(1, chips)]
    packed, gate_near = pl.pallas_call(
        functools.partial(pack_load_kernel, [(0, chunks)]),
        out_shape=(jax.ShapeDtypeStruct((tok_dev, model_width + extra), jnp.bfloat16), near(0, chunks)),
        in_specs=[hbm] * 4 + [anywhere],
        out_specs=(vmem, vmem),
        scratch_shapes=[
            pltpu.VMEM((tok_dev, experts_all), jnp.float32),
            pltpu.VMEM((top, tok_dev), jnp.int32),
            pltpu.VMEM((tok_dev, extra), jnp.float32),
            pltpu.SemaphoreType.DMA((3,)),
            pltpu.SemaphoreType.DMA((chunks,)),
        ],
        compiler_params=scoped(0),
        cost_estimate=cost(chunks, 0),
        name="load_gate_pack",
    )(keep_far(logits), keep_far(routes.T), keep_far(cotangent), gate, tokens_beside)
    packed_far = [swap(packed, "dp", chip * CORES) for chip in range(1, chips)]
    packed_beside = swap(packed, "dp", 1)

    tokens_far, gate_near = lax.optimization_barrier((tokens_far, gate_near))
    token_pieces = [tokens, tokens_beside]
    for far in tokens_far:
        token_pieces += [far, swap(far, "dp", 1)]
    up_0 = load((0, up_cut), up, tokens_far[0])

    plan = [(up_cut, chunks), (0, half)]
    loads = sum(last - first for first, last in plan)
    hidden_0, mine, rows, up_1, down_0 = pl.pallas_call(
        functools.partial(first_hidden_kernel, distances, plan),
        out_shape=(
            jax.ShapeDtypeStruct((half, total_tokens, chunk_rows), jnp.float32),
            jax.ShapeDtypeStruct((total_tokens, model_width // data_count), jnp.bfloat16),
            jax.ShapeDtypeStruct((total_tokens, model_width), jnp.bfloat16),
            near(*plan[0]),
            near(*plan[1]),
        ),
        in_specs=[vmem] * (data_count + 2) + [hbm] * 2,
        out_specs=(vmem,) * 5,
        scratch_shapes=[pltpu.SemaphoreType.DMA((loads,)), pltpu.SemaphoreType.DMA],
        compiler_params=scoped(0),
        cost_estimate=cost(loads, 2 * half),
        name="hidden_first",
    )(*token_pieces, gate_near, up_0, up, down)

    packed_far, hidden_0, rows = lax.optimization_barrier((packed_far, hidden_0, rows))
    packed_pieces = [packed, packed_beside]
    for far in packed_far:
        packed_pieces += [far, swap(far, "dp", 1)]

    plan = [(half, chunks)]
    hidden_1, down_1 = pl.pallas_call(
        functools.partial(second_hidden_kernel, (0, up_cut), plan),
        out_shape=(
            jax.ShapeDtypeStruct((chunks - half, total_tokens, chunk_rows), jnp.float32),
            near(*plan[0]),
        ),
        in_specs=[vmem] * 4 + [hbm, anywhere],
        out_specs=(vmem, vmem),
        scratch_shapes=[pltpu.SemaphoreType.DMA((chunks - half,))],
        compiler_params=scoped(0),
        cost_estimate=cost(chunks - half, 2 * (chunks - half)),
        name="hidden_second",
    )(rows, gate_near, up_0, up_1, down, packed_far[0])

    table = jax.ShapeDtypeStruct((experts_all, total_tokens), jnp.float32)
    partial, probs, chosen = pl.pallas_call(
        functools.partial(score_kernel, distances, top),
        out_shape=(
            jax.ShapeDtypeStruct((data_count * expert_count, local_experts, total_tokens), jnp.float32),
            table,
            table,
        ),
        in_specs=[vmem] * (data_count + 4),
        out_specs=(vmem, vmem, vmem),
        scratch_shapes=[
            pltpu.VMEM((total_tokens, model_width + extra), jnp.bfloat16),
            pltpu.VMEM((local_experts, total_tokens, unit), jnp.float32),
        ],
        compiler_params=scoped(2 * row_bytes),
        cost_estimate=cost(0, chunks),
        name="scores",
    )(*packed_pieces, hidden_0, hidden_1, down_0, down_1)

    score_blocks = lax.all_to_all(partial, ("dp", "expert"), split_axis=0, concat_axis=0, tiled=True)

    logit_grad, router_grad = pl.pallas_call(
        functools.partial(gradient_kernel, data_count),
        out_shape=(
            jax.ShapeDtypeStruct((tok_dev, experts_all), jnp.float32),
            jax.ShapeDtypeStruct((experts_all, model_width // data_count), jnp.float32),
        ),
        in_specs=[vmem] * 4,
        out_specs=(vmem, vmem),
        scratch_shapes=[pltpu.VMEM((total_tokens, experts_all), jnp.float32)],
        compiler_params=scoped(4 << 20),
        name="gradient",
    )(score_blocks, probs, chosen, mine)
    return logit_grad, router_grad.T


def solution(mesh):
    placed = (
        P("dp", None),
        P("dp", None),
        P("dp", None),
        P("dp", None),
        P("expert", "dp", None),
        P("expert", "dp", None),
        P("expert", "dp", None),
    )
    return jax.shard_map(
        per_device,
        mesh=mesh,
        in_specs=placed,
        out_specs=(P("dp", None), P("dp", None)),
        check_vma=False,
    )
```

```python
import functools

import jax
import jax.numpy as jnp
from jax import lax
from jax.experimental import pallas as pl
from jax.experimental.pallas import tpu as pltpu
from jax.sharding import PartitionSpec as P

CORES = 2


def dot_rows(a, b):
    return lax.dot_general(a, b, (((1,), (1,)), ((), ())), preferred_element_type=jnp.float32)


def unit_dots(rows, weights, accs):
    edge = weights[0].shape[0]
    steps = weights[0].shape[1] // edge

    def push(step):
        for unit, weight in enumerate(weights):
            part = weight[:, step * edge : (step + 1) * edge]
            pltpu.matmul_push_rhs(part, step % 2, unit, transpose=True)

    push(0)
    for step in range(steps):
        if step + 1 < steps:
            push(step + 1)
        for acc in accs[: len(weights)]:
            pltpu.matmul_acc_lhs(acc, rows[:, step * edge : (step + 1) * edge], load_staged_rhs=step % 2)
    return [pltpu.matmul_pop(acc) for acc in accs[: len(weights)]]


def with_accs(kernel, shapes):
    if not shapes:
        return kernel

    def body(*refs):
        pl.run_scoped(lambda *accs: kernel(*refs, accs=(accs[:2], accs[2:])), *shapes)

    return body


def pair_dots(rows, weights, accs):
    if accs:
        return unit_dots(rows, weights, accs)
    return [dot_rows(rows[...], weight[...]) for weight in weights]


def place_rows(pieces, distances, rows):
    me = lax.axis_index("dp")
    tok_dev = pieces[0].shape[0]
    for piece, distance in zip(pieces, distances):
        start = pl.multiple_of(jnp.bitwise_xor(me, distance) * tok_dev, tok_dev)
        rows[pl.ds(start, tok_dev), :] = piece[...]


def start_loads(plan, sources, nears, sems):
    copies, number = [], 0
    for (first, last), source, near in zip(plan, sources, nears):
        for chunk in range(first, last):
            copies.append(pltpu.make_async_copy(source.at[chunk], near.at[chunk - first], sems.at[number]))
            number += 1
    for copy in copies:
        copy.start()
    return copies


def load_kernel(plan, source, after, near, sems):
    for copy in start_loads(plan, [source], [near], sems):
        copy.wait()


def pack_load_kernel(plan, logits, routes, cotangent, source, after, packed, near, *scratch):
    logits_near, routes_near, columns, pack_sems, sems = scratch
    model_width = cotangent.shape[1]
    copies = [
        pltpu.make_async_copy(logits, logits_near, pack_sems.at[0]),
        pltpu.make_async_copy(routes, routes_near, pack_sems.at[1]),
        pltpu.make_async_copy(cotangent, packed.at[:, :model_width], pack_sems.at[2]),
    ]
    for copy in copies:
        copy.start()
    loads = start_loads(plan, [source], [near], sems)
    columns[...] = jnp.zeros(columns.shape, jnp.float32)
    copies[0].wait()
    left = logits_near[...]
    experts_all = left.shape[1]
    for term in range(3):
        rounded = left.astype(jnp.bfloat16).astype(jnp.float32)
        columns[:, term * experts_all : (term + 1) * experts_all] = rounded
        left = left - rounded
    copies[1].wait()
    columns[:, 3 * experts_all : 3 * experts_all + routes.shape[0]] = routes_near[...].astype(jnp.float32).T
    packed[:, model_width:] = columns[...].astype(jnp.bfloat16)
    copies[2].wait()
    for copy in loads:
        copy.wait()


def find_chunk(parts, chunk):
    for first, buffer in reversed(parts):
        if chunk >= first:
            return buffer.at[chunk - first]


def hidden_chunk(rows, gate_rows, up_rows, accs):
    gate_pre, up_pre = pair_dots(rows, [gate_rows, up_rows], accs)
    return gate_pre / (1.0 + jnp.exp(-gate_pre)) * up_pre


def first_hidden_kernel(distances, plan, *refs, accs=()):
    count = len(distances)
    pieces, refs = refs[:count], refs[count:]
    gate, up, up_far, down_far, hidden, mine, rows, up_near, down_near, sems, mine_sem = refs
    loads = start_loads(plan, [up_far, down_far], [up_near, down_near], sems)
    place_rows(pieces, distances, rows)
    width = mine.shape[1]
    start = pl.multiple_of(lax.axis_index("dp") * width, width)
    own = pltpu.make_async_copy(rows.at[:, pl.ds(start, width)], mine, mine_sem)
    own.start()
    for chunk in range(hidden.shape[0]):
        hidden[chunk] = hidden_chunk(rows, gate.at[chunk], up.at[chunk], accs and accs[chunk % 2])
    own.wait()
    for copy in loads:
        copy.wait()


def second_hidden_kernel(up_starts, plan, rows, gate, up_0, up_1, down_far, after, hidden, down_near, sems, accs=()):
    loads = start_loads(plan, [down_far], [down_near], sems)
    up_parts = list(zip(up_starts, (up_0, up_1)))
    for number in range(hidden.shape[0]):
        chunk = plan[0][0] + number
        hidden[number] = hidden_chunk(rows, gate.at[chunk], find_chunk(up_parts, chunk), accs and accs[chunk % 2])
    for copy in loads:
        copy.wait()


def score_kernel(distances, top, *refs, accs=()):
    count = len(distances)
    pieces, refs = refs[:count], refs[count:]
    hidden, down, partial, probs, chosen, rows, total = refs[:2], refs[2:4], *refs[4:]
    model_width = down[0].shape[2]
    experts_all = probs.shape[0]
    place_rows(pieces, distances, rows)
    packed = rows[:, model_width:].astype(jnp.float32).T
    terms = [packed[term * experts_all : (term + 1) * experts_all] for term in range(3)]
    logits = terms[0] + terms[1] + terms[2]
    raised = jnp.exp(logits - jnp.max(logits, axis=0, keepdims=True))
    probs[...] = raised / jnp.sum(raised, axis=0, keepdims=True)
    number = lax.broadcasted_iota(jnp.int32, logits.shape, 0).astype(jnp.float32)
    named = jnp.zeros(logits.shape, jnp.float32)
    for slot in range(3 * experts_all, 3 * experts_all + top):
        named = named + (packed[slot : slot + 1] == number).astype(jnp.float32)
    chosen[...] = named
    local_experts, _, unit = total.shape
    half, chunks = down[0].shape[0], down[0].shape[0] + down[1].shape[0]
    per_chunk = down[0].shape[1] // unit
    per_expert = chunks * per_chunk // local_experts
    sums = [None] * local_experts
    near = rows.at[:, :model_width]
    for first in range(0, chunks, 2):
        places = [(chunk // half, chunk % half) for chunk in range(first, min(first + 2, chunks))]
        paired = pair_dots(near, [down[side].at[at] for side, at in places], accs and accs[first // 2 % 2])
        for number, (side, at) in enumerate(places):
            product = hidden[side][at] * paired[number]
            for part in range(per_chunk):
                expert = ((first + number) * per_chunk + part) // per_expert
                term = product[:, part * unit : (part + 1) * unit]
                sums[expert] = term if sums[expert] is None else sums[expert] + term
    for expert in range(local_experts):
        total[expert] = sums[expert]
        partial[:, expert : expert + 1, :] = jnp.broadcast_to(
            jnp.sum(total[expert].T, axis=0, keepdims=True)[None], (partial.shape[0], 1, partial.shape[2])
        )


def add_kernel(parts, copies):
    copies[...] = jnp.broadcast_to(jnp.sum(parts[...], axis=0, keepdims=True), copies.shape)


def gradient_kernel(blocks, probs_ref, chosen_ref, mine, logit_grad, router_grad, grads):
    experts_all, total_tokens = probs_ref.shape
    scores = blocks[...].reshape((experts_all, total_tokens))
    probs, chosen = probs_ref[...], chosen_ref[...]
    mass = jnp.sum(probs * chosen, axis=0, keepdims=True)
    weighted = jnp.sum(probs * chosen * scores, axis=0, keepdims=True)
    prob_grad = scores / mass - chosen * weighted / (mass * mass)
    grad = probs * (prob_grad - jnp.sum(probs * prob_grad, axis=0, keepdims=True))
    router_grad[...] = jnp.dot(grad.astype(jnp.bfloat16), mine[...], preferred_element_type=jnp.float32)
    grads[...] = grad.T
    tok_dev = logit_grad.shape[0]
    logit_grad[...] = grads[pl.ds(pl.multiple_of(lax.axis_index("dp") * tok_dev, tok_dev), tok_dev), :]


def swap(value, axis, distance):
    return lax.ppermute(value, axis, [(index, index ^ distance) for index in range(lax.axis_size(axis))])


def per_device(tokens, cotangent, logits, routes, gate_weight, up_weight, down_weight):
    data_count = lax.axis_size("dp")
    expert_count = lax.axis_size("expert")
    tok_dev, model_width = tokens.shape
    local_experts, ff_dev = gate_weight.shape[:2]
    total_tokens = tok_dev * data_count
    experts_all = local_experts * expert_count
    top = routes.shape[1]
    unit = 128 if ff_dev % 128 == 0 else ff_dev
    units = local_experts * ff_dev // unit
    chunk_rows = unit * (2 if unit == 128 and units % 2 == 0 else 1)
    chunks = local_experts * ff_dev // chunk_rows
    extra = -(-(3 * experts_all + top) // 128) * 128
    chips = data_count // CORES
    distances = [chip * CORES + core for chip in range(chips) for core in range(CORES)]
    half = chunks // 2
    up_cut = 5 * chunks // 6

    vmem = pl.BlockSpec(memory_space=pltpu.VMEM)
    hbm = pl.BlockSpec(memory_space=pltpu.HBM)
    anywhere = pl.BlockSpec(memory_space=pl.ANY)
    row_bytes = total_tokens * model_width * 2
    chunk_bytes = chunk_rows * model_width * 2
    chunk_flops = 2 * chunk_rows * model_width * total_tokens

    def keep_far(value):
        return pltpu.with_memory_space_constraint(value, pltpu.HBM)

    def near(first, last):
        return pltpu.VMEM((last - first, chunk_rows, model_width), jnp.bfloat16)

    def cost(loads, dots):
        return pl.CostEstimate(flops=dots * chunk_flops, bytes_accessed=loads * chunk_bytes, transcendentals=0)

    def scoped(size):
        return pltpu.CompilerParams(vmem_limit_bytes=size + (2 << 20))

    def load(part, source, after):
        return pl.pallas_call(
            functools.partial(load_kernel, [part]),
            out_shape=near(*part),
            in_specs=[hbm, anywhere],
            out_specs=vmem,
            scratch_shapes=[pltpu.SemaphoreType.DMA((part[1] - part[0],))],
            compiler_params=scoped(0),
            cost_estimate=cost(part[1] - part[0], 0),
            name="load_up",
        )(source, after)

    edge = pltpu.get_tpu_info().mxu_column_size
    accs = []
    if chunk_rows == edge and model_width % edge == 0 and total_tokens <= 512:
        accs = [pltpu.ACC(number % 2)((total_tokens, edge), jnp.float32) for number in range(4)]
    cut = (chunks, chunk_rows, model_width)
    gate, up, down = (keep_far(weight.reshape(cut)) for weight in (gate_weight, up_weight, down_weight))

    tokens_beside = swap(tokens, "dp", 1)
    tokens_far = [swap(tokens, "dp", chip * CORES) for chip in range(1, chips)]
    packed, gate_near = pl.pallas_call(
        functools.partial(pack_load_kernel, [(0, chunks)]),
        out_shape=(jax.ShapeDtypeStruct((tok_dev, model_width + extra), jnp.bfloat16), near(0, chunks)),
        in_specs=[hbm] * 4 + [anywhere],
        out_specs=(vmem, vmem),
        scratch_shapes=[
            pltpu.VMEM((tok_dev, experts_all), jnp.float32),
            pltpu.VMEM((top, tok_dev), jnp.int32),
            pltpu.VMEM((tok_dev, extra), jnp.float32),
            pltpu.SemaphoreType.DMA((3,)),
            pltpu.SemaphoreType.DMA((chunks,)),
        ],
        compiler_params=scoped(0),
        cost_estimate=cost(chunks, 0),
        name="load_gate_pack",
    )(keep_far(logits), keep_far(routes.T), keep_far(cotangent), gate, tokens_beside)
    packed_far = [swap(packed, "dp", chip * CORES) for chip in range(1, chips)]
    packed_beside = swap(packed, "dp", 1)

    tokens_far, gate_near = lax.optimization_barrier((tokens_far, gate_near))
    token_pieces = [tokens, tokens_beside]
    for far in tokens_far:
        token_pieces += [far, swap(far, "dp", 1)]
    up_0 = load((0, up_cut), up, tokens_far[0])

    plan = [(up_cut, chunks), (0, half)]
    loads = sum(last - first for first, last in plan)
    hidden_0, mine, rows, up_1, down_0 = pl.pallas_call(
        with_accs(functools.partial(first_hidden_kernel, distances, plan), accs),
        out_shape=(
            jax.ShapeDtypeStruct((half, total_tokens, chunk_rows), jnp.float32),
            jax.ShapeDtypeStruct((total_tokens, model_width // data_count), jnp.bfloat16),
            jax.ShapeDtypeStruct((total_tokens, model_width), jnp.bfloat16),
            near(*plan[0]),
            near(*plan[1]),
        ),
        in_specs=[vmem] * (data_count + 2) + [hbm] * 2,
        out_specs=(vmem,) * 5,
        scratch_shapes=[pltpu.SemaphoreType.DMA((loads,)), pltpu.SemaphoreType.DMA],
        compiler_params=scoped(0),
        cost_estimate=cost(loads, 2 * half),
        name="hidden_first",
    )(*token_pieces, gate_near, up_0, up, down)

    packed_far, hidden_0, rows = lax.optimization_barrier((packed_far, hidden_0, rows))
    packed_pieces = [packed, packed_beside]
    for far in packed_far:
        packed_pieces += [far, swap(far, "dp", 1)]

    plan = [(half, chunks)]
    hidden_1, down_1 = pl.pallas_call(
        with_accs(functools.partial(second_hidden_kernel, (0, up_cut), plan), accs),
        out_shape=(
            jax.ShapeDtypeStruct((chunks - half, total_tokens, chunk_rows), jnp.float32),
            near(*plan[0]),
        ),
        in_specs=[vmem] * 4 + [hbm, anywhere],
        out_specs=(vmem, vmem),
        scratch_shapes=[pltpu.SemaphoreType.DMA((chunks - half,))],
        compiler_params=scoped(0),
        cost_estimate=cost(chunks - half, 2 * (chunks - half)),
        name="hidden_second",
    )(rows, gate_near, up_0, up_1, down, packed_far[0])

    table = jax.ShapeDtypeStruct((experts_all, total_tokens), jnp.float32)
    partial, probs, chosen = pl.pallas_call(
        with_accs(functools.partial(score_kernel, distances, top), accs),
        out_shape=(
            jax.ShapeDtypeStruct((data_count, local_experts, total_tokens), jnp.float32),
            table,
            table,
        ),
        in_specs=[vmem] * (data_count + 4),
        out_specs=(vmem, vmem, vmem),
        scratch_shapes=[
            pltpu.VMEM((total_tokens, model_width + extra), jnp.bfloat16),
            pltpu.VMEM((local_experts, total_tokens, unit), jnp.float32),
        ]
       ,
        compiler_params=scoped(2 * row_bytes),
        cost_estimate=cost(0, chunks),
        name="scores",
    )(*packed_pieces, hidden_0, hidden_1, down_0, down_1)

    parts = lax.all_to_all(partial, "dp", split_axis=0, concat_axis=0, tiled=True)
    summed = pl.pallas_call(
        add_kernel,
        out_shape=jax.ShapeDtypeStruct((expert_count, local_experts, total_tokens), jnp.float32),
        in_specs=[vmem],
        out_specs=vmem,
        compiler_params=scoped(0),
        name="add_parts",
    )(parts)
    score_blocks = lax.all_to_all(summed, "expert", split_axis=0, concat_axis=0, tiled=True)

    logit_grad, router_grad = pl.pallas_call(
        gradient_kernel,
        out_shape=(
            jax.ShapeDtypeStruct((tok_dev, experts_all), jnp.float32),
            jax.ShapeDtypeStruct((experts_all, model_width // data_count), jnp.float32),
        ),
        in_specs=[vmem] * 4,
        out_specs=(vmem, vmem),
        scratch_shapes=[pltpu.VMEM((total_tokens, experts_all), jnp.float32)],
        compiler_params=scoped(4 << 20),
        name="gradient",
    )(score_blocks, probs, chosen, mine)
    return logit_grad, router_grad.T


def solution(mesh):
    placed = (
        P("dp", None),
        P("dp", None),
        P("dp", None),
        P("dp", None),
        P("expert", "dp", None),
        P("expert", "dp", None),
        P("expert", "dp", None),
    )
    mapped = jax.shard_map(
        per_device,
        mesh=mesh,
        in_specs=placed,
        out_specs=(P("dp", None), P("dp", None)),
        check_vma=False,
    )

    def run(*args):
        with jax.sharding.use_abstract_mesh(mesh.abstract_mesh):
            return mapped(*args)

    return run
```

```python
import functools

import jax
import jax.numpy as jnp
from jax import lax
from jax.experimental import pallas as pl
from jax.experimental.pallas import tpu as pltpu
from jax.sharding import PartitionSpec as P

CORES = 2


def dot_rows(a, b):
    return lax.dot_general(a, b, (((1,), (1,)), ((), ())), preferred_element_type=jnp.float32)


def stream_dots(rows, jobs, accs, finish):
    if not accs:
        for number, weights in enumerate(jobs):
            finish(number, [dot_rows(rows[...], weight[...]) for weight in weights])
        return
    edge = jobs[0][0].shape[0]
    order = [(number, step) for number in range(len(jobs)) for step in range(jobs[0][0].shape[1] // edge)]

    def push(at):
        number, step = order[at]
        for unit, weight in enumerate(jobs[number]):
            part = weight[:, step * edge : (step + 1) * edge]
            pltpu.matmul_push_rhs(part, at % 2, unit, transpose=True)

    def pop(number):
        finish(number, [pltpu.matmul_pop(acc) for acc in accs[number % 2][: len(jobs[number])]])

    push(0)
    for at, (number, step) in enumerate(order):
        if at + 1 < len(order):
            push(at + 1)
        for acc in accs[number % 2][: len(jobs[number])]:
            pltpu.matmul_acc_lhs(acc, rows[:, step * edge : (step + 1) * edge], load_staged_rhs=at % 2)
        if step == 1 and number > 0:
            pop(number - 1)
    pop(len(jobs) - 1)


def with_accs(kernel, shapes):
    if not shapes:
        return kernel

    def body(*refs):
        pl.run_scoped(lambda *accs: kernel(*refs, accs=(accs[:2], accs[2:])), *shapes)

    return body


def place_rows(pieces, distances, rows):
    me = lax.axis_index("dp")
    tok_dev = pieces[0].shape[0]
    for piece, distance in zip(pieces, distances):
        start = pl.multiple_of(jnp.bitwise_xor(me, distance) * tok_dev, tok_dev)
        rows[pl.ds(start, tok_dev), :] = piece[...]


def start_loads(plan, sources, nears, sems):
    copies, number = [], 0
    for (first, last), source, near in zip(plan, sources, nears):
        for chunk in range(first, last):
            copies.append(pltpu.make_async_copy(source.at[chunk], near.at[chunk - first], sems.at[number]))
            number += 1
    for copy in copies:
        copy.start()
    return copies


def pack_load_kernel(plan, logits, routes, cotangent, gate, up, after, packed, gate_near, up_near, *scratch):
    logits_near, routes_near, columns, pack_sems, sems = scratch
    model_width = cotangent.shape[1]
    copies = [
        pltpu.make_async_copy(logits, logits_near, pack_sems.at[0]),
        pltpu.make_async_copy(routes, routes_near, pack_sems.at[1]),
        pltpu.make_async_copy(cotangent, packed.at[:, :model_width], pack_sems.at[2]),
    ]
    for copy in copies:
        copy.start()
    loads = start_loads(plan, [gate, up], [gate_near, up_near], sems)
    columns[...] = jnp.zeros(columns.shape, jnp.float32)
    copies[0].wait()
    left = logits_near[...]
    experts_all = left.shape[1]
    for term in range(3):
        rounded = left.astype(jnp.bfloat16).astype(jnp.float32)
        columns[:, term * experts_all : (term + 1) * experts_all] = rounded
        left = left - rounded
    copies[1].wait()
    columns[:, 3 * experts_all : 3 * experts_all + routes.shape[0]] = routes_near[...].astype(jnp.float32).T
    packed[:, model_width:] = columns[...].astype(jnp.bfloat16)
    copies[2].wait()
    for copy in loads:
        copy.wait()


def find_chunk(parts, chunk):
    for first, buffer in reversed(parts):
        if chunk >= first:
            return buffer.at[chunk - first]


def gated(dots):
    gate_pre, up_pre = dots
    return gate_pre / (1.0 + jnp.exp(-gate_pre)) * up_pre


def first_hidden_kernel(distances, plan, *refs, accs=()):
    count = len(distances)
    pieces, refs = refs[:count], refs[count:]
    gate, up, up_far, down_far, hidden, mine, rows, up_near, down_near, sems, mine_sem = refs
    loads = start_loads(plan, [up_far, down_far], [up_near, down_near], sems)
    place_rows(pieces, distances, rows)
    width = mine.shape[1]
    start = pl.multiple_of(lax.axis_index("dp") * width, width)
    own = pltpu.make_async_copy(rows.at[:, pl.ds(start, width)], mine, mine_sem)
    own.start()
    jobs = [[gate.at[chunk], up.at[chunk]] for chunk in range(hidden.shape[0])]

    def finish(number, dots):
        hidden[number] = gated(dots)

    stream_dots(rows, jobs, accs, finish)
    own.wait()
    for copy in loads:
        copy.wait()


def second_hidden_kernel(plan, rows, gate, up, down_far, after, hidden, down_near, sems, accs=()):
    loads = start_loads(plan, [down_far], [down_near], sems)
    first = gate.shape[0] - hidden.shape[0]
    jobs = [[gate.at[first + chunk], up.at[chunk]] for chunk in range(hidden.shape[0])]

    def finish(number, dots):
        hidden[number] = gated(dots)

    stream_dots(rows, jobs, accs, finish)
    for copy in loads:
        copy.wait()


def score_kernel(distances, top, down_starts, *refs, accs=()):
    count = len(distances)
    pieces, refs = refs[:count], refs[count:]
    hidden_0, hidden_1, down_0, down_1, partial, probs, chosen, rows, total = refs
    model_width = down_0.shape[2]
    experts_all = probs.shape[0]
    place_rows(pieces, distances, rows)
    local_experts, _, unit = total.shape
    half = hidden_0.shape[0]
    chunks = half + hidden_1.shape[0]
    per_chunk = down_0.shape[1] // unit
    per_expert = chunks * per_chunk // local_experts
    hidden_parts = [(0, hidden_0), (half, hidden_1)]
    down_parts = list(zip(down_starts, (down_0, down_1)))
    jobs = [
        [find_chunk(down_parts, chunk) for chunk in range(first, min(first + 2, chunks))]
        for first in range(0, chunks, 2)
    ]
    sums = [None] * local_experts

    def routing():
        packed = rows[:, model_width:].astype(jnp.float32).T
        terms = [packed[term * experts_all : (term + 1) * experts_all] for term in range(3)]
        logits = terms[0] + terms[1] + terms[2]
        raised = jnp.exp(logits - jnp.max(logits, axis=0, keepdims=True))
        probs[...] = raised / jnp.sum(raised, axis=0, keepdims=True)
        number = lax.broadcasted_iota(jnp.int32, logits.shape, 0).astype(jnp.float32)
        named = jnp.zeros(logits.shape, jnp.float32)
        for slot in range(3 * experts_all, 3 * experts_all + top):
            named = named + (packed[slot : slot + 1] == number).astype(jnp.float32)
        chosen[...] = named

    def finish(number, dots):
        if number == 0:
            routing()
        for side, paired in enumerate(dots):
            chunk = 2 * number + side
            product = find_chunk(hidden_parts, chunk)[...] * paired
            for part in range(per_chunk):
                expert = (chunk * per_chunk + part) // per_expert
                term = product[:, part * unit : (part + 1) * unit]
                sums[expert] = term if sums[expert] is None else sums[expert] + term

    stream_dots(rows.at[:, :model_width], jobs, accs, finish)
    for expert in range(local_experts):
        total[expert] = sums[expert]
    lines = [jnp.sum(total[expert].T, axis=0, keepdims=True) for expert in range(local_experts)]
    partial[...] = jnp.concatenate(lines, axis=0)


def joined(distance, held, other):
    second = jnp.bitwise_and(lax.axis_index("expert"), distance) != 0
    return jnp.concatenate([jnp.where(second, other, held), jnp.where(second, held, other)], axis=0)


def join_kernel(distance, held, other, both):
    both[...] = joined(distance, held[...], other[...])


def gradient_kernel(distance, held, other, probs_ref, chosen_ref, mine, logit_grad, router_grad, grads):
    scores = joined(distance, held[...], other[...])
    probs, chosen = probs_ref[...], chosen_ref[...]
    mass = jnp.sum(probs * chosen, axis=0, keepdims=True)
    weighted = jnp.sum(probs * chosen * scores, axis=0, keepdims=True)
    prob_grad = scores / mass - chosen * weighted / (mass * mass)
    grad = probs * (prob_grad - jnp.sum(probs * prob_grad, axis=0, keepdims=True))
    router_grad[...] = jnp.dot(grad.astype(jnp.bfloat16), mine[...], preferred_element_type=jnp.float32)
    grads[...] = grad.T
    tok_dev = logit_grad.shape[0]
    logit_grad[...] = grads[pl.ds(pl.multiple_of(lax.axis_index("dp") * tok_dev, tok_dev), tok_dev), :]


def swap(value, axis, distance):
    return lax.ppermute(value, axis, [(index, index ^ distance) for index in range(lax.axis_size(axis))])


def per_device(tokens, cotangent, logits, routes, gate_weight, up_weight, down_weight):
    data_count = lax.axis_size("dp")
    expert_count = lax.axis_size("expert")
    tok_dev, model_width = tokens.shape
    local_experts, ff_dev = gate_weight.shape[:2]
    total_tokens = tok_dev * data_count
    experts_all = local_experts * expert_count
    top = routes.shape[1]
    unit = 128 if ff_dev % 128 == 0 else ff_dev
    units = local_experts * ff_dev // unit
    chunk_rows = unit * (2 if unit == 128 and units % 2 == 0 else 1)
    chunks = local_experts * ff_dev // chunk_rows
    extra = -(-(3 * experts_all + top) // 128) * 128
    chips = data_count // CORES
    distances = [chip * CORES + core for chip in range(chips) for core in range(CORES)]
    half = chunks // 2
    down_cut = max(1, chunks // 6)

    vmem = pl.BlockSpec(memory_space=pltpu.VMEM)
    hbm = pl.BlockSpec(memory_space=pltpu.HBM)
    anywhere = pl.BlockSpec(memory_space=pl.ANY)
    row_bytes = total_tokens * model_width * 2

    def keep_far(value):
        return pltpu.with_memory_space_constraint(value, pltpu.HBM)

    def near(first, last):
        return pltpu.VMEM((last - first, chunk_rows, model_width), jnp.bfloat16)

    def cost(loads, dots):
        return pl.CostEstimate(flops=dots, bytes_accessed=loads, transcendentals=0)

    def scoped(size):
        return pltpu.CompilerParams(vmem_limit_bytes=size + (2 << 20))

    edge = pltpu.get_tpu_info().mxu_column_size
    accs = []
    if chunk_rows == edge and model_width % edge == 0 and total_tokens <= 512:
        accs = [pltpu.ACC(number % 2)((total_tokens, edge), jnp.float32) for number in range(4)]
    cut = (chunks, chunk_rows, model_width)
    gate, up, down = (keep_far(weight.reshape(cut)) for weight in (gate_weight, up_weight, down_weight))

    tokens_beside = swap(tokens, "dp", 1)
    tokens_far = [swap(tokens, "dp", chip * CORES) for chip in range(1, chips)]
    plan = [(0, chunks), (0, half)]
    loads = chunks + half
    packed, gate_near, up_0 = pl.pallas_call(
        functools.partial(pack_load_kernel, plan),
        out_shape=(
            jax.ShapeDtypeStruct((tok_dev, model_width + extra), jnp.bfloat16),
            near(*plan[0]),
            near(*plan[1]),
        ),
        in_specs=[hbm] * 5 + [anywhere],
        out_specs=(vmem,) * 3,
        scratch_shapes=[
            pltpu.VMEM((tok_dev, experts_all), jnp.float32),
            pltpu.VMEM((top, tok_dev), jnp.int32),
            pltpu.VMEM((tok_dev, extra), jnp.float32),
            pltpu.SemaphoreType.DMA((3,)),
            pltpu.SemaphoreType.DMA((loads,)),
        ],
        compiler_params=scoped(0),
        cost_estimate=cost(loads, 0),
        name="load_pack",
    )(keep_far(logits), keep_far(routes.T), keep_far(cotangent), gate, up, tokens_beside)
    packed_far = [swap(packed, "dp", chip * CORES) for chip in range(1, chips)]
    packed_beside = swap(packed, "dp", 1)

    tokens_far, gate_near, up_0 = lax.optimization_barrier((tokens_far, gate_near, up_0))
    token_pieces = [tokens, tokens_beside]
    for far in tokens_far:
        token_pieces += [far, swap(far, "dp", 1)]

    plan = [(half, chunks), (0, down_cut)]
    loads = sum(last - first for first, last in plan)
    hidden_0, mine, rows, up_1, down_0 = pl.pallas_call(
        with_accs(functools.partial(first_hidden_kernel, distances, plan), accs),
        out_shape=(
            jax.ShapeDtypeStruct((half, total_tokens, chunk_rows), jnp.float32),
            jax.ShapeDtypeStruct((total_tokens, model_width // data_count), jnp.bfloat16),
            jax.ShapeDtypeStruct((total_tokens, model_width), jnp.bfloat16),
            near(*plan[0]),
            near(*plan[1]),
        ),
        in_specs=[vmem] * (data_count + 2) + [hbm] * 2,
        out_specs=(vmem,) * 5,
        scratch_shapes=[pltpu.SemaphoreType.DMA((loads,)), pltpu.SemaphoreType.DMA],
        compiler_params=scoped(0),
        cost_estimate=cost(loads, 2 * half),
        name="hidden_first",
    )(*token_pieces, gate_near, up_0, up, down)

    packed_far, hidden_0, rows = lax.optimization_barrier((packed_far, hidden_0, rows))
    packed_pieces = [packed, packed_beside]
    for far in packed_far:
        packed_pieces += [far, swap(far, "dp", 1)]

    plan = [(down_cut, chunks)]
    hidden_1, down_1 = pl.pallas_call(
        with_accs(functools.partial(second_hidden_kernel, plan), accs),
        out_shape=(
            jax.ShapeDtypeStruct((chunks - half, total_tokens, chunk_rows), jnp.float32),
            near(*plan[0]),
        ),
        in_specs=[vmem] * 3 + [hbm, anywhere],
        out_specs=(vmem, vmem),
        scratch_shapes=[pltpu.SemaphoreType.DMA((chunks - down_cut,))],
        compiler_params=scoped(0),
        cost_estimate=cost(chunks - down_cut, 2 * (chunks - half)),
        name="hidden_second",
    )(rows, gate_near, up_1, down, packed_far[0])

    table = jax.ShapeDtypeStruct((experts_all, total_tokens), jnp.float32)
    partial, probs, chosen = pl.pallas_call(
        with_accs(functools.partial(score_kernel, distances, top, (0, down_cut)), accs),
        out_shape=(
            jax.ShapeDtypeStruct((local_experts, total_tokens), jnp.float32),
            table,
            table,
        ),
        in_specs=[vmem] * (data_count + 4),
        out_specs=(vmem, vmem, vmem),
        scratch_shapes=[
            pltpu.VMEM((total_tokens, model_width + extra), jnp.bfloat16),
            pltpu.VMEM((local_experts, total_tokens, unit), jnp.float32),
        ]
       ,
        compiler_params=scoped(2 * row_bytes),
        cost_estimate=cost(0, chunks),
        name="scores",
    )(*packed_pieces, hidden_0, hidden_1, down_0, down_1)

    scores = partial
    distance = 1
    while distance < data_count:
        scores = scores + swap(scores, "dp", distance)
        distance *= 2
    distance = 1
    while 2 * distance < expert_count:
        rows_held = distance * local_experts
        scores = pl.pallas_call(
            functools.partial(join_kernel, distance),
            out_shape=jax.ShapeDtypeStruct((2 * rows_held, total_tokens), jnp.float32),
            in_specs=[vmem] * 2,
            out_specs=vmem,
            compiler_params=scoped(0),
            cost_estimate=cost(1, 1),
            name="join_scores",
        )(scores, swap(scores, "expert", distance))
        distance *= 2
    others = swap(scores, "expert", distance)

    logit_grad, router_grad = pl.pallas_call(
        functools.partial(gradient_kernel, distance),
        out_shape=(
            jax.ShapeDtypeStruct((tok_dev, experts_all), jnp.float32),
            jax.ShapeDtypeStruct((experts_all, model_width // data_count), jnp.float32),
        ),
        in_specs=[vmem] * 5,
        out_specs=(vmem, vmem),
        scratch_shapes=[pltpu.VMEM((total_tokens, experts_all), jnp.float32)],
        compiler_params=scoped(4 << 20),
        name="gradient",
    )(scores, others, probs, chosen, mine)
    return logit_grad, router_grad.T


def solution(mesh):
    placed = (
        P("dp", None),
        P("dp", None),
        P("dp", None),
        P("dp", None),
        P("expert", "dp", None),
        P("expert", "dp", None),
        P("expert", "dp", None),
    )
    mapped = jax.shard_map(
        per_device,
        mesh=mesh,
        in_specs=placed,
        out_specs=(P("dp", None), P("dp", None)),
        check_vma=False,
    )

    def run(*args):
        with jax.sharding.use_abstract_mesh(mesh.abstract_mesh):
            return mapped(*args)

    return run
```

```python
import functools

import jax
import jax.numpy as jnp
from jax import lax
from jax.experimental import pallas as pl
from jax.experimental.pallas import tpu as pltpu
from jax.sharding import PartitionSpec as P

CORES = 2


def dot_rows(a, b):
    return lax.dot_general(a, b, (((1,), (1,)), ((), ())), preferred_element_type=jnp.float32)


def stream_dots(rows, lanes, accs, finish):
    places = len(lanes[0])
    if not accs:
        for place in range(places):
            finish(place, [dot_rows(lane[place][...], rows[...]) for lane in lanes])
        return
    total_tokens, edge = rows.shape[0], accs[0][0].shape[1]
    steps = rows.shape[1] // edge

    def push(step):
        part = rows[:, step * edge : (step + 1) * edge]
        both = jnp.concatenate([part] * (edge // total_tokens), axis=0)
        for unit in range(len(lanes)):
            pltpu.matmul_push_rhs(both, step % 2, unit, transpose=True)

    push(0)
    for step in range(steps):
        for place in range(places):
            for lane, acc in zip(lanes, accs):
                part = lane[place][:, step * edge : (step + 1) * edge]
                pltpu.matmul_acc_lhs(acc[place], part, load_staged_rhs=step % 2 if place == 0 else None)
            if place == 0 and step + 1 < steps:
                push(step + 1)
    for place in range(places):
        finish(place, [pltpu.matmul_pop(acc[place])[:, :total_tokens] for acc in accs])


def with_accs(kernel, shapes):
    if not shapes:
        return kernel
    half = len(shapes) // 2

    def body(*refs):
        pl.run_scoped(lambda *accs: kernel(*refs, accs=(accs[:half], accs[half:])), *shapes)

    return body


def place_rows(pieces, distances, rows):
    me = lax.axis_index("dp")
    tok_dev = pieces[0].shape[0]
    for piece, distance in zip(pieces, distances):
        start = pl.multiple_of(jnp.bitwise_xor(me, distance) * tok_dev, tok_dev)
        rows[pl.ds(start, tok_dev), :] = piece[...]


def start_loads(plan, sources, nears, sems):
    copies, number = [], 0
    for (first, last), source, near in zip(plan, sources, nears):
        for chunk in range(first, last):
            copies.append(pltpu.make_async_copy(source.at[chunk], near.at[chunk - first], sems.at[number]))
            number += 1
    for copy in copies:
        copy.start()
    return copies


def pack_kernel(logits, routes, cotangent, packed, logits_near, routes_near, columns, sems):
    model_width = cotangent.shape[1]
    copies = [
        pltpu.make_async_copy(logits, logits_near, sems.at[0]),
        pltpu.make_async_copy(routes, routes_near, sems.at[1]),
        pltpu.make_async_copy(cotangent, packed.at[:, :model_width], sems.at[2]),
    ]
    for copy in copies:
        copy.start()
    columns[...] = jnp.zeros(columns.shape, jnp.float32)
    copies[0].wait()
    left = logits_near[...]
    experts_all = left.shape[1]
    for term in range(3):
        rounded = left.astype(jnp.bfloat16).astype(jnp.float32)
        columns[:, term * experts_all : (term + 1) * experts_all] = rounded
        left = left - rounded
    copies[1].wait()
    columns[:, 3 * experts_all : 3 * experts_all + routes.shape[0]] = routes_near[...].astype(jnp.float32).T
    packed[:, model_width:] = columns[...].astype(jnp.bfloat16)
    copies[2].wait()


def load_kernel(plan, gate, up, after, gate_near, up_near, sems):
    for copy in start_loads(plan, [gate, up], [gate_near, up_near], sems):
        copy.wait()


def blocks_of(buffers, unit):
    return [
        buffer.at[chunk, first : first + unit]
        for buffer in buffers
        for chunk in range(buffer.shape[0])
        for first in range(0, buffer.shape[1], unit)
    ]


def gated(dots):
    gate_pre, up_pre = dots
    return gate_pre / (1.0 + jnp.exp(-gate_pre)) * up_pre


def first_hidden_kernel(distances, plan, *refs, accs=()):
    count = len(distances)
    pieces, refs = refs[:count], refs[count:]
    gate, up, up_far, down_far, hidden, mine, rows, up_near, down_near, sems, mine_sem = refs
    loads = start_loads(plan, [up_far, down_far], [up_near, down_near], sems)
    place_rows(pieces, distances, rows)
    width = mine.shape[1]
    start = pl.multiple_of(lax.axis_index("dp") * width, width)
    own = pltpu.make_async_copy(rows.at[:, pl.ds(start, width)], mine, mine_sem)
    own.start()
    places, unit = hidden.shape[:2]
    lanes = [blocks_of([gate], unit)[:places], blocks_of([up], unit)]

    def finish(place, dots):
        hidden[place] = gated(dots)

    stream_dots(rows, lanes, accs, finish)
    own.wait()
    for copy in loads:
        copy.wait()


def second_hidden_kernel(plan, rows, gate, up, down_far, after, hidden, down_near, sems, accs=()):
    loads = start_loads(plan, [down_far], [down_near], sems)
    places, unit = hidden.shape[:2]
    lanes = [blocks_of([gate], unit)[-places:], blocks_of([up], unit)]

    def finish(place, dots):
        hidden[place] = gated(dots)

    stream_dots(rows, lanes, accs, finish)
    for copy in loads:
        copy.wait()


def score_kernel(distances, top, *refs, accs=()):
    count = len(distances)
    pieces, refs = refs[:count], refs[count:]
    hidden_0, hidden_1, down_0, down_1, partial, probs, chosen, rows = refs
    model_width = down_0.shape[2]
    experts_all = probs.shape[0]
    place_rows(pieces, distances, rows)
    local_experts = partial.shape[1]
    unit = hidden_0.shape[1]
    blocks = blocks_of([down_0, down_1], unit)
    places = len(blocks) // 2
    per_expert = len(blocks) // local_experts
    sums = [None] * local_experts

    def routing():
        packed = rows[:, model_width:].astype(jnp.float32).T
        terms = [packed[term * experts_all : (term + 1) * experts_all] for term in range(3)]
        logits = terms[0] + terms[1] + terms[2]
        raised = jnp.exp(logits - jnp.max(logits, axis=0, keepdims=True))
        probs[...] = raised / jnp.sum(raised, axis=0, keepdims=True)
        number = lax.broadcasted_iota(jnp.int32, logits.shape, 0).astype(jnp.float32)
        named = jnp.zeros(logits.shape, jnp.float32)
        for slot in range(3 * experts_all, 3 * experts_all + top):
            named = named + (packed[slot : slot + 1] == number).astype(jnp.float32)
        chosen[...] = named

    def finish(place, dots):
        for held, block, paired in zip((hidden_0, hidden_1), (place, places + place), dots):
            product = held[place] * paired
            expert = block // per_expert
            sums[expert] = product if sums[expert] is None else sums[expert] + product

    routing()
    stream_dots(rows.at[:, :model_width], [blocks[:places], blocks[places:]], accs, finish)
    lines = [jnp.sum(term, axis=0, keepdims=True) for term in sums]
    partial[...] = jnp.broadcast_to(jnp.concatenate(lines, axis=0)[None], partial.shape)


def gradient_kernel(data_count, blocks, probs_ref, chosen_ref, mine, logit_grad, router_grad, grads):
    experts_all, total_tokens = probs_ref.shape
    scores = jnp.sum(blocks[...].reshape((data_count, experts_all, total_tokens)), axis=0)
    probs, chosen = probs_ref[...], chosen_ref[...]
    mass = jnp.sum(probs * chosen, axis=0, keepdims=True)
    weighted = jnp.sum(probs * chosen * scores, axis=0, keepdims=True)
    prob_grad = scores / mass - chosen * weighted / (mass * mass)
    grad = probs * (prob_grad - jnp.sum(probs * prob_grad, axis=0, keepdims=True))
    router_grad[...] = jnp.dot(grad.astype(jnp.bfloat16), mine[...], preferred_element_type=jnp.float32)
    grads[...] = grad.T
    tok_dev = logit_grad.shape[0]
    logit_grad[...] = grads[pl.ds(pl.multiple_of(lax.axis_index("dp") * tok_dev, tok_dev), tok_dev), :]


def swap(value, axis, distance):
    return lax.ppermute(value, axis, [(index, index ^ distance) for index in range(lax.axis_size(axis))])


def per_device(tokens, cotangent, logits, routes, gate_weight, up_weight, down_weight):
    data_count = lax.axis_size("dp")
    expert_count = lax.axis_size("expert")
    tok_dev, model_width = tokens.shape
    local_experts, ff_dev = gate_weight.shape[:2]
    total_tokens = tok_dev * data_count
    experts_all = local_experts * expert_count
    top = routes.shape[1]
    unit = 128 if ff_dev % 128 == 0 else ff_dev
    units = local_experts * ff_dev // unit
    chunk_rows = unit * (2 if unit == 128 and units % 2 == 0 else 1)
    chunks = local_experts * ff_dev // chunk_rows
    extra = -(-(3 * experts_all + top) // 128) * 128
    chips = data_count // CORES
    distances = [chip * CORES + core for chip in range(chips) for core in range(CORES)]
    half = chunks // 2
    down_cut = max(1, chunks // 6)

    vmem = pl.BlockSpec(memory_space=pltpu.VMEM)
    hbm = pl.BlockSpec(memory_space=pltpu.HBM)
    anywhere = pl.BlockSpec(memory_space=pl.ANY)
    row_bytes = total_tokens * model_width * 2

    def keep_far(value):
        return pltpu.with_memory_space_constraint(value, pltpu.HBM)

    def near(first, last):
        return pltpu.VMEM((last - first, chunk_rows, model_width), jnp.bfloat16)

    def roomy():
        return scoped(0 if accs else 2 * row_bytes)

    def cost(loads, dots):
        return pl.CostEstimate(flops=dots, bytes_accessed=loads, transcendentals=0)

    def scoped(size):
        return pltpu.CompilerParams(vmem_limit_bytes=size + (2 << 20))

    edge = pltpu.get_tpu_info().mxu_column_size
    accs = []
    places = half * chunk_rows // unit
    if edge == 2 * total_tokens and model_width % edge == 0 and 2 * half == chunks and places * unit <= 1024:
        accs = [pltpu.ACC(number)((unit, edge), jnp.float32) for number in range(2) for _ in range(places)]
    cut = (chunks, chunk_rows, model_width)
    gate, up, down = (keep_far(weight.reshape(cut)) for weight in (gate_weight, up_weight, down_weight))

    tokens_beside = swap(tokens, "dp", 1)
    tokens_far = [swap(tokens, "dp", chip * CORES) for chip in range(1, chips)]
    packed = pl.pallas_call(
        pack_kernel,
        out_shape=jax.ShapeDtypeStruct((tok_dev, model_width + extra), jnp.bfloat16),
        in_specs=[hbm] * 3,
        out_specs=vmem,
        scratch_shapes=[
            pltpu.VMEM((tok_dev, experts_all), jnp.float32),
            pltpu.VMEM((top, tok_dev), jnp.int32),
            pltpu.VMEM((tok_dev, extra), jnp.float32),
            pltpu.SemaphoreType.DMA((3,)),
        ],
        compiler_params=scoped(0),
        cost_estimate=cost(1, 0),
        name="pack",
    )(keep_far(logits), keep_far(routes.T), keep_far(cotangent))
    packed_far = [swap(packed, "dp", chip * CORES) for chip in range(1, chips)]
    packed_beside = swap(packed, "dp", 1)
    plan = [(0, chunks), (0, half)]
    gate_near, up_0 = pl.pallas_call(
        functools.partial(load_kernel, plan),
        out_shape=(near(*plan[0]), near(*plan[1])),
        in_specs=[hbm, hbm, anywhere],
        out_specs=(vmem, vmem),
        scratch_shapes=[pltpu.SemaphoreType.DMA((chunks + half,))],
        compiler_params=scoped(0),
        cost_estimate=cost(chunks + half, 0),
        name="load",
    )(gate, up, packed)

    tokens_far, gate_near, up_0 = lax.optimization_barrier((tokens_far, gate_near, up_0))
    token_pieces = [tokens, tokens_beside]
    for far in tokens_far:
        token_pieces += [far, swap(far, "dp", 1)]

    plan = [(half, chunks), (0, down_cut)]
    loads = sum(last - first for first, last in plan)
    hidden_0, mine, rows, up_1, down_0 = pl.pallas_call(
        with_accs(functools.partial(first_hidden_kernel, distances, plan), accs),
        out_shape=(
            jax.ShapeDtypeStruct((places, unit, total_tokens), jnp.float32),
            jax.ShapeDtypeStruct((total_tokens, model_width // data_count), jnp.bfloat16),
            jax.ShapeDtypeStruct((total_tokens, model_width), jnp.bfloat16),
            near(*plan[0]),
            near(*plan[1]),
        ),
        in_specs=[vmem] * (data_count + 2) + [hbm] * 2,
        out_specs=(vmem,) * 5,
        scratch_shapes=[pltpu.SemaphoreType.DMA((loads,)), pltpu.SemaphoreType.DMA],
        compiler_params=roomy(),
        cost_estimate=cost(loads, 2 * half),
        name="hidden_first",
    )(*token_pieces, gate_near, up_0, up, down)

    packed_far, hidden_0, rows = lax.optimization_barrier((packed_far, hidden_0, rows))
    packed_pieces = [packed, packed_beside]
    for far in packed_far:
        packed_pieces += [far, swap(far, "dp", 1)]

    plan = [(down_cut, chunks)]
    hidden_1, down_1 = pl.pallas_call(
        with_accs(functools.partial(second_hidden_kernel, plan), accs),
        out_shape=(
            jax.ShapeDtypeStruct((units - places, unit, total_tokens), jnp.float32),
            near(*plan[0]),
        ),
        in_specs=[vmem] * 3 + [hbm, anywhere],
        out_specs=(vmem, vmem),
        scratch_shapes=[pltpu.SemaphoreType.DMA((chunks - down_cut,))],
        compiler_params=roomy(),
        cost_estimate=cost(chunks - down_cut, 2 * (chunks - half)),
        name="hidden_second",
    )(rows, gate_near, up_1, down, packed_far[0])

    table = jax.ShapeDtypeStruct((experts_all, total_tokens), jnp.float32)
    partial, probs, chosen = pl.pallas_call(
        with_accs(functools.partial(score_kernel, distances, top), accs),
        out_shape=(
            jax.ShapeDtypeStruct((data_count * expert_count, local_experts, total_tokens), jnp.float32),
            table,
            table,
        ),
        in_specs=[vmem] * (data_count + 4),
        out_specs=(vmem, vmem, vmem),
        scratch_shapes=[
            pltpu.VMEM((total_tokens, model_width + extra), jnp.bfloat16),
        ]
       ,
        compiler_params=scoped(2 * row_bytes),
        cost_estimate=cost(0, chunks),
        name="scores",
    )(*packed_pieces, hidden_0, hidden_1, down_0, down_1)

    score_blocks = lax.all_to_all(partial, ("dp", "expert"), split_axis=0, concat_axis=0, tiled=True)

    logit_grad, router_grad = pl.pallas_call(
        functools.partial(gradient_kernel, data_count),
        out_shape=(
            jax.ShapeDtypeStruct((tok_dev, experts_all), jnp.float32),
            jax.ShapeDtypeStruct((experts_all, model_width // data_count), jnp.float32),
        ),
        in_specs=[vmem] * 4,
        out_specs=(vmem, vmem),
        scratch_shapes=[pltpu.VMEM((total_tokens, experts_all), jnp.float32)],
        compiler_params=scoped(4 << 20),
        name="gradient",
    )(score_blocks, probs, chosen, mine)
    return logit_grad, router_grad.T


def solution(mesh):
    placed = (
        P("dp", None),
        P("dp", None),
        P("dp", None),
        P("dp", None),
        P("expert", "dp", None),
        P("expert", "dp", None),
        P("expert", "dp", None),
    )
    mapped = jax.shard_map(
        per_device,
        mesh=mesh,
        in_specs=placed,
        out_specs=(P("dp", None), P("dp", None)),
        check_vma=False,
    )

    def run(*args):
        with jax.sharding.use_abstract_mesh(mesh.abstract_mesh):
            return mapped(*args)

    return run
```

```python
import functools

import jax
import jax.numpy as jnp
from jax import lax
from jax.experimental import pallas as pl
from jax.experimental.pallas import tpu as pltpu
from jax.sharding import PartitionSpec as P

CORES = 2


def dot_rows(a, b):
    return lax.dot_general(a, b, (((1,), (1,)), ((), ())), preferred_element_type=jnp.float32)


def stream_dots(rows, lanes, accs, finish):
    places = len(lanes[0])
    if not accs:
        for place in range(places):
            finish(place, [dot_rows(lane[place][...], rows[...]) for lane in lanes])
        return
    total_tokens, edge = rows.shape[0], accs[0][0].shape[1]
    steps = rows.shape[1] // edge

    def push(step):
        part = rows[:, step * edge : (step + 1) * edge]
        both = jnp.concatenate([part] * (edge // total_tokens), axis=0)
        for unit in range(len(lanes)):
            pltpu.matmul_push_rhs(both, step % 2, unit, transpose=True)

    push(0)
    for step in range(steps):
        for place in range(places):
            for lane, acc in zip(lanes, accs):
                part = lane[place][:, step * edge : (step + 1) * edge]
                pltpu.matmul_acc_lhs(acc[place], part, load_staged_rhs=step % 2 if place == 0 else None)
            if place == 0 and step + 1 < steps:
                push(step + 1)
    for place in range(places):
        finish(place, [pltpu.matmul_pop(acc[place])[:, :total_tokens] for acc in accs])


def with_accs(kernel, shapes):
    if not shapes:
        return kernel
    half = len(shapes) // 2

    def body(*refs):
        pl.run_scoped(lambda *accs: kernel(*refs, accs=(accs[:half], accs[half:])), *shapes)

    return body


def place_rows(pieces, distances, rows):
    me = lax.axis_index("dp")
    tok_dev = pieces[0].shape[0]
    for piece, distance in zip(pieces, distances):
        start = pl.multiple_of(jnp.bitwise_xor(me, distance) * tok_dev, tok_dev)
        rows[pl.ds(start, tok_dev), :] = piece[...]


def start_loads(plan, sources, nears, sems):
    copies, number = [], 0
    for (first, last), source, near in zip(plan, sources, nears):
        for chunk in range(first, last):
            copies.append(pltpu.make_async_copy(source.at[chunk], near.at[chunk - first], sems.at[number]))
            number += 1
    for copy in copies:
        copy.start()
    return copies


def pack_load_kernel(plan, logits, routes, cotangent, gate, packed, gate_near, *scratch):
    logits_near, routes_near, columns, sems, load_sems = scratch
    model_width = cotangent.shape[1]
    copies = [
        pltpu.make_async_copy(logits, logits_near, sems.at[0]),
        pltpu.make_async_copy(routes, routes_near, sems.at[1]),
        pltpu.make_async_copy(cotangent, packed.at[:, :model_width], sems.at[2]),
    ]
    for copy in copies:
        copy.start()
    loads = start_loads(plan, [gate], [gate_near], load_sems)
    columns[...] = jnp.zeros(columns.shape, jnp.float32)
    copies[0].wait()
    left = logits_near[...]
    experts_all = left.shape[1]
    for term in range(3):
        rounded = left.astype(jnp.bfloat16).astype(jnp.float32)
        columns[:, term * experts_all : (term + 1) * experts_all] = rounded
        left = left - rounded
    copies[1].wait()
    columns[:, 3 * experts_all : 3 * experts_all + routes.shape[0]] = routes_near[...].astype(jnp.float32).T
    packed[:, model_width:] = columns[...].astype(jnp.bfloat16)
    copies[2].wait()
    for copy in loads:
        copy.wait()


def load_kernel(plan, *refs):
    count = len(plan)
    sources, nears, sems = refs[:count], refs[count + 1 : 2 * count + 1], refs[-1]
    for copy in start_loads(plan, sources, nears, sems):
        copy.wait()


def blocks_of(buffers, unit):
    return [
        buffer.at[chunk, first : first + unit]
        for buffer in buffers
        for chunk in range(buffer.shape[0])
        for first in range(0, buffer.shape[1], unit)
    ]


def gated(dots):
    gate_pre, up_pre = dots
    return gate_pre / (1.0 + jnp.exp(-gate_pre)) * up_pre


def first_hidden_kernel(distances, plan, *refs, accs=()):
    count = len(distances)
    pieces, refs = refs[:count], refs[count:]
    gate_0, gate_1, up, up_far, down_far, after, hidden, mine, rows, up_near, down_near, sems, mine_sem = refs
    loads = start_loads(plan, [up_far, down_far], [up_near, down_near], sems)
    place_rows(pieces, distances, rows)
    width = mine.shape[1]
    start = pl.multiple_of(lax.axis_index("dp") * width, width)
    own = pltpu.make_async_copy(rows.at[:, pl.ds(start, width)], mine, mine_sem)
    own.start()
    places, unit = hidden.shape[:2]
    lanes = [blocks_of([gate_0, gate_1], unit)[:places], blocks_of([up], unit)]

    def finish(place, dots):
        hidden[place] = gated(dots)

    stream_dots(rows, lanes, accs, finish)
    own.wait()
    for copy in loads:
        copy.wait()


def second_hidden_kernel(plan, rows, gate, up_1, up_2, down_far, after, hidden, down_near, sems, accs=()):
    loads = start_loads(plan, [down_far], [down_near], sems)
    places, unit = hidden.shape[:2]
    lanes = [blocks_of([gate], unit)[-places:], blocks_of([up_1, up_2], unit)]

    def finish(place, dots):
        hidden[place] = gated(dots)

    stream_dots(rows, lanes, accs, finish)
    for copy in loads:
        copy.wait()


def score_kernel(distances, top, *refs, accs=()):
    count = len(distances)
    pieces, refs = refs[:count], refs[count:]
    hidden_0, hidden_1, down_0, down_1, partial, probs, chosen, rows = refs
    model_width = down_0.shape[2]
    experts_all = probs.shape[0]
    place_rows(pieces, distances, rows)
    local_experts = partial.shape[1]
    unit = hidden_0.shape[1]
    blocks = blocks_of([down_0, down_1], unit)
    hidden = [held.at[place] for held in (hidden_0, hidden_1) for place in range(held.shape[0])]
    places = len(blocks) // 2
    per_expert = len(blocks) // local_experts
    sums = [None] * local_experts

    def routing():
        packed = rows[:, model_width:].astype(jnp.float32).T
        terms = [packed[term * experts_all : (term + 1) * experts_all] for term in range(3)]
        logits = terms[0] + terms[1] + terms[2]
        raised = jnp.exp(logits - jnp.max(logits, axis=0, keepdims=True))
        probs[...] = raised / jnp.sum(raised, axis=0, keepdims=True)
        number = lax.broadcasted_iota(jnp.int32, logits.shape, 0).astype(jnp.float32)
        named = jnp.zeros(logits.shape, jnp.float32)
        for slot in range(3 * experts_all, 3 * experts_all + top):
            named = named + (packed[slot : slot + 1] == number).astype(jnp.float32)
        chosen[...] = named

    def finish(place, dots):
        for block, paired in zip((place, places + place), dots):
            product = hidden[block][...] * paired
            expert = block // per_expert
            sums[expert] = product if sums[expert] is None else sums[expert] + product

    routing()
    stream_dots(rows.at[:, :model_width], [blocks[:places], blocks[places:]], accs, finish)
    lines = [jnp.sum(term, axis=0, keepdims=True) for term in sums]
    partial[...] = jnp.broadcast_to(jnp.concatenate(lines, axis=0)[None], partial.shape)


def gradient_kernel(data_count, blocks, probs_ref, chosen_ref, mine, logit_grad, router_grad, grads):
    experts_all, total_tokens = probs_ref.shape
    scores = jnp.sum(blocks[...].reshape((data_count, experts_all, total_tokens)), axis=0)
    probs, chosen = probs_ref[...], chosen_ref[...]
    mass = jnp.sum(probs * chosen, axis=0, keepdims=True)
    weighted = jnp.sum(probs * chosen * scores, axis=0, keepdims=True)
    prob_grad = scores / mass - chosen * weighted / (mass * mass)
    grad = probs * (prob_grad - jnp.sum(probs * prob_grad, axis=0, keepdims=True))
    router_grad[...] = jnp.dot(grad.astype(jnp.bfloat16), mine[...], preferred_element_type=jnp.float32)
    grads[...] = grad.T
    tok_dev = logit_grad.shape[0]
    logit_grad[...] = grads[pl.ds(pl.multiple_of(lax.axis_index("dp") * tok_dev, tok_dev), tok_dev), :]


def swap(value, axis, distance):
    return lax.ppermute(value, axis, [(index, index ^ distance) for index in range(lax.axis_size(axis))])


def per_device(tokens, cotangent, logits, routes, gate_weight, up_weight, down_weight):
    data_count = lax.axis_size("dp")
    expert_count = lax.axis_size("expert")
    tok_dev, model_width = tokens.shape
    local_experts, ff_dev = gate_weight.shape[:2]
    total_tokens = tok_dev * data_count
    experts_all = local_experts * expert_count
    top = routes.shape[1]
    unit = 128 if ff_dev % 128 == 0 else ff_dev
    units = local_experts * ff_dev // unit
    chunk_rows = unit * (2 if unit == 128 and units % 2 == 0 else 1)
    chunks = local_experts * ff_dev // chunk_rows
    extra = -(-(3 * experts_all + top) // 128) * 128
    chips = data_count // CORES
    distances = [chip * CORES + core for chip in range(chips) for core in range(CORES)]
    gate_cut = chunks // 2
    first = 2 * chunks // 3

    vmem = pl.BlockSpec(memory_space=pltpu.VMEM)
    hbm = pl.BlockSpec(memory_space=pltpu.HBM)
    anywhere = pl.BlockSpec(memory_space=pl.ANY)
    row_bytes = total_tokens * model_width * 2

    def keep_far(value):
        return pltpu.with_memory_space_constraint(value, pltpu.HBM)

    def near(first, last):
        return pltpu.VMEM((last - first, chunk_rows, model_width), jnp.bfloat16)

    def roomy():
        return scoped(0 if accs(1) else 2 * row_bytes)

    def cost(loads, dots):
        return pl.CostEstimate(flops=dots, bytes_accessed=loads, transcendentals=0)

    def scoped(size):
        return pltpu.CompilerParams(vmem_limit_bytes=size + (2 << 20))

    edge = pltpu.get_tpu_info().mxu_column_size
    accs = []
    places = first * chunk_rows // unit

    def accs(count):
        if edge != 2 * total_tokens or model_width % edge != 0 or units % 2 != 0 or count * unit > 1024:
            return []
        return [pltpu.ACC(number)((unit, edge), jnp.float32) for number in range(2) for _ in range(count)]

    def load(parts, after, name):
        plan = [(begin, end) for _, begin, end in parts]
        count = sum(end - begin for begin, end in plan)
        return pl.pallas_call(
            functools.partial(load_kernel, plan),
            out_shape=[near(*part) for part in plan],
            in_specs=[hbm] * len(plan) + [anywhere],
            out_specs=[vmem] * len(plan),
            scratch_shapes=[pltpu.SemaphoreType.DMA((count,))],
            compiler_params=scoped(0),
            cost_estimate=cost(count, 0),
            name=name,
        )(*(source for source, _, _ in parts), after)

    cut = (chunks, chunk_rows, model_width)
    gate, up, down = (keep_far(weight.reshape(cut)) for weight in (gate_weight, up_weight, down_weight))

    tokens_beside = swap(tokens, "dp", 1)
    tokens_far = [swap(tokens, "dp", chip * CORES) for chip in range(1, chips)]
    plan = [(0, gate_cut)]
    packed, gate_0 = pl.pallas_call(
        functools.partial(pack_load_kernel, plan),
        out_shape=(jax.ShapeDtypeStruct((tok_dev, model_width + extra), jnp.bfloat16), near(*plan[0])),
        in_specs=[hbm] * 4,
        out_specs=(vmem, vmem),
        scratch_shapes=[
            pltpu.VMEM((tok_dev, experts_all), jnp.float32),
            pltpu.VMEM((top, tok_dev), jnp.int32),
            pltpu.VMEM((tok_dev, extra), jnp.float32),
            pltpu.SemaphoreType.DMA((3,)),
            pltpu.SemaphoreType.DMA((gate_cut,)),
        ],
        compiler_params=scoped(0),
        cost_estimate=cost(gate_cut, 0),
        name="load_pack",
    )(keep_far(logits), keep_far(routes.T), keep_far(cotangent), gate)
    packed_far = [swap(packed, "dp", chip * CORES) for chip in range(1, chips)]
    packed_beside = swap(packed, "dp", 1)
    gate_1, up_0 = load([(gate, gate_cut, chunks), (up, 0, first)], packed, "load_second")
    tokens_far, gate_1, up_0 = lax.optimization_barrier((tokens_far, gate_1, up_0))
    token_pieces = [tokens, tokens_beside]
    for far in tokens_far:
        token_pieces += [far, swap(far, "dp", 1)]
    (up_1,) = load([(up, first, first + 1)], tokens_far[0], "load_third")

    plan = [(first + 1, chunks), (0, first)]
    loads = sum(last - first for first, last in plan)
    hidden_0, mine, rows, up_2, down_0 = pl.pallas_call(
        with_accs(functools.partial(first_hidden_kernel, distances, plan), accs(places)),
        out_shape=(
            jax.ShapeDtypeStruct((places, unit, total_tokens), jnp.float32),
            jax.ShapeDtypeStruct((total_tokens, model_width // data_count), jnp.bfloat16),
            jax.ShapeDtypeStruct((total_tokens, model_width), jnp.bfloat16),
            near(*plan[0]),
            near(*plan[1]),
        ),
        in_specs=[vmem] * (data_count + 3) + [hbm] * 2 + [anywhere],
        out_specs=(vmem,) * 5,
        scratch_shapes=[pltpu.SemaphoreType.DMA((loads,)), pltpu.SemaphoreType.DMA],
        compiler_params=roomy(),
        cost_estimate=cost(loads, 2 * first),
        name="hidden_first",
    )(*token_pieces, gate_0, gate_1, up_0, up, down, up_1)

    packed_far, hidden_0, rows = lax.optimization_barrier((packed_far, hidden_0, rows))
    packed_pieces = [packed, packed_beside]
    for far in packed_far:
        packed_pieces += [far, swap(far, "dp", 1)]

    plan = [(first, chunks)]
    hidden_1, down_1 = pl.pallas_call(
        with_accs(functools.partial(second_hidden_kernel, plan), accs(units - places)),
        out_shape=(
            jax.ShapeDtypeStruct((units - places, unit, total_tokens), jnp.float32),
            near(*plan[0]),
        ),
        in_specs=[vmem] * 4 + [hbm, anywhere],
        out_specs=(vmem, vmem),
        scratch_shapes=[pltpu.SemaphoreType.DMA((chunks - first,))],
        compiler_params=roomy(),
        cost_estimate=cost(chunks - first, 2 * (chunks - first)),
        name="hidden_second",
    )(rows, gate_1, up_1, up_2, down, packed_far[0])

    table = jax.ShapeDtypeStruct((experts_all, total_tokens), jnp.float32)
    partial, probs, chosen = pl.pallas_call(
        with_accs(functools.partial(score_kernel, distances, top), accs(units // 2)),
        out_shape=(
            jax.ShapeDtypeStruct((data_count * expert_count, local_experts, total_tokens), jnp.float32),
            table,
            table,
        ),
        in_specs=[vmem] * (data_count + 4),
        out_specs=(vmem, vmem, vmem),
        scratch_shapes=[
            pltpu.VMEM((total_tokens, model_width + extra), jnp.bfloat16),
        ]
       ,
        compiler_params=scoped(2 * row_bytes),
        cost_estimate=cost(0, chunks),
        name="scores",
    )(*packed_pieces, hidden_0, hidden_1, down_0, down_1)

    score_blocks = lax.all_to_all(partial, ("dp", "expert"), split_axis=0, concat_axis=0, tiled=True)

    logit_grad, router_grad = pl.pallas_call(
        functools.partial(gradient_kernel, data_count),
        out_shape=(
            jax.ShapeDtypeStruct((tok_dev, experts_all), jnp.float32),
            jax.ShapeDtypeStruct((experts_all, model_width // data_count), jnp.float32),
        ),
        in_specs=[vmem] * 4,
        out_specs=(vmem, vmem),
        scratch_shapes=[pltpu.VMEM((total_tokens, experts_all), jnp.float32)],
        compiler_params=scoped(4 << 20),
        name="gradient",
    )(score_blocks, probs, chosen, mine)
    return logit_grad, router_grad.T


def solution(mesh):
    placed = (
        P("dp", None),
        P("dp", None),
        P("dp", None),
        P("dp", None),
        P("expert", "dp", None),
        P("expert", "dp", None),
        P("expert", "dp", None),
    )
    mapped = jax.shard_map(
        per_device,
        mesh=mesh,
        in_specs=placed,
        out_specs=(P("dp", None), P("dp", None)),
        check_vma=False,
    )

    def run(*args):
        with jax.sharding.use_abstract_mesh(mesh.abstract_mesh):
            return mapped(*args)

    return run
```

```python
import functools

import jax
import jax.numpy as jnp
from jax import lax
from jax.experimental import pallas as pl
from jax.experimental.pallas import tpu as pltpu
from jax.sharding import PartitionSpec as P

CORES = 2


def dot_rows(a, b):
    return lax.dot_general(a, b, (((1,), (1,)), ((), ())), preferred_element_type=jnp.float32)


def stream_dots(rows, lanes, size, accs, ready, finish):
    groups = [range(first, first + size) for first in range(0, len(lanes[0]), size)]

    def dots_of(number, place):
        if not accs:
            return [dot_rows(lane[place][...], rows[...]) for lane in lanes]
        at = number % 2 * size + place % size
        return [pltpu.matmul_pop(acc[at])[:, : rows.shape[0]] for acc in accs]

    def read(number):
        for place in groups[number]:
            finish(place, dots_of(number, place))

    if not accs:
        for number in range(len(groups)):
            ready(number)
            read(number)
        return
    edge = accs[0][0].shape[1]
    steps = rows.shape[1] // edge

    def push(turn):
        first = turn % steps * edge
        both = jnp.concatenate([rows[:, first : first + edge]] * (edge // rows.shape[0]), axis=0)
        for unit in range(len(lanes)):
            pltpu.matmul_push_rhs(both, turn % 2, unit, transpose=True)

    push(0)
    for turn in range(len(groups) * steps):
        number, step = divmod(turn, steps)
        if step == 0:
            ready(number)
        for place in groups[number]:
            for lane, acc in zip(lanes, accs):
                part = lane[place][:, step * edge : (step + 1) * edge]
                staged = turn % 2 if place == groups[number][0] else None
                pltpu.matmul_acc_lhs(acc[number % 2 * size + place % size], part, load_staged_rhs=staged)
            if place == groups[number][0] and turn + 1 < len(groups) * steps:
                push(turn + 1)
        if step == 0 and number > 0:
            read(number - 1)
    read(len(groups) - 1)


def with_accs(kernel, shapes):
    if not shapes:
        return kernel
    half = len(shapes) // 2

    def body(*refs):
        pl.run_scoped(lambda *accs: kernel(*refs, accs=(accs[:half], accs[half:])), *shapes)

    return body


def place_rows(pieces, distances, rows):
    me = lax.axis_index("dp")
    tok_dev = pieces[0].shape[0]
    for piece, distance in zip(pieces, distances):
        start = pl.multiple_of(jnp.bitwise_xor(me, distance) * tok_dev, tok_dev)
        rows[pl.ds(start, tok_dev), :] = piece[...]


def start_loads(plan, sources, nears, sems):
    copies, number = [], 0
    for (first, last), source, near in zip(plan, sources, nears):
        for chunk in range(first, last):
            copies.append(pltpu.make_async_copy(source.at[chunk], near.at[chunk - first], sems.at[number]))
            number += 1
    for copy in copies:
        copy.start()
    return copies


def load_pack_kernel(plan, logits, routes, cotangent, gate, up, packed, gate_near, up_near, *scratch):
    logits_near, routes_near, columns, sems, load_sems = scratch
    model_width = cotangent.shape[1]
    copies = [
        pltpu.make_async_copy(logits, logits_near, sems.at[0]),
        pltpu.make_async_copy(routes, routes_near, sems.at[1]),
        pltpu.make_async_copy(cotangent, packed.at[:, :model_width], sems.at[2]),
    ]
    for copy in copies:
        copy.start()
    loads = start_loads(plan, [gate, up], [gate_near, up_near], load_sems)
    columns[...] = jnp.zeros(columns.shape, jnp.float32)
    copies[0].wait()
    left = logits_near[...]
    experts_all = left.shape[1]
    for term in range(3):
        rounded = left.astype(jnp.bfloat16).astype(jnp.float32)
        columns[:, term * experts_all : (term + 1) * experts_all] = rounded
        left = left - rounded
    copies[1].wait()
    columns[:, 3 * experts_all : 3 * experts_all + routes.shape[0]] = routes_near[...].astype(jnp.float32).T
    packed[:, model_width:] = columns[...].astype(jnp.bfloat16)
    copies[2].wait()
    for copy in loads:
        copy.wait()


def blocks_of(buffers, unit):
    return [
        buffer.at[chunk, first : first + unit]
        for buffer in buffers
        for chunk in range(buffer.shape[0])
        for first in range(0, buffer.shape[1], unit)
    ]


def gated(dots):
    gate_pre, up_pre = dots
    return gate_pre / (1.0 + jnp.exp(-gate_pre)) * up_pre


def hidden_kernel(distances, plan, size, *refs, accs=()):
    count = len(distances)
    pieces, refs = refs[:count], refs[count:]
    gate, up_near, up_far, down_far, hidden, mine, down_near, rows, up_late, sems, mine_sem = refs
    loads = start_loads(plan, [up_far, down_far], [up_late, down_near], sems)
    late = up_late.shape[0]
    place_rows(pieces, distances, rows)
    width = mine.shape[1]
    start = pl.multiple_of(lax.axis_index("dp") * width, width)
    own = pltpu.make_async_copy(rows.at[:, pl.ds(start, width)], mine, mine_sem)
    own.start()
    places, unit = hidden.shape[:2]
    lanes = [blocks_of([gate], unit), blocks_of([up_near, up_late], unit)]
    per_chunk = places // gate.shape[0]
    waited = [0]

    def ready(group):
        needed = -(-(group + 1) * size // per_chunk) - up_near.shape[0]
        while waited[0] < min(needed, late):
            loads[waited[0]].wait()
            waited[0] += 1

    def finish(place, dots):
        gate_pre, up_pre = dots
        hidden[place] = gate_pre / (1.0 + jnp.exp(-gate_pre)) * up_pre

    stream_dots(rows, lanes, size, accs, ready, finish)
    own.wait()
    for copy in loads[late:]:
        copy.wait()


def score_kernel(distances, plan, top, *refs, accs=()):
    count = len(distances)
    pieces, refs = refs[:count], refs[count:]
    hidden, down_near, down_far, partial, probs, chosen, rows, down_late, sems = refs
    loads = start_loads(plan, [down_far], [down_late], sems)
    model_width = down_far.shape[2]
    experts_all = probs.shape[0]
    place_rows(pieces, distances, rows)
    local_experts = partial.shape[1]
    blocks = blocks_of([down_near, down_late], hidden.shape[1])
    per_expert = len(blocks) // local_experts
    size = len(blocks) // 4
    order = [
        [group * 2 * size + lane * size + place for group in range(2) for place in range(size)] for lane in range(2)
    ]
    sums = [None] * local_experts

    def routing():
        packed = rows[:, model_width:].astype(jnp.float32).T
        terms = [packed[term * experts_all : (term + 1) * experts_all] for term in range(3)]
        logits = terms[0] + terms[1] + terms[2]
        raised = jnp.exp(logits - jnp.max(logits, axis=0, keepdims=True))
        probs[...] = raised / jnp.sum(raised, axis=0, keepdims=True)
        number = lax.broadcasted_iota(jnp.int32, logits.shape, 0).astype(jnp.float32)
        named = jnp.zeros(logits.shape, jnp.float32)
        for slot in range(3 * experts_all, 3 * experts_all + top):
            named = named + (packed[slot : slot + 1] == number).astype(jnp.float32)
        chosen[...] = named

    def ready(group):
        if group == 1:
            for copy in loads:
                copy.wait()

    def finish(place, dots):
        for lane, paired in zip(order, dots):
            block = lane[place]
            product = hidden[block] * paired
            expert = block // per_expert
            sums[expert] = product if sums[expert] is None else sums[expert] + product

    routing()
    lanes = [[blocks[block] for block in lane] for lane in order]
    stream_dots(rows.at[:, :model_width], lanes, size, accs, ready, finish)
    lines = [jnp.sum(term, axis=0, keepdims=True) for term in sums]
    partial[...] = jnp.broadcast_to(jnp.concatenate(lines, axis=0)[None], partial.shape)


def gradient_kernel(data_count, blocks, probs_ref, chosen_ref, mine, logit_grad, router_grad, grads):
    experts_all, total_tokens = probs_ref.shape
    scores = jnp.sum(blocks[...].reshape((data_count, experts_all, total_tokens)), axis=0)
    probs, chosen = probs_ref[...], chosen_ref[...]
    mass = jnp.sum(probs * chosen, axis=0, keepdims=True)
    weighted = jnp.sum(probs * chosen * scores, axis=0, keepdims=True)
    prob_grad = scores / mass - chosen * weighted / (mass * mass)
    grad = probs * (prob_grad - jnp.sum(probs * prob_grad, axis=0, keepdims=True))
    router_grad[...] = jnp.dot(grad.astype(jnp.bfloat16), mine[...], preferred_element_type=jnp.float32)
    grads[...] = grad.T
    tok_dev = logit_grad.shape[0]
    logit_grad[...] = grads[pl.ds(pl.multiple_of(lax.axis_index("dp") * tok_dev, tok_dev), tok_dev), :]


def swap(value, axis, distance):
    return lax.ppermute(value, axis, [(index, index ^ distance) for index in range(lax.axis_size(axis))])


def per_device(tokens, cotangent, logits, routes, gate_weight, up_weight, down_weight):
    data_count = lax.axis_size("dp")
    expert_count = lax.axis_size("expert")
    tok_dev, model_width = tokens.shape
    local_experts, ff_dev = gate_weight.shape[:2]
    total_tokens = tok_dev * data_count
    experts_all = local_experts * expert_count
    top = routes.shape[1]
    unit = 128 if ff_dev % 128 == 0 else ff_dev
    units = local_experts * ff_dev // unit
    chunk_rows = unit * (2 if unit == 128 and units % 2 == 0 else 1)
    chunks = local_experts * ff_dev // chunk_rows
    extra = -(-(3 * experts_all + top) // 128) * 128
    chips = data_count // CORES
    distances = [chip * CORES + core for chip in range(chips) for core in range(CORES)]
    up_cut = chunks // 2
    down_cut = 2 * chunks // 3

    vmem = pl.BlockSpec(memory_space=pltpu.VMEM)
    hbm = pl.BlockSpec(memory_space=pltpu.HBM)
    anywhere = pl.BlockSpec(memory_space=pl.ANY)
    row_bytes = total_tokens * model_width * 2

    def keep_far(value):
        return pltpu.with_memory_space_constraint(value, pltpu.HBM)

    def near(first, last):
        return pltpu.VMEM((last - first, chunk_rows, model_width), jnp.bfloat16)

    def cost(loads, dots):
        return pl.CostEstimate(flops=dots, bytes_accessed=loads, transcendentals=0)

    def scoped(size):
        return pltpu.CompilerParams(vmem_limit_bytes=size + (2 << 20))

    edge = pltpu.get_tpu_info().mxu_column_size
    accs = []
    size = units // 3 if units % 3 == 0 else 1

    def accs(count):
        if edge != 2 * total_tokens or model_width % edge != 0 or 2 * count * unit > 1024 or units % 12 != 0:
            return []
        return [pltpu.ACC(number)((unit, edge), jnp.float32) for number in range(2) for _ in range(2 * count)]

    cut = (chunks, chunk_rows, model_width)
    gate, up, down = (keep_far(weight.reshape(cut)) for weight in (gate_weight, up_weight, down_weight))

    tokens_beside = swap(tokens, "dp", 1)
    tokens_far = [swap(tokens, "dp", chip * CORES) for chip in range(1, chips)]
    plan = [(0, chunks), (0, up_cut)]
    packed, gate_near, up_near = pl.pallas_call(
        functools.partial(load_pack_kernel, plan),
        out_shape=(
            jax.ShapeDtypeStruct((tok_dev, model_width + extra), jnp.bfloat16),
            near(*plan[0]),
            near(*plan[1]),
        ),
        in_specs=[hbm] * 5,
        out_specs=(vmem,) * 3,
        scratch_shapes=[
            pltpu.VMEM((tok_dev, experts_all), jnp.float32),
            pltpu.VMEM((top, tok_dev), jnp.int32),
            pltpu.VMEM((tok_dev, extra), jnp.float32),
            pltpu.SemaphoreType.DMA((3,)),
            pltpu.SemaphoreType.DMA((chunks + up_cut,)),
        ],
        compiler_params=scoped(0),
        cost_estimate=cost(chunks + up_cut, 0),
        name="load_pack",
    )(keep_far(logits), keep_far(routes.T), keep_far(cotangent), gate, up)
    packed_far = [swap(packed, "dp", chip * CORES) for chip in range(1, chips)]
    packed_beside = swap(packed, "dp", 1)
    tokens_far, gate_near, up_near = lax.optimization_barrier((tokens_far, gate_near, up_near))
    token_pieces = [tokens, tokens_beside]
    for far in tokens_far:
        token_pieces += [far, swap(far, "dp", 1)]
    plan = [(up_cut, chunks), (0, down_cut)]
    loads = chunks - up_cut + down_cut
    hidden, mine, down_near = pl.pallas_call(
        with_accs(functools.partial(hidden_kernel, distances, plan, size), accs(size)),
        out_shape=(
            jax.ShapeDtypeStruct((units, unit, total_tokens), jnp.float32),
            jax.ShapeDtypeStruct((total_tokens, model_width // data_count), jnp.bfloat16),
            near(*plan[1]),
        ),
        in_specs=[vmem] * (data_count + 2) + [hbm] * 2,
        out_specs=(vmem,) * 3,
        scratch_shapes=[
            pltpu.VMEM((total_tokens, model_width), jnp.bfloat16),
            near(*plan[0]),
            pltpu.SemaphoreType.DMA((loads,)),
            pltpu.SemaphoreType.DMA,
        ],
        compiler_params=scoped((chunks - up_cut) * cut[1] * cut[2] * 2 + (1 if accs(size) else 3) * row_bytes),
        cost_estimate=cost(loads, 2 * chunks),
        name="hidden",
    )(*token_pieces, gate_near, up_near, up, down)

    packed_far, hidden = lax.optimization_barrier((packed_far, hidden))
    packed_pieces = [packed, packed_beside]
    for far in packed_far:
        packed_pieces += [far, swap(far, "dp", 1)]

    plan = [(down_cut, chunks)]
    table = jax.ShapeDtypeStruct((experts_all, total_tokens), jnp.float32)
    partial, probs, chosen = pl.pallas_call(
        with_accs(functools.partial(score_kernel, distances, plan, top), accs(units // 4)),
        out_shape=(
            jax.ShapeDtypeStruct((data_count * expert_count, local_experts, total_tokens), jnp.float32),
            table,
            table,
        ),
        in_specs=[vmem] * (data_count + 2) + [hbm],
        out_specs=(vmem, vmem, vmem),
        scratch_shapes=[
            pltpu.VMEM((total_tokens, model_width + extra), jnp.bfloat16),
            near(*plan[0]),
            pltpu.SemaphoreType.DMA((chunks - down_cut,)),
        ],
        compiler_params=scoped((chunks - down_cut) * cut[1] * cut[2] * 2 + 3 * row_bytes),
        cost_estimate=cost(chunks - down_cut, chunks),
        name="scores",
    )(*packed_pieces, hidden, down_near, down)

    score_blocks = lax.all_to_all(partial, ("dp", "expert"), split_axis=0, concat_axis=0, tiled=True)

    logit_grad, router_grad = pl.pallas_call(
        functools.partial(gradient_kernel, data_count),
        out_shape=(
            jax.ShapeDtypeStruct((tok_dev, experts_all), jnp.float32),
            jax.ShapeDtypeStruct((experts_all, model_width // data_count), jnp.float32),
        ),
        in_specs=[vmem] * 4,
        out_specs=(vmem, vmem),
        scratch_shapes=[pltpu.VMEM((total_tokens, experts_all), jnp.float32)],
        compiler_params=scoped(4 << 20),
        name="gradient",
    )(score_blocks, probs, chosen, mine)
    return logit_grad, router_grad.T


def solution(mesh):
    placed = (
        P("dp", None),
        P("dp", None),
        P("dp", None),
        P("dp", None),
        P("expert", "dp", None),
        P("expert", "dp", None),
        P("expert", "dp", None),
    )
    mapped = jax.shard_map(
        per_device,
        mesh=mesh,
        in_specs=placed,
        out_specs=(P("dp", None), P("dp", None)),
        check_vma=False,
    )

    def run(*args):
        with jax.sharding.use_abstract_mesh(mesh.abstract_mesh):
            return mapped(*args)

    return run
```

```python
import functools

import jax
import jax.numpy as jnp
from jax import lax
from jax.experimental import pallas as pl
from jax.experimental.pallas import tpu as pltpu
from jax.sharding import PartitionSpec as P

CORES = 2


def dot_rows(a, b):
    return lax.dot_general(a, b, (((1,), (1,)), ((), ())), preferred_element_type=jnp.float32)


def stream_dots(rows, lanes, size, accs, ready, finish):
    groups = [range(first, first + size) for first in range(0, len(lanes[0]), size)]

    def dots_of(number, place):
        if not accs:
            return [dot_rows(lane[place][...], rows[...]) for lane in lanes]
        at = number % 2 * size + place % size
        return [pltpu.matmul_pop(acc[at])[:, : rows.shape[0]] for acc in accs]

    def read(number):
        for place in groups[number]:
            finish(place, dots_of(number, place))

    if not accs:
        for number in range(len(groups)):
            ready(number)
            read(number)
        return
    edge = accs[0][0].shape[1]
    steps = rows.shape[1] // edge

    def push(turn):
        first = turn % steps * edge
        both = jnp.concatenate([rows[:, first : first + edge]] * (edge // rows.shape[0]), axis=0)
        for unit in range(len(lanes)):
            pltpu.matmul_push_rhs(both, turn % 2, unit, transpose=True)

    push(0)
    for turn in range(len(groups) * steps):
        number, step = divmod(turn, steps)
        if step == 0:
            ready(number)
        for place in groups[number]:
            for lane, acc in zip(lanes, accs):
                part = lane[place][:, step * edge : (step + 1) * edge]
                staged = turn % 2 if place == groups[number][0] else None
                pltpu.matmul_acc_lhs(acc[number % 2 * size + place % size], part, load_staged_rhs=staged)
            if place == groups[number][0] and turn + 1 < len(groups) * steps:
                push(turn + 1)
        if step == 0 and number > 0:
            read(number - 1)
    read(len(groups) - 1)


def with_accs(kernel, shapes):
    if not shapes:
        return kernel
    half = len(shapes) // 2

    def body(*refs):
        pl.run_scoped(lambda *accs: kernel(*refs, accs=(accs[:half], accs[half:])), *shapes)

    return body


def place_rows(pieces, distances, rows):
    me = lax.axis_index("dp")
    tok_dev = pieces[0].shape[0]
    for piece, distance in zip(pieces, distances):
        start = pl.multiple_of(jnp.bitwise_xor(me, distance) * tok_dev, tok_dev)
        rows[pl.ds(start, tok_dev), :] = piece[...]


def start_loads(plan, sources, nears, sems):
    copies, number = [], 0
    for (first, last), source, near in zip(plan, sources, nears):
        for chunk in range(first, last):
            copies.append(pltpu.make_async_copy(source.at[chunk], near.at[chunk - first], sems.at[number]))
            number += 1
    for copy in copies:
        copy.start()
    return copies


def load_kernel(plan, *refs):
    count = len(plan)
    sources, nears, sems = refs[:count], refs[count + 1 : 2 * count + 1], refs[-1]
    for copy in start_loads(plan, sources, nears, sems):
        copy.wait()


def pack_kernel(logits, routes, cotangent, packed, logits_near, routes_near, columns, sems):
    model_width = cotangent.shape[1]
    copies = [
        pltpu.make_async_copy(logits, logits_near, sems.at[0]),
        pltpu.make_async_copy(routes, routes_near, sems.at[1]),
        pltpu.make_async_copy(cotangent, packed.at[:, :model_width], sems.at[2]),
    ]
    for copy in copies:
        copy.start()
    columns[...] = jnp.zeros(columns.shape, jnp.float32)
    copies[0].wait()
    left = logits_near[...]
    experts_all = left.shape[1]
    for term in range(3):
        rounded = left.astype(jnp.bfloat16).astype(jnp.float32)
        columns[:, term * experts_all : (term + 1) * experts_all] = rounded
        left = left - rounded
    copies[1].wait()
    columns[:, 3 * experts_all : 3 * experts_all + routes.shape[0]] = routes_near[...].astype(jnp.float32).T
    packed[:, model_width:] = columns[...].astype(jnp.bfloat16)
    copies[2].wait()


def blocks_of(buffers, unit):
    return [
        buffer.at[chunk, first : first + unit]
        for buffer in buffers
        for chunk in range(buffer.shape[0])
        for first in range(0, buffer.shape[1], unit)
    ]


def gated(dots):
    gate_pre, up_pre = dots
    return gate_pre / (1.0 + jnp.exp(-gate_pre)) * up_pre


def stream_hidden(rows, lanes, size, accs, ready, hidden):
    def finish(place, dots):
        gate_pre, up_pre = dots
        hidden[place] = gate_pre / (1.0 + jnp.exp(-gate_pre)) * up_pre

    stream_dots(rows, lanes, size, accs, ready, finish)


def first_hidden_kernel(distances, plan, size, *refs, accs=()):
    count = len(distances)
    pieces, refs = refs[:count], refs[count:]
    gate, up, up_far, gate_far, hidden, mine, gate_late, up_late, rows, up_mid, sems, mine_sem = refs
    loads = start_loads(plan, [up_far, gate_far, up_far], [up_mid, gate_late, up_late], sems)
    place_rows(pieces, distances, rows)
    width = mine.shape[1]
    start = pl.multiple_of(lax.axis_index("dp") * width, width)
    own = pltpu.make_async_copy(rows.at[:, pl.ds(start, width)], mine, mine_sem)
    own.start()
    unit = hidden.shape[1]
    waited = up_mid.shape[0]

    def ready(group):
        if group == 1:
            for copy in loads[:waited]:
                copy.wait()

    lanes = [blocks_of([gate], unit), blocks_of([up, up_mid], unit)]
    stream_hidden(rows, lanes, size, accs, ready, hidden)
    own.wait()
    for copy in loads[waited:]:
        copy.wait()


def second_hidden_kernel(distances, plan, size, *refs, accs=()):
    count = len(distances)
    pieces, refs = refs[:count], refs[count:]
    gate, up, down_far, after, hidden, down_near, rows, sems = refs
    loads = start_loads(plan, [down_far], [down_near], sems)
    place_rows(pieces, distances, rows)
    unit = hidden.shape[1]
    lanes = [blocks_of([gate], unit), blocks_of([up], unit)]
    stream_hidden(rows, lanes, size, accs, lambda group: None, hidden)
    for copy in loads:
        copy.wait()


def score_kernel(distances, plan, top, *refs, accs=()):
    count = len(distances)
    pieces, refs = refs[:count], refs[count:]
    hidden_0, hidden_1, down_near, down_far, partial, probs, chosen, rows, down_late, sems = refs
    loads = start_loads(plan, [down_far], [down_late], sems)
    model_width = down_far.shape[2]
    experts_all = probs.shape[0]
    place_rows(pieces, distances, rows)
    local_experts = partial.shape[1]
    blocks = blocks_of([down_near, down_late], hidden_0.shape[1])
    hidden = [held.at[place] for held in (hidden_0, hidden_1) for place in range(held.shape[0])]
    per_expert = len(blocks) // local_experts
    size = len(blocks) // 4
    order = [
        [group * 2 * size + lane * size + place for group in range(2) for place in range(size)] for lane in range(2)
    ]
    sums = [None] * local_experts

    def routing():
        packed = rows[:, model_width:].astype(jnp.float32).T
        terms = [packed[term * experts_all : (term + 1) * experts_all] for term in range(3)]
        logits = terms[0] + terms[1] + terms[2]
        raised = jnp.exp(logits - jnp.max(logits, axis=0, keepdims=True))
        probs[...] = raised / jnp.sum(raised, axis=0, keepdims=True)
        number = lax.broadcasted_iota(jnp.int32, logits.shape, 0).astype(jnp.float32)
        named = jnp.zeros(logits.shape, jnp.float32)
        for slot in range(3 * experts_all, 3 * experts_all + top):
            named = named + (packed[slot : slot + 1] == number).astype(jnp.float32)
        chosen[...] = named

    def ready(group):
        if group == 1:
            for copy in loads:
                copy.wait()

    def finish(place, dots):
        if place == 0:
            routing()
        for lane, paired in zip(order, dots):
            block = lane[place]
            product = hidden[block][...] * paired
            expert = block // per_expert
            sums[expert] = product if sums[expert] is None else sums[expert] + product

    lanes = [[blocks[block] for block in lane] for lane in order]
    stream_dots(rows.at[:, :model_width], lanes, size, accs, ready, finish)
    lines = [jnp.sum(term, axis=0, keepdims=True) for term in sums]
    partial[...] = jnp.broadcast_to(jnp.concatenate(lines, axis=0)[None], partial.shape)


def gradient_kernel(data_count, blocks, probs_ref, chosen_ref, mine, logit_grad, router_grad, grads):
    experts_all, total_tokens = probs_ref.shape
    scores = jnp.sum(blocks[...].reshape((data_count, experts_all, total_tokens)), axis=0)
    probs, chosen = probs_ref[...], chosen_ref[...]
    mass = jnp.sum(probs * chosen, axis=0, keepdims=True)
    weighted = jnp.sum(probs * chosen * scores, axis=0, keepdims=True)
    prob_grad = scores / mass - chosen * weighted / (mass * mass)
    grad = probs * (prob_grad - jnp.sum(probs * prob_grad, axis=0, keepdims=True))
    router_grad[...] = jnp.dot(grad.astype(jnp.bfloat16), mine[...], preferred_element_type=jnp.float32)
    grads[...] = grad.T
    tok_dev = logit_grad.shape[0]
    logit_grad[...] = grads[pl.ds(pl.multiple_of(lax.axis_index("dp") * tok_dev, tok_dev), tok_dev), :]


def swap(value, axis, distance):
    return lax.ppermute(value, axis, [(index, index ^ distance) for index in range(lax.axis_size(axis))])


def per_device(tokens, cotangent, logits, routes, gate_weight, up_weight, down_weight):
    data_count = lax.axis_size("dp")
    expert_count = lax.axis_size("expert")
    tok_dev, model_width = tokens.shape
    local_experts, ff_dev = gate_weight.shape[:2]
    total_tokens = tok_dev * data_count
    experts_all = local_experts * expert_count
    top = routes.shape[1]
    unit = 128 if ff_dev % 128 == 0 else ff_dev
    units = local_experts * ff_dev // unit
    chunk_rows = unit * (2 if unit == 128 and units % 2 == 0 else 1)
    chunks = local_experts * ff_dev // chunk_rows
    extra = -(-(3 * experts_all + top) // 128) * 128
    chips = data_count // CORES
    distances = [chip * CORES + core for chip in range(chips) for core in range(CORES)]
    first = 2 * chunks // 3
    down_cut = chunks // 2

    vmem = pl.BlockSpec(memory_space=pltpu.VMEM)
    hbm = pl.BlockSpec(memory_space=pltpu.HBM)
    anywhere = pl.BlockSpec(memory_space=pl.ANY)
    row_bytes = total_tokens * model_width * 2

    def keep_far(value):
        return pltpu.with_memory_space_constraint(value, pltpu.HBM)

    def near(first, last):
        return pltpu.VMEM((last - first, chunk_rows, model_width), jnp.bfloat16)

    def cost(loads, dots):
        return pl.CostEstimate(flops=dots, bytes_accessed=loads, transcendentals=0)

    def scoped(size):
        return pltpu.CompilerParams(vmem_limit_bytes=size + (2 << 20))

    edge = pltpu.get_tpu_info().mxu_column_size
    accs = []
    size = units // 3 if units % 3 == 0 else 1

    def accs(count):
        if edge != 2 * total_tokens or model_width % edge != 0 or 2 * count * unit > 1024 or units % 12 != 0:
            return []
        return [pltpu.ACC(number)((unit, edge), jnp.float32) for number in range(2) for _ in range(2 * count)]

    cut = (chunks, chunk_rows, model_width)
    gate, up, down = (keep_far(weight.reshape(cut)) for weight in (gate_weight, up_weight, down_weight))

    tokens_beside = swap(tokens, "dp", 1)
    tokens_far = [swap(tokens, "dp", chip * CORES) for chip in range(1, chips)]
    packed = pl.pallas_call(
        pack_kernel,
        out_shape=jax.ShapeDtypeStruct((tok_dev, model_width + extra), jnp.bfloat16),
        in_specs=[hbm] * 3,
        out_specs=vmem,
        scratch_shapes=[
            pltpu.VMEM((tok_dev, experts_all), jnp.float32),
            pltpu.VMEM((top, tok_dev), jnp.int32),
            pltpu.VMEM((tok_dev, extra), jnp.float32),
            pltpu.SemaphoreType.DMA((3,)),
        ],
        compiler_params=scoped(0),
        cost_estimate=cost(1, 0),
        name="pack",
    )(keep_far(logits), keep_far(routes.T), keep_far(cotangent))
    packed_far = [swap(packed, "dp", chip * CORES) for chip in range(1, chips)]
    packed_beside = swap(packed, "dp", 1)
    plan = [(0, first), (0, first - 1)]
    gate_near, up_near = pl.pallas_call(
        functools.partial(load_kernel, plan),
        out_shape=[near(*part) for part in plan],
        in_specs=[hbm, hbm, anywhere],
        out_specs=[vmem, vmem],
        scratch_shapes=[pltpu.SemaphoreType.DMA((2 * first - 1,))],
        compiler_params=scoped(0),
        cost_estimate=cost(2 * first - 1, 0),
        name="load",
    )(gate, up, packed)
    tokens_far, gate_near, up_near = lax.optimization_barrier((tokens_far, gate_near, up_near))
    token_pieces = [tokens, tokens_beside]
    for far in tokens_far:
        token_pieces += [far, swap(far, "dp", 1)]
    plan = [(first - 1, first), (first, chunks), (first, chunks)]
    loads = 1 + 2 * (chunks - first)
    places = units * first // chunks
    rows_scratch = pltpu.VMEM((total_tokens, model_width), jnp.bfloat16)
    hidden_0, mine, gate_late, up_late = pl.pallas_call(
        with_accs(functools.partial(first_hidden_kernel, distances, plan, size), accs(size)),
        out_shape=(
            jax.ShapeDtypeStruct((places, unit, total_tokens), jnp.float32),
            jax.ShapeDtypeStruct((total_tokens, model_width // data_count), jnp.bfloat16),
            near(*plan[1]),
            near(*plan[2]),
        ),
        in_specs=[vmem] * (data_count + 2) + [hbm] * 2,
        out_specs=(vmem,) * 4,
        scratch_shapes=[
            rows_scratch,
            near(*plan[0]),
            pltpu.SemaphoreType.DMA((loads,)),
            pltpu.SemaphoreType.DMA,
        ],
        compiler_params=scoped(cut[1] * cut[2] * 2 + (1 if accs(size) else 3) * row_bytes),
        cost_estimate=cost(loads, 2 * first),
        name="hidden_first",
    )(*token_pieces, gate_near, up_near, up, gate)

    packed_far, hidden_0 = lax.optimization_barrier((packed_far, hidden_0))
    plan = [(0, down_cut)]
    hidden_1, down_near = pl.pallas_call(
        with_accs(functools.partial(second_hidden_kernel, distances, plan, size), accs(size)),
        out_shape=(jax.ShapeDtypeStruct((units - places, unit, total_tokens), jnp.float32), near(*plan[0])),
        in_specs=[vmem] * (data_count + 2) + [hbm, anywhere],
        out_specs=(vmem, vmem),
        scratch_shapes=[rows_scratch, pltpu.SemaphoreType.DMA((down_cut,))],
        compiler_params=scoped((1 if accs(size) else 3) * row_bytes),
        cost_estimate=cost(down_cut, 2 * (chunks - first)),
        name="hidden_second",
    )(*token_pieces, gate_late, up_late, down, packed_far[0])

    packed_pieces = [packed, packed_beside]
    for far in packed_far:
        packed_pieces += [far, swap(far, "dp", 1)]

    plan = [(down_cut, chunks)]
    table = jax.ShapeDtypeStruct((experts_all, total_tokens), jnp.float32)
    partial, probs, chosen = pl.pallas_call(
        with_accs(functools.partial(score_kernel, distances, plan, top), accs(units // 4)),
        out_shape=(
            jax.ShapeDtypeStruct((data_count * expert_count, local_experts, total_tokens), jnp.float32),
            table,
            table,
        ),
        in_specs=[vmem] * (data_count + 3) + [hbm],
        out_specs=(vmem, vmem, vmem),
        scratch_shapes=[
            pltpu.VMEM((total_tokens, model_width + extra), jnp.bfloat16),
            near(*plan[0]),
            pltpu.SemaphoreType.DMA((chunks - down_cut,)),
        ],
        compiler_params=scoped((chunks - down_cut) * cut[1] * cut[2] * 2 + 3 * row_bytes),
        cost_estimate=cost(chunks - down_cut, chunks),
        name="scores",
    )(*packed_pieces, hidden_0, hidden_1, down_near, down)

    score_blocks = lax.all_to_all(partial, ("dp", "expert"), split_axis=0, concat_axis=0, tiled=True)

    logit_grad, router_grad = pl.pallas_call(
        functools.partial(gradient_kernel, data_count),
        out_shape=(
            jax.ShapeDtypeStruct((tok_dev, experts_all), jnp.float32),
            jax.ShapeDtypeStruct((experts_all, model_width // data_count), jnp.float32),
        ),
        in_specs=[vmem] * 4,
        out_specs=(vmem, vmem),
        scratch_shapes=[pltpu.VMEM((total_tokens, experts_all), jnp.float32)],
        compiler_params=scoped(4 << 20),
        name="gradient",
    )(score_blocks, probs, chosen, mine)
    return logit_grad, router_grad.T


def solution(mesh):
    placed = (
        P("dp", None),
        P("dp", None),
        P("dp", None),
        P("dp", None),
        P("expert", "dp", None),
        P("expert", "dp", None),
        P("expert", "dp", None),
    )
    mapped = jax.shard_map(
        per_device,
        mesh=mesh,
        in_specs=placed,
        out_specs=(P("dp", None), P("dp", None)),
        check_vma=False,
    )

    def run(*args):
        with jax.sharding.use_abstract_mesh(mesh.abstract_mesh):
            return mapped(*args)

    return run
```

```python
import functools

import jax
import jax.numpy as jnp
from jax import lax
from jax.experimental import pallas as pl
from jax.experimental.pallas import tpu as pltpu
from jax.sharding import PartitionSpec as P

CORES = 2


def dot_rows(a, b):
    return lax.dot_general(a, b, (((1,), (1,)), ((), ())), preferred_element_type=jnp.float32)


def stream_dots(rows, lanes, size, accs, ready, finish):
    groups = [range(first, first + size) for first in range(0, len(lanes[0]), size)]

    def dots_of(number, place):
        if not accs:
            return [dot_rows(lane[place][...], rows[...]) for lane in lanes]
        at = number % 2 * size + place % size
        return [pltpu.matmul_pop(acc[at])[:, : rows.shape[0]] for acc in accs]

    def read(number):
        for place in groups[number]:
            finish(place, dots_of(number, place))

    if not accs:
        for number in range(len(groups)):
            ready(number)
            read(number)
        return
    edge = accs[0][0].shape[1]
    steps = rows.shape[1] // edge

    def push(turn):
        first = turn % steps * edge
        both = jnp.concatenate([rows[:, first : first + edge]] * (edge // rows.shape[0]), axis=0)
        for unit in range(len(lanes)):
            pltpu.matmul_push_rhs(both, turn % 2, unit, transpose=True)

    push(0)
    for turn in range(len(groups) * steps):
        number, step = divmod(turn, steps)
        if step == 0:
            ready(number)
        for place in groups[number]:
            for lane, acc in zip(lanes, accs):
                part = lane[place][:, step * edge : (step + 1) * edge]
                staged = turn % 2 if place == groups[number][0] else None
                pltpu.matmul_acc_lhs(acc[number % 2 * size + place % size], part, load_staged_rhs=staged)
            if place == groups[number][0] and turn + 1 < len(groups) * steps:
                push(turn + 1)
        if step == 0 and number > 0:
            read(number - 1)
    read(len(groups) - 1)


def with_accs(kernel, shapes):
    if not shapes:
        return kernel
    half = len(shapes) // 2

    def body(*refs):
        pl.run_scoped(lambda *accs: kernel(*refs, accs=(accs[:half], accs[half:])), *shapes)

    return body


def place_rows(pieces, distances, rows):
    me = lax.axis_index("dp")
    tok_dev = pieces[0].shape[0]
    for piece, distance in zip(pieces, distances):
        start = pl.multiple_of(jnp.bitwise_xor(me, distance) * tok_dev, tok_dev)
        rows[pl.ds(start, tok_dev), :] = piece[...]


def start_loads(plan, sources, nears, sems):
    copies, number = [], 0
    for (first, last), source, near in zip(plan, sources, nears):
        for chunk in range(first, last):
            copies.append(pltpu.make_async_copy(source.at[chunk], near.at[chunk - first], sems.at[number]))
            number += 1
    for copy in copies:
        copy.start()
    return copies


def load_pack_kernel(plan, logits, routes, cotangent, gate, up, packed, gate_near, up_near, *scratch):
    logits_near, routes_near, columns, sems, load_sems = scratch
    model_width = cotangent.shape[1]
    copies = [
        pltpu.make_async_copy(logits, logits_near, sems.at[0]),
        pltpu.make_async_copy(routes, routes_near, sems.at[1]),
        pltpu.make_async_copy(cotangent, packed.at[:, :model_width], sems.at[2]),
    ]
    for copy in copies:
        copy.start()
    loads = start_loads(plan, [gate, up], [gate_near, up_near], load_sems)
    columns[...] = jnp.zeros(columns.shape, jnp.float32)
    copies[0].wait()
    left = logits_near[...]
    experts_all = left.shape[1]
    for term in range(3):
        rounded = left.astype(jnp.bfloat16).astype(jnp.float32)
        columns[:, term * experts_all : (term + 1) * experts_all] = rounded
        left = left - rounded
    copies[1].wait()
    columns[:, 3 * experts_all : 3 * experts_all + routes.shape[0]] = routes_near[...].astype(jnp.float32).T
    packed[:, model_width:] = columns[...].astype(jnp.bfloat16)
    copies[2].wait()
    for copy in loads:
        copy.wait()


def load_kernel(plan, source, after, near, sems):
    for copy in start_loads(plan, [source], [near], sems):
        copy.wait()


def blocks_of(buffers, unit):
    return [
        buffer.at[chunk, first : first + unit]
        for buffer in buffers
        for chunk in range(buffer.shape[0])
        for first in range(0, buffer.shape[1], unit)
    ]


def gated(dots):
    gate_pre, up_pre = dots
    return gate_pre / (1.0 + jnp.exp(-gate_pre)) * up_pre


def hidden_kernel(distances, plan, size, *refs, accs=()):
    count = len(distances)
    pieces, refs = refs[:count], refs[count:]
    gate, up_near, up_far, down_far, hidden, mine, down_near, rows, up_late, sems, mine_sem = refs
    loads = start_loads(plan, [up_far, down_far], [up_late, down_near], sems)
    late = up_late.shape[0]
    place_rows(pieces, distances, rows)
    width = mine.shape[1]
    start = pl.multiple_of(lax.axis_index("dp") * width, width)
    own = pltpu.make_async_copy(rows.at[:, pl.ds(start, width)], mine, mine_sem)
    own.start()
    places, unit = hidden.shape[:2]
    lanes = [blocks_of([gate], unit), blocks_of([up_near, up_late], unit)]
    per_chunk = places // gate.shape[0]
    waited = [0]

    def ready(group):
        needed = -(-(group + 1) * size // per_chunk) - up_near.shape[0]
        while waited[0] < min(needed, late):
            loads[waited[0]].wait()
            waited[0] += 1

    def finish(place, dots):
        gate_pre, up_pre = dots
        hidden[place] = gate_pre / (1.0 + jnp.exp(-gate_pre)) * up_pre

    stream_dots(rows, lanes, size, accs, ready, finish)
    own.wait()
    for copy in loads[late:]:
        copy.wait()


def score_kernel(distances, plan, top, *refs, accs=()):
    count = len(distances)
    pieces, refs = refs[:count], refs[count:]
    hidden, down_near, down_mid, down_far, partial, probs, chosen, rows, down_late, sems = refs
    loads = start_loads(plan, [down_far], [down_late], sems)
    model_width = down_far.shape[2]
    experts_all = probs.shape[0]
    place_rows(pieces, distances, rows)
    local_experts = partial.shape[1]
    blocks = blocks_of([down_near, down_mid, down_late], hidden.shape[1])
    per_expert = len(blocks) // local_experts
    size = len(blocks) // 4
    order = [
        [group * 2 * size + lane * size + place for group in range(2) for place in range(size)] for lane in range(2)
    ]
    sums = [None] * local_experts

    def routing():
        packed = rows[:, model_width:].astype(jnp.float32).T
        terms = [packed[term * experts_all : (term + 1) * experts_all] for term in range(3)]
        logits = terms[0] + terms[1] + terms[2]
        raised = jnp.exp(logits - jnp.max(logits, axis=0, keepdims=True))
        probs[...] = raised / jnp.sum(raised, axis=0, keepdims=True)
        number = lax.broadcasted_iota(jnp.int32, logits.shape, 0).astype(jnp.float32)
        named = jnp.zeros(logits.shape, jnp.float32)
        for slot in range(3 * experts_all, 3 * experts_all + top):
            named = named + (packed[slot : slot + 1] == number).astype(jnp.float32)
        chosen[...] = named

    def ready(group):
        if group == 1:
            for copy in loads:
                copy.wait()

    def finish(place, dots):
        if place == 0:
            routing()
        for lane, paired in zip(order, dots):
            block = lane[place]
            product = hidden[block] * paired
            expert = block // per_expert
            sums[expert] = product if sums[expert] is None else sums[expert] + product

    lanes = [[blocks[block] for block in lane] for lane in order]
    stream_dots(rows.at[:, :model_width], lanes, size, accs, ready, finish)
    lines = [jnp.sum(term, axis=0, keepdims=True) for term in sums]
    partial[...] = jnp.broadcast_to(jnp.concatenate(lines, axis=0)[None], partial.shape)


def gradient_kernel(data_count, blocks, probs_ref, chosen_ref, mine, logit_grad, router_grad, grads, held, sems):
    experts_all, total_tokens = probs_ref.shape
    scores = jnp.sum(blocks[...].reshape((data_count, experts_all, total_tokens)), axis=0)
    probs, chosen = probs_ref[...], chosen_ref[...]
    mass = jnp.sum(probs * chosen, axis=0, keepdims=True)
    weighted = jnp.sum(probs * chosen * scores, axis=0, keepdims=True)
    prob_grad = scores / mass - chosen * weighted / (mass * mass)
    grad = probs * (prob_grad - jnp.sum(probs * prob_grad, axis=0, keepdims=True))
    half = mine.shape[1] // 2
    copies = []
    for number in range(2):
        part = pl.ds(number * half, half)
        held[:, part] = jnp.dot(grad.astype(jnp.bfloat16), mine[:, part], preferred_element_type=jnp.float32)
        copies.append(pltpu.make_async_copy(held.at[:, part], router_grad.at[:, part], sems.at[number]))
        copies[number].start()
    grads[...] = grad.T
    tok_dev = logit_grad.shape[0]
    start = pl.multiple_of(lax.axis_index("dp") * tok_dev, tok_dev)
    copies.append(pltpu.make_async_copy(grads.at[pl.ds(start, tok_dev)], logit_grad, sems.at[2]))
    copies[2].start()
    for copy in copies:
        copy.wait()


def swap(value, axis, distance):
    return lax.ppermute(value, axis, [(index, index ^ distance) for index in range(lax.axis_size(axis))])


def per_device(tokens, cotangent, logits, routes, gate_weight, up_weight, down_weight):
    data_count = lax.axis_size("dp")
    expert_count = lax.axis_size("expert")
    tok_dev, model_width = tokens.shape
    local_experts, ff_dev = gate_weight.shape[:2]
    total_tokens = tok_dev * data_count
    experts_all = local_experts * expert_count
    top = routes.shape[1]
    unit = 128 if ff_dev % 128 == 0 else ff_dev
    units = local_experts * ff_dev // unit
    chunk_rows = unit * (2 if unit == 128 and units % 2 == 0 else 1)
    chunks = local_experts * ff_dev // chunk_rows
    extra = -(-(3 * experts_all + top) // 128) * 128
    chips = data_count // CORES
    distances = [chip * CORES + core for chip in range(chips) for core in range(CORES)]
    up_cut = chunks // 3
    down_cut = 2 * chunks // 3

    vmem = pl.BlockSpec(memory_space=pltpu.VMEM)
    hbm = pl.BlockSpec(memory_space=pltpu.HBM)
    anywhere = pl.BlockSpec(memory_space=pl.ANY)
    row_bytes = total_tokens * model_width * 2

    def keep_far(value):
        return pltpu.with_memory_space_constraint(value, pltpu.HBM)

    def near(first, last):
        return pltpu.VMEM((last - first, chunk_rows, model_width), jnp.bfloat16)

    def cost(loads, dots):
        return pl.CostEstimate(flops=dots, bytes_accessed=loads, transcendentals=0)

    def scoped(size):
        return pltpu.CompilerParams(vmem_limit_bytes=size + (2 << 20))

    edge = pltpu.get_tpu_info().mxu_column_size
    accs = []
    size = units // 3 if units % 3 == 0 else 1

    def accs(count):
        if edge != 2 * total_tokens or model_width % edge != 0 or 2 * count * unit > 1024 or units % 12 != 0:
            return []
        return [pltpu.ACC(number)((unit, edge), jnp.float32) for number in range(2) for _ in range(2 * count)]

    cut = (chunks, chunk_rows, model_width)
    gate, up, down = (keep_far(weight.reshape(cut)) for weight in (gate_weight, up_weight, down_weight))

    tokens_beside = swap(tokens, "dp", 1)
    tokens_far = [swap(tokens, "dp", chip * CORES) for chip in range(1, chips)]
    plan = [(0, chunks), (0, up_cut)]
    packed, gate_near, up_near = pl.pallas_call(
        functools.partial(load_pack_kernel, plan),
        out_shape=(
            jax.ShapeDtypeStruct((tok_dev, model_width + extra), jnp.bfloat16),
            near(*plan[0]),
            near(*plan[1]),
        ),
        in_specs=[hbm] * 5,
        out_specs=(vmem,) * 3,
        scratch_shapes=[
            pltpu.VMEM((tok_dev, experts_all), jnp.float32),
            pltpu.VMEM((top, tok_dev), jnp.int32),
            pltpu.VMEM((tok_dev, extra), jnp.float32),
            pltpu.SemaphoreType.DMA((3,)),
            pltpu.SemaphoreType.DMA((chunks + up_cut,)),
        ],
        compiler_params=scoped(0),
        cost_estimate=cost(chunks + up_cut, 0),
        name="load_pack",
    )(keep_far(logits), keep_far(routes.T), keep_far(cotangent), gate, up)
    packed_far = [swap(packed, "dp", chip * CORES) for chip in range(1, chips)]
    packed_beside = swap(packed, "dp", 1)
    tokens_far, gate_near, up_near = lax.optimization_barrier((tokens_far, gate_near, up_near))
    token_pieces = [tokens, tokens_beside]
    for far in tokens_far:
        token_pieces += [far, swap(far, "dp", 1)]
    plan = [(up_cut, chunks), (0, down_cut)]
    loads = chunks - up_cut + down_cut
    hidden, mine, down_near = pl.pallas_call(
        with_accs(functools.partial(hidden_kernel, distances, plan, size), accs(size)),
        out_shape=(
            jax.ShapeDtypeStruct((units, unit, total_tokens), jnp.float32),
            jax.ShapeDtypeStruct((total_tokens, model_width // data_count), jnp.bfloat16),
            near(*plan[1]),
        ),
        in_specs=[vmem] * (data_count + 2) + [hbm] * 2,
        out_specs=(vmem,) * 3,
        scratch_shapes=[
            pltpu.VMEM((total_tokens, model_width), jnp.bfloat16),
            near(*plan[0]),
            pltpu.SemaphoreType.DMA((loads,)),
            pltpu.SemaphoreType.DMA,
        ],
        compiler_params=scoped((chunks - up_cut) * cut[1] * cut[2] * 2 + (1 if accs(size) else 3) * row_bytes),
        cost_estimate=cost(loads, 2 * chunks),
        name="hidden",
    )(*token_pieces, gate_near, up_near, up, down)

    packed_far, hidden = lax.optimization_barrier((packed_far, hidden))
    packed_pieces = [packed, packed_beside]
    for far in packed_far:
        packed_pieces += [far, swap(far, "dp", 1)]
    plan = [(down_cut, down_cut + 1)]
    down_mid = pl.pallas_call(
        functools.partial(load_kernel, plan),
        out_shape=near(*plan[0]),
        in_specs=[hbm, anywhere],
        out_specs=vmem,
        scratch_shapes=[pltpu.SemaphoreType.DMA((1,))],
        compiler_params=scoped(0),
        cost_estimate=cost(1, 0),
        name="load_down",
    )(down, packed_far[0])

    plan = [(down_cut + 1, chunks)]
    table = jax.ShapeDtypeStruct((experts_all, total_tokens), jnp.float32)
    partial, probs, chosen = pl.pallas_call(
        with_accs(functools.partial(score_kernel, distances, plan, top), accs(units // 4)),
        out_shape=(
            jax.ShapeDtypeStruct((data_count * expert_count, local_experts, total_tokens), jnp.float32),
            table,
            table,
        ),
        in_specs=[vmem] * (data_count + 3) + [hbm],
        out_specs=(vmem, vmem, vmem),
        scratch_shapes=[
            pltpu.VMEM((total_tokens, model_width + extra), jnp.bfloat16),
            near(*plan[0]),
            pltpu.SemaphoreType.DMA((chunks - down_cut - 1,)),
        ],
        compiler_params=scoped((chunks - down_cut - 1) * cut[1] * cut[2] * 2 + 3 * row_bytes),
        cost_estimate=cost(chunks - down_cut, chunks),
        name="scores",
    )(*packed_pieces, hidden, down_near, down_mid, down)

    score_blocks = lax.all_to_all(partial, ("dp", "expert"), split_axis=0, concat_axis=0, tiled=True)

    logit_grad, router_grad = pl.pallas_call(
        functools.partial(gradient_kernel, data_count),
        out_shape=(
            jax.ShapeDtypeStruct((tok_dev, experts_all), jnp.float32),
            jax.ShapeDtypeStruct((experts_all, model_width // data_count), jnp.float32),
        ),
        in_specs=[vmem] * 4,
        out_specs=(hbm, hbm),
        scratch_shapes=[
            pltpu.VMEM((total_tokens, experts_all), jnp.float32),
            pltpu.VMEM((experts_all, model_width // data_count), jnp.float32),
            pltpu.SemaphoreType.DMA((3,)),
        ],
        compiler_params=scoped(4 << 20),
        name="gradient",
    )(score_blocks, probs, chosen, mine)
    return logit_grad, router_grad.T


def solution(mesh):
    placed = (
        P("dp", None),
        P("dp", None),
        P("dp", None),
        P("dp", None),
        P("expert", "dp", None),
        P("expert", "dp", None),
        P("expert", "dp", None),
    )
    mapped = jax.shard_map(
        per_device,
        mesh=mesh,
        in_specs=placed,
        out_specs=(P("dp", None), P("dp", None)),
        check_vma=False,
    )

    def run(*args):
        with jax.sharding.use_abstract_mesh(mesh.abstract_mesh):
            return mapped(*args)

    return run
```

```python
import functools

import jax
import jax.numpy as jnp
from jax import lax
from jax.experimental import pallas as pl
from jax.experimental.pallas import tpu as pltpu
from jax.sharding import PartitionSpec as P

CORES = 2


def dot_rows(a, b):
    return lax.dot_general(a, b, (((1,), (1,)), ((), ())), preferred_element_type=jnp.float32)


def stream_dots(rows, lanes, size, accs, ready, finish):
    count = len(lanes[0])
    groups = [range(first, min(first + size, count)) for first in range(0, count, size)]

    def dots_of(number, place):
        if not accs:
            return [dot_rows(lane[place][...], rows[...]) for lane in lanes]
        at = number % 2 * size + place % size
        return [pltpu.matmul_pop(acc[at])[:, : rows.shape[0]] for acc in accs]

    def read(number):
        for place in groups[number]:
            finish(place, dots_of(number, place))

    if not accs:
        for number in range(len(groups)):
            ready(number)
            read(number)
        return
    edge = accs[0][0].shape[1]
    steps = rows.shape[1] // edge

    def push(turn):
        first = turn % steps * edge
        both = jnp.concatenate([rows[:, first : first + edge]] * (edge // rows.shape[0]), axis=0)
        for unit in range(len(lanes)):
            pltpu.matmul_push_rhs(both, turn % 2, unit, transpose=True)

    push(0)
    for turn in range(len(groups) * steps):
        number, step = divmod(turn, steps)
        if step == 0:
            ready(number)
        for place in groups[number]:
            for lane, acc in zip(lanes, accs):
                part = lane[place][:, step * edge : (step + 1) * edge]
                staged = turn % 2 if place == groups[number][0] else None
                pltpu.matmul_acc_lhs(acc[number % 2 * size + place % size], part, load_staged_rhs=staged)
            if place == groups[number][0] and turn + 1 < len(groups) * steps:
                push(turn + 1)
        if step == 0 and number > 0:
            read(number - 1)
    read(len(groups) - 1)


def with_accs(kernel, shapes):
    if not shapes:
        return kernel
    half = len(shapes) // 2

    def body(*refs):
        pl.run_scoped(lambda *accs: kernel(*refs, accs=(accs[:half], accs[half:])), *shapes)

    return body


def place_rows(pieces, distances, rows):
    me = lax.axis_index("dp")
    tok_dev = pieces[0].shape[0]
    for piece, distance in zip(pieces, distances):
        start = pl.multiple_of(jnp.bitwise_xor(me, distance) * tok_dev, tok_dev)
        rows[pl.ds(start, tok_dev), :] = piece[...]


def start_loads(plan, sources, nears, sems):
    copies, number = [], 0
    for (first, last), source, near in zip(plan, sources, nears):
        for chunk in range(first, last):
            copies.append(pltpu.make_async_copy(source.at[chunk], near.at[chunk - first], sems.at[number]))
            number += 1
    for copy in copies:
        copy.start()
    return copies


def load_pack_kernel(plan, logits, routes, cotangent, gate, up, packed, gate_near, up_near, *scratch):
    logits_near, routes_near, columns, sems, load_sems = scratch
    model_width = cotangent.shape[1]
    copies = [
        pltpu.make_async_copy(logits, logits_near, sems.at[0]),
        pltpu.make_async_copy(routes, routes_near, sems.at[1]),
        pltpu.make_async_copy(cotangent, packed.at[:, :model_width], sems.at[2]),
    ]
    for copy in copies:
        copy.start()
    loads = start_loads(plan, [gate, up], [gate_near, up_near], load_sems)
    columns[...] = jnp.zeros(columns.shape, jnp.float32)
    copies[0].wait()
    left = logits_near[...]
    experts_all = left.shape[1]
    for term in range(3):
        rounded = left.astype(jnp.bfloat16).astype(jnp.float32)
        columns[:, term * experts_all : (term + 1) * experts_all] = rounded
        left = left - rounded
    copies[1].wait()
    columns[:, 3 * experts_all : 3 * experts_all + routes.shape[0]] = routes_near[...].astype(jnp.float32).T
    packed[:, model_width:] = columns[...].astype(jnp.bfloat16)
    copies[2].wait()
    for copy in loads:
        copy.wait()


def blocks_of(buffers, unit):
    return [
        buffer.at[chunk, first : first + unit]
        for buffer in buffers
        for chunk in range(buffer.shape[0])
        for first in range(0, buffer.shape[1], unit)
    ]


def gated(dots):
    gate_pre, up_pre = dots
    return gate_pre / (1.0 + jnp.exp(-gate_pre)) * up_pre


def stream_hidden(rows, lanes, size, accs, ready, hidden):
    def finish(place, dots):
        gate_pre, up_pre = dots
        hidden[place] = gate_pre / (1.0 + jnp.exp(-gate_pre)) * up_pre

    stream_dots(rows, lanes, size, accs, ready, finish)


def first_hidden_kernel(distances, plan, size, *refs, accs=()):
    count = len(distances)
    pieces, refs = refs[:count], refs[count:]
    gate, up, gate_far, up_far, hidden, mine, gate_last, up_last, rows, gate_mid, up_mid, sems, mine_sem = refs
    loads = start_loads(
        plan, [gate_far, up_far, gate_far, up_far], [gate_mid, up_mid, gate_last, up_last], sems
    )
    place_rows(pieces, distances, rows)
    width = mine.shape[1]
    start = pl.multiple_of(lax.axis_index("dp") * width, width)
    own = pltpu.make_async_copy(rows.at[:, pl.ds(start, width)], mine, mine_sem)
    own.start()
    unit = hidden.shape[1]
    lanes = [blocks_of([gate, gate_mid], unit), blocks_of([up, up_mid], unit)]
    there = gate.shape[0] * gate.shape[1] // unit
    waited = [0]

    def ready(group):
        if (group + 1) * size > there and waited[0] == 0:
            waited[0] = gate_mid.shape[0] + up_mid.shape[0]
            for copy in loads[: waited[0]]:
                copy.wait()

    stream_hidden(rows, lanes, size, accs, ready, hidden)
    own.wait()
    for copy in loads[waited[0] :]:
        copy.wait()


def second_hidden_kernel(distances, size, *refs, accs=()):
    count = len(distances)
    pieces, (gate, up, after, hidden, rows) = refs[:count], refs[count:]
    place_rows(pieces, distances, rows)
    unit = hidden.shape[1]
    lanes = [blocks_of([gate], unit), blocks_of([up], unit)]
    stream_hidden(rows, lanes, size, accs, lambda group: None, hidden)


def score_kernel(distances, top, *refs, accs=()):
    count = len(distances)
    pieces, refs = refs[:count], refs[count:]
    hidden_0, hidden_1, down, partial, probs, chosen, rows = refs
    model_width = down.shape[2]
    experts_all = probs.shape[0]
    place_rows(pieces, distances, rows)
    local_experts = partial.shape[1]
    blocks = blocks_of([down], hidden_0.shape[1])
    hidden = [held.at[place] for held in (hidden_0, hidden_1) for place in range(held.shape[0])]
    per_expert = len(blocks) // local_experts
    size = len(blocks) // 4
    order = [
        [group * 2 * size + lane * size + place for group in range(2) for place in range(size)] for lane in range(2)
    ]
    sums = [None] * local_experts

    def routing():
        packed = rows[:, model_width:].astype(jnp.float32).T
        terms = [packed[term * experts_all : (term + 1) * experts_all] for term in range(3)]
        logits = terms[0] + terms[1] + terms[2]
        raised = jnp.exp(logits - jnp.max(logits, axis=0, keepdims=True))
        probs[...] = raised / jnp.sum(raised, axis=0, keepdims=True)
        number = lax.broadcasted_iota(jnp.int32, logits.shape, 0).astype(jnp.float32)
        named = jnp.zeros(logits.shape, jnp.float32)
        for slot in range(3 * experts_all, 3 * experts_all + top):
            named = named + (packed[slot : slot + 1] == number).astype(jnp.float32)
        chosen[...] = named

    def finish(place, dots):
        if place == 0:
            routing()
        for lane, paired in zip(order, dots):
            block = lane[place]
            product = hidden[block][...] * paired
            expert = block // per_expert
            sums[expert] = product if sums[expert] is None else sums[expert] + product

    lanes = [[blocks[block] for block in lane] for lane in order]
    stream_dots(rows.at[:, :model_width], lanes, size, accs, lambda group: None, finish)
    lines = [jnp.sum(term, axis=0, keepdims=True) for term in sums]
    partial[...] = jnp.broadcast_to(jnp.concatenate(lines, axis=0)[None], partial.shape)


def gradient_kernel(data_count, blocks, probs_ref, chosen_ref, mine, logit_grad, router_grad, grads, held, sems):
    experts_all, total_tokens = probs_ref.shape
    scores = jnp.sum(blocks[...].reshape((data_count, experts_all, total_tokens)), axis=0)
    probs, chosen = probs_ref[...], chosen_ref[...]
    mass = jnp.sum(probs * chosen, axis=0, keepdims=True)
    weighted = jnp.sum(probs * chosen * scores, axis=0, keepdims=True)
    prob_grad = scores / mass - chosen * weighted / (mass * mass)
    grad = probs * (prob_grad - jnp.sum(probs * prob_grad, axis=0, keepdims=True))
    half = mine.shape[1] // 2
    copies = []
    for number in range(2):
        part = pl.ds(number * half, half)
        held[:, part] = jnp.dot(grad.astype(jnp.bfloat16), mine[:, part], preferred_element_type=jnp.float32)
        copies.append(pltpu.make_async_copy(held.at[:, part], router_grad.at[:, part], sems.at[number]))
        copies[number].start()
    grads[...] = grad.T
    tok_dev = logit_grad.shape[0]
    start = pl.multiple_of(lax.axis_index("dp") * tok_dev, tok_dev)
    copies.append(pltpu.make_async_copy(grads.at[pl.ds(start, tok_dev)], logit_grad, sems.at[2]))
    copies[2].start()
    for copy in copies:
        copy.wait()


def swap(value, axis, distance):
    return lax.ppermute(value, axis, [(index, index ^ distance) for index in range(lax.axis_size(axis))])


def per_device(tokens, cotangent, logits, routes, gate_weight, up_weight, down_weight):
    data_count = lax.axis_size("dp")
    expert_count = lax.axis_size("expert")
    tok_dev, model_width = tokens.shape
    local_experts, ff_dev = gate_weight.shape[:2]
    total_tokens = tok_dev * data_count
    experts_all = local_experts * expert_count
    top = routes.shape[1]
    unit = 128 if ff_dev % 128 == 0 else ff_dev
    units = local_experts * ff_dev // unit
    chunk_rows = unit * (2 if unit == 128 and units % 2 == 0 else 1)
    chunks = local_experts * ff_dev // chunk_rows
    extra = -(-(3 * experts_all + top) // 128) * 128
    chips = data_count // CORES
    distances = [chip * CORES + core for chip in range(chips) for core in range(CORES)]
    first = 2 * chunks // 3

    vmem = pl.BlockSpec(memory_space=pltpu.VMEM)
    hbm = pl.BlockSpec(memory_space=pltpu.HBM)
    anywhere = pl.BlockSpec(memory_space=pl.ANY)
    row_bytes = total_tokens * model_width * 2

    def keep_far(value):
        return pltpu.with_memory_space_constraint(value, pltpu.HBM)

    def near(first, last):
        return pltpu.VMEM((last - first, chunk_rows, model_width), jnp.bfloat16)

    def cost(loads, dots):
        return pl.CostEstimate(flops=dots, bytes_accessed=loads, transcendentals=0)

    def scoped(size):
        return pltpu.CompilerParams(vmem_limit_bytes=size + (2 << 20))

    edge = pltpu.get_tpu_info().mxu_column_size
    accs = []
    size = units // 3 if units % 3 == 0 else 1

    def accs(count):
        if edge != 2 * total_tokens or model_width % edge != 0 or 2 * count * unit > 1024 or units % 12 != 0:
            return []
        return [pltpu.ACC(number)((unit, edge), jnp.float32) for number in range(2) for _ in range(2 * count)]

    cut = (chunks, chunk_rows, model_width)
    gate, up = (keep_far(weight.reshape(cut)) for weight in (gate_weight, up_weight))
    down = pltpu.with_memory_space_constraint(down_weight.reshape(cut), pltpu.VMEM)

    tokens_beside = swap(tokens, "dp", 1)
    tokens_far = [swap(tokens, "dp", chip * CORES) for chip in range(1, chips)]
    plan = [(0, first), (0, first)]
    packed, gate_near, up_near = pl.pallas_call(
        functools.partial(load_pack_kernel, plan),
        out_shape=(
            jax.ShapeDtypeStruct((tok_dev, model_width + extra), jnp.bfloat16),
            near(*plan[0]),
            near(*plan[1]),
        ),
        in_specs=[hbm] * 5,
        out_specs=(vmem,) * 3,
        scratch_shapes=[
            pltpu.VMEM((tok_dev, experts_all), jnp.float32),
            pltpu.VMEM((top, tok_dev), jnp.int32),
            pltpu.VMEM((tok_dev, extra), jnp.float32),
            pltpu.SemaphoreType.DMA((3,)),
            pltpu.SemaphoreType.DMA((2 * first,)),
        ],
        compiler_params=scoped(0),
        cost_estimate=cost(2 * first, 0),
        name="load_pack",
    )(keep_far(logits), keep_far(routes.T), keep_far(cotangent), gate, up)
    packed_far = [swap(packed, "dp", chip * CORES) for chip in range(1, chips)]
    packed_beside = swap(packed, "dp", 1)
    tokens_far, gate_near, up_near = lax.optimization_barrier((tokens_far, gate_near, up_near))
    token_pieces = [tokens, tokens_beside]
    for far in tokens_far:
        token_pieces += [far, swap(far, "dp", 1)]
    plan = [(first, chunks - 1), (first, chunks - 1), (chunks - 1, chunks), (chunks - 1, chunks)]
    loads = 2 * (chunks - first)
    places = units // chunks
    rows_scratch = pltpu.VMEM((total_tokens, model_width), jnp.bfloat16)
    hidden_0, mine, gate_last, up_last = pl.pallas_call(
        with_accs(functools.partial(first_hidden_kernel, distances, plan, size), accs(size)),
        out_shape=(
            jax.ShapeDtypeStruct((units - places, unit, total_tokens), jnp.float32),
            jax.ShapeDtypeStruct((total_tokens, model_width // data_count), jnp.bfloat16),
            near(*plan[2]),
            near(*plan[3]),
        ),
        in_specs=[vmem] * (data_count + 2) + [hbm] * 2,
        out_specs=(vmem,) * 4,
        scratch_shapes=[
            rows_scratch,
            near(*plan[0]),
            near(*plan[1]),
            pltpu.SemaphoreType.DMA((loads,)),
            pltpu.SemaphoreType.DMA,
        ],
        compiler_params=scoped(loads * cut[1] * cut[2] * 2 + (1 if accs(size) else 3) * row_bytes),
        cost_estimate=cost(loads, 2 * chunks),
        name="hidden_first",
    )(*token_pieces, gate_near, up_near, gate, up)

    packed_far, hidden_0 = lax.optimization_barrier((packed_far, hidden_0))
    hidden_1 = pl.pallas_call(
        with_accs(functools.partial(second_hidden_kernel, distances, size), accs(size)),
        out_shape=jax.ShapeDtypeStruct((places, unit, total_tokens), jnp.float32),
        in_specs=[vmem] * (data_count + 2) + [anywhere],
        out_specs=vmem,
        scratch_shapes=[rows_scratch],
        compiler_params=scoped((1 if accs(size) else 3) * row_bytes),
        cost_estimate=cost(1, 2),
        name="hidden_second",
    )(*token_pieces, gate_last, up_last, packed_far[0])

    packed_pieces = [packed, packed_beside]
    for far in packed_far:
        packed_pieces += [far, swap(far, "dp", 1)]
    table = jax.ShapeDtypeStruct((experts_all, total_tokens), jnp.float32)
    partial, probs, chosen = pl.pallas_call(
        with_accs(functools.partial(score_kernel, distances, top), accs(units // 4)),
        out_shape=(
            jax.ShapeDtypeStruct((data_count * expert_count, local_experts, total_tokens), jnp.float32),
            table,
            table,
        ),
        in_specs=[vmem] * (data_count + 3),
        out_specs=(vmem, vmem, vmem),
        scratch_shapes=[
            pltpu.VMEM((total_tokens, model_width + extra), jnp.bfloat16),
        ],
        compiler_params=scoped(3 * row_bytes),
        cost_estimate=cost(1, 1),
        name="scores",
    )(*packed_pieces, hidden_0, hidden_1, down)

    score_blocks = lax.all_to_all(partial, ("dp", "expert"), split_axis=0, concat_axis=0, tiled=True)

    logit_grad, router_grad = pl.pallas_call(
        functools.partial(gradient_kernel, data_count),
        out_shape=(
            jax.ShapeDtypeStruct((tok_dev, experts_all), jnp.float32),
            jax.ShapeDtypeStruct((experts_all, model_width // data_count), jnp.float32),
        ),
        in_specs=[vmem] * 4,
        out_specs=(hbm, hbm),
        scratch_shapes=[
            pltpu.VMEM((total_tokens, experts_all), jnp.float32),
            pltpu.VMEM((experts_all, model_width // data_count), jnp.float32),
            pltpu.SemaphoreType.DMA((3,)),
        ],
        compiler_params=scoped(4 << 20),
        name="gradient",
    )(score_blocks, probs, chosen, mine)
    return logit_grad, router_grad.T


def solution(mesh):
    placed = (
        P("dp", None),
        P("dp", None),
        P("dp", None),
        P("dp", None),
        P("expert", "dp", None),
        P("expert", "dp", None),
        P("expert", "dp", None),
    )
    mapped = jax.shard_map(
        per_device,
        mesh=mesh,
        in_specs=placed,
        out_specs=(P("dp", None), P("dp", None)),
        check_vma=False,
    )

    def run(*args):
        with jax.sharding.use_abstract_mesh(mesh.abstract_mesh):
            return mapped(*args)

    return run
```

```python
import functools

import jax
import jax.numpy as jnp
from jax import lax
from jax.experimental import pallas as pl
from jax.experimental.pallas import tpu as pltpu
from jax.sharding import PartitionSpec as P

CORES = 2


def dot_rows(a, b):
    return lax.dot_general(a, b, (((1,), (1,)), ((), ())), preferred_element_type=jnp.float32)


def stream_dots(rows, lanes, size, accs, ready, finish):
    count = len(lanes[0])
    groups = [range(first, min(first + size, count)) for first in range(0, count, size)]

    def dots_of(number, place):
        if not accs:
            return [dot_rows(lane[place][...], rows[...]) for lane in lanes]
        at = number % 2 * size + place % size
        return [pltpu.matmul_pop(acc[at])[:, : rows.shape[0]] for acc in accs]

    def read(number):
        for place in groups[number]:
            finish(place, dots_of(number, place))

    if not accs:
        for number in range(len(groups)):
            ready(number)
            read(number)
        return
    edge = accs[0][0].shape[1]
    steps = rows.shape[1] // edge

    def push(turn):
        first = turn % steps * edge
        both = jnp.concatenate([rows[:, first : first + edge]] * (edge // rows.shape[0]), axis=0)
        for unit in range(len(lanes)):
            pltpu.matmul_push_rhs(both, turn % 2, unit, transpose=True)

    push(0)
    for turn in range(len(groups) * steps):
        number, step = divmod(turn, steps)
        if step == 0:
            ready(number)
        for place in groups[number]:
            for lane, acc in zip(lanes, accs):
                part = lane[place][:, step * edge : (step + 1) * edge]
                staged = turn % 2 if place == groups[number][0] else None
                pltpu.matmul_acc_lhs(acc[number % 2 * size + place % size], part, load_staged_rhs=staged)
            if place == groups[number][0] and turn + 1 < len(groups) * steps:
                push(turn + 1)
        if step == 0 and number > 0:
            read(number - 1)
    read(len(groups) - 1)


def with_accs(kernel, shapes):
    if not shapes:
        return kernel
    half = len(shapes) // 2

    def body(*refs):
        pl.run_scoped(lambda *accs: kernel(*refs, accs=(accs[:half], accs[half:])), *shapes)

    return body


def place_rows(pieces, distances, rows):
    me = lax.axis_index("dp")
    tok_dev = pieces[0].shape[0]
    for piece, distance in zip(pieces, distances):
        start = pl.multiple_of(jnp.bitwise_xor(me, distance) * tok_dev, tok_dev)
        rows[pl.ds(start, tok_dev), :] = piece[...]


def start_loads(plan, sources, nears, sems):
    copies, number = [], 0
    for (first, last), source, near in zip(plan, sources, nears):
        for chunk in range(first, last):
            copies.append(pltpu.make_async_copy(source.at[chunk], near.at[chunk - first], sems.at[number]))
            number += 1
    for copy in copies:
        copy.start()
    return copies


def load_pack_kernel(plan, logits, routes, cotangent, gate, up, packed, gate_near, up_near, *scratch):
    logits_near, routes_near, columns, sems, load_sems = scratch
    model_width = cotangent.shape[1]
    copies = [
        pltpu.make_async_copy(logits, logits_near, sems.at[0]),
        pltpu.make_async_copy(routes, routes_near, sems.at[1]),
        pltpu.make_async_copy(cotangent, packed.at[:, :model_width], sems.at[2]),
    ]
    for copy in copies:
        copy.start()
    loads = start_loads(plan, [gate, up], [gate_near, up_near], load_sems)
    columns[...] = jnp.zeros(columns.shape, jnp.float32)
    copies[0].wait()
    left = logits_near[...]
    experts_all = left.shape[1]
    for term in range(3):
        rounded = left.astype(jnp.bfloat16).astype(jnp.float32)
        columns[:, term * experts_all : (term + 1) * experts_all] = rounded
        left = left - rounded
    copies[1].wait()
    columns[:, 3 * experts_all : 3 * experts_all + routes.shape[0]] = routes_near[...].astype(jnp.float32).T
    packed[:, model_width:] = columns[...].astype(jnp.bfloat16)
    copies[2].wait()
    for copy in loads:
        copy.wait()


def blocks_of(buffers, unit):
    return [
        buffer.at[chunk, first : first + unit]
        for buffer in buffers
        for chunk in range(buffer.shape[0])
        for first in range(0, buffer.shape[1], unit)
    ]


def gated(dots):
    gate_pre, up_pre = dots
    return gate_pre / (1.0 + jnp.exp(-gate_pre)) * up_pre


def stream_hidden(rows, lanes, size, accs, ready, hidden):
    def finish(place, dots):
        gate_pre, up_pre = dots
        hidden[place] = gate_pre / (1.0 + jnp.exp(-gate_pre)) * up_pre

    stream_dots(rows, lanes, size, accs, ready, finish)


def first_hidden_kernel(distances, plan, size, *refs, accs=()):
    count = len(distances)
    pieces, refs = refs[:count], refs[count:]
    gate, up, gate_far, up_far, hidden, mine, gate_last, up_last, rows, gate_mid, up_mid, sems, mine_sem = refs
    loads = start_loads(
        plan, [gate_far, up_far, gate_far, up_far], [gate_mid, up_mid, gate_last, up_last], sems
    )
    place_rows(pieces, distances, rows)
    width = mine.shape[1]
    start = pl.multiple_of(lax.axis_index("dp") * width, width)
    own = pltpu.make_async_copy(rows.at[:, pl.ds(start, width)], mine, mine_sem)
    own.start()
    unit = hidden.shape[1]
    lanes = [blocks_of([gate, gate_mid], unit), blocks_of([up, up_mid], unit)]
    there = gate.shape[0] * gate.shape[1] // unit
    waited = [0]

    def ready(group):
        if (group + 1) * size > there and waited[0] == 0:
            waited[0] = gate_mid.shape[0] + up_mid.shape[0]
            for copy in loads[: waited[0]]:
                copy.wait()

    stream_hidden(rows, lanes, size, accs, ready, hidden)
    own.wait()
    for copy in loads[waited[0] :]:
        copy.wait()


def second_hidden_kernel(distances, size, *refs, accs=()):
    count = len(distances)
    pieces, (gate, up, after, hidden, rows) = refs[:count], refs[count:]
    place_rows(pieces, distances, rows)
    unit = hidden.shape[1]
    lanes = [blocks_of([gate], unit), blocks_of([up], unit)]
    stream_hidden(rows, lanes, size, accs, lambda group: None, hidden)


def score_kernel(distances, top, *refs, accs=()):
    count = len(distances)
    pieces, refs = refs[:count], refs[count:]
    hidden_0, hidden_1, down, partial, probs, chosen, rows = refs
    model_width = down.shape[2]
    experts_all = probs.shape[0]
    place_rows(pieces, distances, rows)
    local_experts = partial.shape[1]
    blocks = blocks_of([down], hidden_0.shape[1])
    hidden = [held.at[place] for held in (hidden_0, hidden_1) for place in range(held.shape[0])]
    per_expert = len(blocks) // local_experts
    size = len(blocks) // 4
    order = [
        [group * 2 * size + lane * size + place for group in range(2) for place in range(size)] for lane in range(2)
    ]
    sums = [None] * local_experts

    def routing():
        packed = rows[:, model_width:].astype(jnp.float32).T
        terms = [packed[term * experts_all : (term + 1) * experts_all] for term in range(3)]
        logits = terms[0] + terms[1] + terms[2]
        raised = jnp.exp(logits - jnp.max(logits, axis=0, keepdims=True))
        probs[...] = raised / jnp.sum(raised, axis=0, keepdims=True)
        number = lax.broadcasted_iota(jnp.int32, logits.shape, 0).astype(jnp.float32)
        named = jnp.zeros(logits.shape, jnp.float32)
        for slot in range(3 * experts_all, 3 * experts_all + top):
            named = named + (packed[slot : slot + 1] == number).astype(jnp.float32)
        chosen[...] = named

    def finish(place, dots):
        if place == 0:
            routing()
        for lane, paired in zip(order, dots):
            block = lane[place]
            product = hidden[block][...] * paired
            expert = block // per_expert
            sums[expert] = product if sums[expert] is None else sums[expert] + product

    lanes = [[blocks[block] for block in lane] for lane in order]
    stream_dots(rows.at[:, :model_width], lanes, size, accs, lambda group: None, finish)
    lines = [jnp.sum(term, axis=0, keepdims=True) for term in sums]
    partial[...] = jnp.broadcast_to(jnp.concatenate(lines, axis=0)[None], partial.shape)


def gradient_kernel(data_count, blocks, probs_ref, chosen_ref, mine, logit_grad, router_grad, grads, held, sems):
    experts_all, total_tokens = probs_ref.shape
    rows_of = [
        sum(blocks[first + part] for part in range(1, data_count)) + blocks[first]
        for first in range(0, blocks.shape[0], data_count)
    ]
    scores = jnp.concatenate(rows_of, axis=0)
    probs, chosen = probs_ref[...], chosen_ref[...]
    mass = jnp.sum(probs * chosen, axis=0, keepdims=True)
    weighted = jnp.sum(probs * chosen * scores, axis=0, keepdims=True)
    prob_grad = scores / mass - chosen * weighted / (mass * mass)
    grad = probs * (prob_grad - jnp.sum(probs * prob_grad, axis=0, keepdims=True))
    half = mine.shape[1] // 2
    copies = []
    for number in range(2):
        part = pl.ds(number * half, half)
        held[:, part] = jnp.dot(grad.astype(jnp.bfloat16), mine[:, part], preferred_element_type=jnp.float32)
        copies.append(pltpu.make_async_copy(held.at[:, part], router_grad.at[:, part], sems.at[number]))
        copies[number].start()
    grads[...] = grad.T
    tok_dev = logit_grad.shape[0]
    start = pl.multiple_of(lax.axis_index("dp") * tok_dev, tok_dev)
    copies.append(pltpu.make_async_copy(grads.at[pl.ds(start, tok_dev)], logit_grad, sems.at[2]))
    copies[2].start()
    for copy in copies:
        copy.wait()


def swap(value, axis, distance):
    return lax.ppermute(value, axis, [(index, index ^ distance) for index in range(lax.axis_size(axis))])


def per_device(tokens, cotangent, logits, routes, gate_weight, up_weight, down_weight):
    data_count = lax.axis_size("dp")
    expert_count = lax.axis_size("expert")
    tok_dev, model_width = tokens.shape
    local_experts, ff_dev = gate_weight.shape[:2]
    total_tokens = tok_dev * data_count
    experts_all = local_experts * expert_count
    top = routes.shape[1]
    unit = 128 if ff_dev % 128 == 0 else ff_dev
    units = local_experts * ff_dev // unit
    chunk_rows = unit * (2 if unit == 128 and units % 2 == 0 else 1)
    chunks = local_experts * ff_dev // chunk_rows
    extra = -(-(3 * experts_all + top) // 128) * 128
    chips = data_count // CORES
    distances = [chip * CORES + core for chip in range(chips) for core in range(CORES)]
    first = 2 * chunks // 3

    vmem = pl.BlockSpec(memory_space=pltpu.VMEM)
    hbm = pl.BlockSpec(memory_space=pltpu.HBM)
    anywhere = pl.BlockSpec(memory_space=pl.ANY)
    row_bytes = total_tokens * model_width * 2

    def keep_far(value):
        return pltpu.with_memory_space_constraint(value, pltpu.HBM)

    def near(first, last):
        return pltpu.VMEM((last - first, chunk_rows, model_width), jnp.bfloat16)

    def cost(loads, dots):
        return pl.CostEstimate(flops=dots, bytes_accessed=loads, transcendentals=0)

    def scoped(size):
        return pltpu.CompilerParams(vmem_limit_bytes=size + (2 << 20))

    edge = pltpu.get_tpu_info().mxu_column_size
    accs = []
    size = units // 3 if units % 3 == 0 else 1

    def accs(count):
        if edge != 2 * total_tokens or model_width % edge != 0 or 2 * count * unit > 1024 or units % 12 != 0:
            return []
        return [pltpu.ACC(number)((unit, edge), jnp.float32) for number in range(2) for _ in range(2 * count)]

    cut = (chunks, chunk_rows, model_width)
    gate, up = (keep_far(weight.reshape(cut)) for weight in (gate_weight, up_weight))
    down = pltpu.with_memory_space_constraint(down_weight.reshape(cut), pltpu.VMEM)

    tokens_beside = swap(tokens, "dp", 1)
    tokens_far = [swap(tokens, "dp", chip * CORES) for chip in range(1, chips)]
    plan = [(0, first), (0, first)]
    packed, gate_near, up_near = pl.pallas_call(
        functools.partial(load_pack_kernel, plan),
        out_shape=(
            jax.ShapeDtypeStruct((tok_dev, model_width + extra), jnp.bfloat16),
            near(*plan[0]),
            near(*plan[1]),
        ),
        in_specs=[hbm] * 5,
        out_specs=(vmem,) * 3,
        scratch_shapes=[
            pltpu.VMEM((tok_dev, experts_all), jnp.float32),
            pltpu.VMEM((top, tok_dev), jnp.int32),
            pltpu.VMEM((tok_dev, extra), jnp.float32),
            pltpu.SemaphoreType.DMA((3,)),
            pltpu.SemaphoreType.DMA((2 * first,)),
        ],
        compiler_params=scoped(0),
        cost_estimate=cost(2 * first, 0),
        name="load_pack",
    )(keep_far(logits), keep_far(routes.T), keep_far(cotangent), gate, up)
    packed_far = [swap(packed, "dp", chip * CORES) for chip in range(1, chips)]
    packed_beside = swap(packed, "dp", 1)
    tokens_far, gate_near, up_near = lax.optimization_barrier((tokens_far, gate_near, up_near))
    token_pieces = [tokens, tokens_beside]
    for far in tokens_far:
        token_pieces += [far, swap(far, "dp", 1)]
    plan = [(first, chunks - 1), (first, chunks - 1), (chunks - 1, chunks), (chunks - 1, chunks)]
    loads = 2 * (chunks - first)
    places = units // chunks
    rows_scratch = pltpu.VMEM((total_tokens, model_width), jnp.bfloat16)
    hidden_0, mine, gate_last, up_last = pl.pallas_call(
        with_accs(functools.partial(first_hidden_kernel, distances, plan, size), accs(size)),
        out_shape=(
            jax.ShapeDtypeStruct((units - places, unit, total_tokens), jnp.float32),
            jax.ShapeDtypeStruct((total_tokens, model_width // data_count), jnp.bfloat16),
            near(*plan[2]),
            near(*plan[3]),
        ),
        in_specs=[vmem] * (data_count + 2) + [hbm] * 2,
        out_specs=(vmem,) * 4,
        scratch_shapes=[
            rows_scratch,
            near(*plan[0]),
            near(*plan[1]),
            pltpu.SemaphoreType.DMA((loads,)),
            pltpu.SemaphoreType.DMA,
        ],
        compiler_params=scoped(loads * cut[1] * cut[2] * 2 + (1 if accs(size) else 3) * row_bytes),
        cost_estimate=cost(loads, 2 * chunks),
        name="hidden_first",
    )(*token_pieces, gate_near, up_near, gate, up)

    packed_far, hidden_0 = lax.optimization_barrier((packed_far, hidden_0))
    hidden_1 = pl.pallas_call(
        with_accs(functools.partial(second_hidden_kernel, distances, size), accs(size)),
        out_shape=jax.ShapeDtypeStruct((places, unit, total_tokens), jnp.float32),
        in_specs=[vmem] * (data_count + 2) + [anywhere],
        out_specs=vmem,
        scratch_shapes=[rows_scratch],
        compiler_params=scoped((1 if accs(size) else 3) * row_bytes),
        cost_estimate=cost(1, 2),
        name="hidden_second",
    )(*token_pieces, gate_last, up_last, packed_far[0])

    packed_pieces = [packed, packed_beside]
    for far in packed_far:
        packed_pieces += [far, swap(far, "dp", 1)]
    table = jax.ShapeDtypeStruct((experts_all, total_tokens), jnp.float32)
    partial, probs, chosen = pl.pallas_call(
        with_accs(functools.partial(score_kernel, distances, top), accs(units // 4)),
        out_shape=(
            jax.ShapeDtypeStruct((data_count * expert_count, local_experts, total_tokens), jnp.float32),
            table,
            table,
        ),
        in_specs=[vmem] * (data_count + 3),
        out_specs=(vmem, vmem, vmem),
        scratch_shapes=[
            pltpu.VMEM((total_tokens, model_width + extra), jnp.bfloat16),
        ],
        compiler_params=scoped(3 * row_bytes),
        cost_estimate=cost(1, 1),
        name="scores",
    )(*packed_pieces, hidden_0, hidden_1, down)

    score_blocks = lax.all_to_all(partial, ("expert", "dp"), split_axis=0, concat_axis=0, tiled=True)

    logit_grad, router_grad = pl.pallas_call(
        functools.partial(gradient_kernel, data_count),
        out_shape=(
            jax.ShapeDtypeStruct((tok_dev, experts_all), jnp.float32),
            jax.ShapeDtypeStruct((experts_all, model_width // data_count), jnp.float32),
        ),
        in_specs=[vmem] * 4,
        out_specs=(hbm, hbm),
        scratch_shapes=[
            pltpu.VMEM((total_tokens, experts_all), jnp.float32),
            pltpu.VMEM((experts_all, model_width // data_count), jnp.float32),
            pltpu.SemaphoreType.DMA((3,)),
        ],
        compiler_params=scoped(4 << 20),
        name="gradient",
    )(score_blocks, probs, chosen, mine)
    return logit_grad, router_grad.T


def solution(mesh):
    placed = (
        P("dp", None),
        P("dp", None),
        P("dp", None),
        P("dp", None),
        P("expert", "dp", None),
        P("expert", "dp", None),
        P("expert", "dp", None),
    )
    mapped = jax.shard_map(
        per_device,
        mesh=mesh,
        in_specs=placed,
        out_specs=(P("dp", None), P("dp", None)),
        check_vma=False,
    )

    def run(*args):
        with jax.sharding.use_abstract_mesh(mesh.abstract_mesh):
            return mapped(*args)

    return run
```

```python
import functools

import jax
import jax.numpy as jnp
from jax import lax
from jax.experimental import pallas as pl
from jax.experimental.pallas import tpu as pltpu
from jax.sharding import PartitionSpec as P

CORES = 2


def dot_rows(a, b):
    return lax.dot_general(a, b, (((1,), (1,)), ((), ())), preferred_element_type=jnp.float32)


def stream_dots(pieces, rows, lanes, size, accs, ready, finish):
    count = len(lanes[0])
    groups = [range(first, min(first + size, count)) for first in range(0, count, size)]

    def dots_of(number, place):
        if not accs:
            return [dot_rows(lane[place][...], rows[...]) for lane in lanes]
        at = number % 2 * size + place % size
        return [pltpu.matmul_pop(acc[at])[:, : rows.shape[0]] for acc in accs]

    def read(number):
        for place in groups[number]:
            finish(place, dots_of(number, place))

    if not accs:
        held = pieces[0].shape[0]
        for number, piece in enumerate(pieces):
            rows[number * held : (number + 1) * held, :] = piece[...]
        for number in range(len(groups)):
            ready(number)
            read(number)
        return
    edge = accs[0][0].shape[1]
    steps = rows.shape[1] // edge

    def push(turn):
        first = turn % steps * edge
        parts = [piece[:, first : first + edge] for piece in pieces]
        both = jnp.concatenate(parts * (edge // rows.shape[0]), axis=0)
        for unit in range(len(lanes)):
            pltpu.matmul_push_rhs(both, turn % 2, unit, transpose=True)

    push(0)
    for turn in range(len(groups) * steps):
        number, step = divmod(turn, steps)
        if step == 0:
            ready(number)
        for place in groups[number]:
            for lane, acc in zip(lanes, accs):
                part = lane[place][:, step * edge : (step + 1) * edge]
                staged = turn % 2 if place == groups[number][0] else None
                pltpu.matmul_acc_lhs(acc[number % 2 * size + place % size], part, load_staged_rhs=staged)
            if place == groups[number][0] and turn + 1 < len(groups) * steps:
                push(turn + 1)
        if step == 0 and number > 0:
            read(number - 1)
    read(len(groups) - 1)


def with_accs(kernel, shapes):
    if not shapes:
        return kernel
    half = len(shapes) // 2

    def body(*refs):
        pl.run_scoped(lambda *accs: kernel(*refs, accs=(accs[:half], accs[half:])), *shapes)

    return body


def place_rows(pieces, distances, rows):
    me = lax.axis_index("dp")
    tok_dev = pieces[0].shape[0]
    for piece, distance in zip(pieces, distances):
        start = pl.multiple_of(jnp.bitwise_xor(me, distance) * tok_dev, tok_dev)
        rows[pl.ds(start, tok_dev), :] = piece[...]


def start_loads(plan, sources, nears, sems):
    copies, number = [], 0
    for (first, last), source, near in zip(plan, sources, nears):
        for chunk in range(first, last):
            copies.append(pltpu.make_async_copy(source.at[chunk], near.at[chunk - first], sems.at[number]))
            number += 1
    for copy in copies:
        copy.start()
    return copies


def load_pack_kernel(plan, logits, routes, cotangent, gate, up, packed, gate_near, up_near, *scratch):
    logits_near, routes_near, columns, sems, load_sems = scratch
    model_width = cotangent.shape[1]
    copies = [
        pltpu.make_async_copy(logits, logits_near, sems.at[0]),
        pltpu.make_async_copy(routes, routes_near, sems.at[1]),
        pltpu.make_async_copy(cotangent, packed.at[:, :model_width], sems.at[2]),
    ]
    for copy in copies:
        copy.start()
    loads = start_loads(plan, [gate, up], [gate_near, up_near], load_sems)
    columns[...] = jnp.zeros(columns.shape, jnp.float32)
    copies[0].wait()
    left = logits_near[...]
    experts_all = left.shape[1]
    for term in range(3):
        rounded = left.astype(jnp.bfloat16).astype(jnp.float32)
        columns[:, term * experts_all : (term + 1) * experts_all] = rounded
        left = left - rounded
    copies[1].wait()
    columns[:, 3 * experts_all : 3 * experts_all + routes.shape[0]] = routes_near[...].astype(jnp.float32).T
    packed[:, model_width:] = columns[...].astype(jnp.bfloat16)
    copies[2].wait()
    for copy in loads:
        copy.wait()


def blocks_of(buffers, unit):
    return [
        buffer.at[chunk, first : first + unit]
        for buffer in buffers
        for chunk in range(buffer.shape[0])
        for first in range(0, buffer.shape[1], unit)
    ]


def gated(dots):
    gate_pre, up_pre = dots
    return gate_pre / (1.0 + jnp.exp(-gate_pre)) * up_pre


def stream_hidden(pieces, rows, lanes, size, accs, ready, hidden):
    def finish(place, dots):
        gate_pre, up_pre = dots
        hidden[place] = gate_pre / (1.0 + jnp.exp(-gate_pre)) * up_pre

    stream_dots(pieces, rows, lanes, size, accs, ready, finish)


def first_hidden_kernel(distances, plan, size, *refs, accs=()):
    count = len(distances)
    pieces, refs = refs[:count], refs[count:]
    gate, up, gate_far, up_far, hidden, mine, gate_last, up_last, rows, gate_mid, up_mid, sems, mine_sems = refs
    loads = start_loads(
        plan, [gate_far, up_far, gate_far, up_far], [gate_mid, up_mid, gate_last, up_last], sems
    )
    me = lax.axis_index("dp")
    width, held = mine.shape[1], pieces[0].shape[0]
    columns = pl.ds(pl.multiple_of(me * width, width), width)
    own = []
    for number, piece in enumerate(pieces):
        start = pl.multiple_of(jnp.bitwise_xor(me, distances[number]) * held, held)
        own.append(pltpu.make_async_copy(piece.at[:, columns], mine.at[pl.ds(start, held)], mine_sems.at[number]))
        own[number].start()
    unit = hidden.shape[1]
    lanes = [blocks_of([gate, gate_mid], unit), blocks_of([up, up_mid], unit)]
    there = gate.shape[0] * gate.shape[1] // unit
    waited = [0]

    def ready(group):
        if (group + 1) * size > there and waited[0] == 0:
            waited[0] = gate_mid.shape[0] + up_mid.shape[0]
            for copy in loads[: waited[0]]:
                copy.wait()

    stream_hidden(pieces, rows, lanes, size, accs, ready, hidden)
    for copy in own + loads[waited[0] :]:
        copy.wait()


def second_hidden_kernel(count, size, *refs, accs=()):
    pieces, (gate, up, after, hidden, rows) = refs[:count], refs[count:]
    unit = hidden.shape[1]
    lanes = [blocks_of([gate], unit), blocks_of([up], unit)]
    stream_hidden(pieces, rows, lanes, size, accs, lambda group: None, hidden)


def token_order(lines, count):
    me = lax.axis_index("dp")
    tokens = lines.shape[1]
    lane = lax.broadcasted_iota(jnp.int32, lines.shape, 1)
    distance = 1
    while distance < count:
        step = distance * (tokens // count)
        above, below = pltpu.roll(lines, tokens - step, 1), pltpu.roll(lines, step, 1)
        swapped = jnp.where(jnp.bitwise_and(lane, step) == 0, above, below)
        lines = jnp.where(jnp.bitwise_and(me, distance) != 0, swapped, lines)
        distance *= 2
    return lines


def score_kernel(distances, top, *refs, accs=()):
    count = len(distances)
    pieces, refs = refs[:count], refs[count:]
    hidden_0, hidden_1, down, partial, probs, chosen, rows, routing_rows = refs
    model_width = down.shape[2]
    experts_all = probs.shape[0]
    place_rows([piece.at[:, model_width:] for piece in pieces], distances, routing_rows)
    local_experts = partial.shape[1]
    blocks = blocks_of([down], hidden_0.shape[1])
    hidden = [held.at[place] for held in (hidden_0, hidden_1) for place in range(held.shape[0])]
    per_expert = len(blocks) // local_experts
    size = len(blocks) // 4
    order = [
        [group * 2 * size + lane * size + place for group in range(2) for place in range(size)] for lane in range(2)
    ]
    sums = [None] * local_experts

    def routing():
        packed = routing_rows[...].astype(jnp.float32).T
        terms = [packed[term * experts_all : (term + 1) * experts_all] for term in range(3)]
        logits = terms[0] + terms[1] + terms[2]
        raised = jnp.exp(logits - jnp.max(logits, axis=0, keepdims=True))
        probs[...] = raised / jnp.sum(raised, axis=0, keepdims=True)
        number = lax.broadcasted_iota(jnp.int32, logits.shape, 0).astype(jnp.float32)
        named = jnp.zeros(logits.shape, jnp.float32)
        for slot in range(3 * experts_all, 3 * experts_all + top):
            named = named + (packed[slot : slot + 1] == number).astype(jnp.float32)
        chosen[...] = named

    def finish(place, dots):
        if place == 0:
            routing()
        for lane, paired in zip(order, dots):
            block = lane[place]
            product = hidden[block][...] * paired
            expert = block // per_expert
            sums[expert] = product if sums[expert] is None else sums[expert] + product

    lanes = [[blocks[block] for block in lane] for lane in order]
    stream_dots([piece.at[:, :model_width] for piece in pieces], rows, lanes, size, accs, lambda group: None, finish)
    lines = [jnp.sum(term, axis=0, keepdims=True) for term in sums]
    scores = token_order(jnp.concatenate(lines, axis=0), count)
    partial[...] = jnp.broadcast_to(scores[None], partial.shape)


def gradient_kernel(data_count, blocks, probs_ref, chosen_ref, mine, logit_grad, router_grad, grads, held, sems):
    experts_all, total_tokens = probs_ref.shape
    scores = jnp.sum(blocks[...].reshape((data_count, experts_all, total_tokens)), axis=0)
    probs, chosen = probs_ref[...], chosen_ref[...]
    mass = jnp.sum(probs * chosen, axis=0, keepdims=True)
    weighted = jnp.sum(probs * chosen * scores, axis=0, keepdims=True)
    prob_grad = scores / mass - chosen * weighted / (mass * mass)
    grad = probs * (prob_grad - jnp.sum(probs * prob_grad, axis=0, keepdims=True))
    half = mine.shape[1] // 2
    copies = []
    for number in range(2):
        part = pl.ds(number * half, half)
        held[:, part] = jnp.dot(grad.astype(jnp.bfloat16), mine[:, part], preferred_element_type=jnp.float32)
        copies.append(pltpu.make_async_copy(held.at[:, part], router_grad.at[:, part], sems.at[number]))
        copies[number].start()
    grads[...] = grad.T
    tok_dev = logit_grad.shape[0]
    start = pl.multiple_of(lax.axis_index("dp") * tok_dev, tok_dev)
    copies.append(pltpu.make_async_copy(grads.at[pl.ds(start, tok_dev)], logit_grad, sems.at[2]))
    copies[2].start()
    for copy in copies:
        copy.wait()


def swap(value, axis, distance):
    return lax.ppermute(value, axis, [(index, index ^ distance) for index in range(lax.axis_size(axis))])


def per_device(tokens, cotangent, logits, routes, gate_weight, up_weight, down_weight):
    data_count = lax.axis_size("dp")
    expert_count = lax.axis_size("expert")
    tok_dev, model_width = tokens.shape
    local_experts, ff_dev = gate_weight.shape[:2]
    total_tokens = tok_dev * data_count
    experts_all = local_experts * expert_count
    top = routes.shape[1]
    unit = 128 if ff_dev % 128 == 0 else ff_dev
    units = local_experts * ff_dev // unit
    chunk_rows = unit * (2 if unit == 128 and units % 2 == 0 else 1)
    chunks = local_experts * ff_dev // chunk_rows
    extra = -(-(3 * experts_all + top) // 128) * 128
    chips = data_count // CORES
    distances = [chip * CORES + core for chip in range(chips) for core in range(CORES)]
    first = 2 * chunks // 3

    vmem = pl.BlockSpec(memory_space=pltpu.VMEM)
    hbm = pl.BlockSpec(memory_space=pltpu.HBM)
    anywhere = pl.BlockSpec(memory_space=pl.ANY)
    row_bytes = total_tokens * model_width * 2

    def keep_far(value):
        return pltpu.with_memory_space_constraint(value, pltpu.HBM)

    def near(first, last):
        return pltpu.VMEM((last - first, chunk_rows, model_width), jnp.bfloat16)

    def cost(loads, dots):
        return pl.CostEstimate(flops=dots, bytes_accessed=loads, transcendentals=0)

    def scoped(size):
        return pltpu.CompilerParams(vmem_limit_bytes=size + (2 << 20))

    edge = pltpu.get_tpu_info().mxu_column_size
    accs = []
    size = units // 3 if units % 3 == 0 else 1

    def accs(count):
        if edge != 2 * total_tokens or model_width % edge != 0 or 2 * count * unit > 1024 or units % 12 != 0:
            return []
        return [pltpu.ACC(number)((unit, edge), jnp.float32) for number in range(2) for _ in range(2 * count)]

    cut = (chunks, chunk_rows, model_width)
    gate, up = (keep_far(weight.reshape(cut)) for weight in (gate_weight, up_weight))
    down = pltpu.with_memory_space_constraint(down_weight.reshape(cut), pltpu.VMEM)

    tokens_beside = swap(tokens, "dp", 1)
    tokens_far = [swap(tokens, "dp", chip * CORES) for chip in range(1, chips)]
    plan = [(0, first), (0, first)]
    packed, gate_near, up_near = pl.pallas_call(
        functools.partial(load_pack_kernel, plan),
        out_shape=(
            jax.ShapeDtypeStruct((tok_dev, model_width + extra), jnp.bfloat16),
            near(*plan[0]),
            near(*plan[1]),
        ),
        in_specs=[hbm] * 5,
        out_specs=(vmem,) * 3,
        scratch_shapes=[
            pltpu.VMEM((tok_dev, experts_all), jnp.float32),
            pltpu.VMEM((top, tok_dev), jnp.int32),
            pltpu.VMEM((tok_dev, extra), jnp.float32),
            pltpu.SemaphoreType.DMA((3,)),
            pltpu.SemaphoreType.DMA((2 * first,)),
        ],
        compiler_params=scoped(0),
        cost_estimate=cost(2 * first, 0),
        name="load_pack",
    )(keep_far(logits), keep_far(routes.T), keep_far(cotangent), gate, up)
    packed_far = [swap(packed, "dp", chip * CORES) for chip in range(1, chips)]
    packed_beside = swap(packed, "dp", 1)
    tokens_far, gate_near, up_near = lax.optimization_barrier((tokens_far, gate_near, up_near))
    token_pieces = [tokens, tokens_beside]
    for far in tokens_far:
        token_pieces += [far, swap(far, "dp", 1)]
    plan = [(first, chunks - 1), (first, chunks - 1), (chunks - 1, chunks), (chunks - 1, chunks)]
    loads = 2 * (chunks - first)
    places = units // chunks
    rows_scratch = pltpu.VMEM((total_tokens, model_width), jnp.bfloat16)
    hidden_0, mine, gate_last, up_last = pl.pallas_call(
        with_accs(functools.partial(first_hidden_kernel, distances, plan, size), accs(size)),
        out_shape=(
            jax.ShapeDtypeStruct((units - places, unit, total_tokens), jnp.float32),
            jax.ShapeDtypeStruct((total_tokens, model_width // data_count), jnp.bfloat16),
            near(*plan[2]),
            near(*plan[3]),
        ),
        in_specs=[vmem] * (data_count + 2) + [hbm] * 2,
        out_specs=(vmem,) * 4,
        scratch_shapes=[
            rows_scratch,
            near(*plan[0]),
            near(*plan[1]),
            pltpu.SemaphoreType.DMA((loads,)),
            pltpu.SemaphoreType.DMA((data_count,)),
        ],
        compiler_params=scoped(loads * cut[1] * cut[2] * 2 + (1 if accs(size) else 3) * row_bytes),
        cost_estimate=cost(loads, 2 * chunks),
        name="hidden_first",
    )(*token_pieces, gate_near, up_near, gate, up)

    packed_far, hidden_0 = lax.optimization_barrier((packed_far, hidden_0))
    hidden_1 = pl.pallas_call(
        with_accs(functools.partial(second_hidden_kernel, data_count, size), accs(size)),
        out_shape=jax.ShapeDtypeStruct((places, unit, total_tokens), jnp.float32),
        in_specs=[vmem] * (data_count + 2) + [anywhere],
        out_specs=vmem,
        scratch_shapes=[rows_scratch],
        compiler_params=scoped((1 if accs(size) else 3) * row_bytes),
        cost_estimate=cost(1, 2),
        name="hidden_second",
    )(*token_pieces, gate_last, up_last, packed_far[0])

    packed_pieces = [packed, packed_beside]
    for far in packed_far:
        packed_pieces += [far, swap(far, "dp", 1)]
    table = jax.ShapeDtypeStruct((experts_all, total_tokens), jnp.float32)
    partial, probs, chosen = pl.pallas_call(
        with_accs(functools.partial(score_kernel, distances, top), accs(units // 4)),
        out_shape=(
            jax.ShapeDtypeStruct((data_count * expert_count, local_experts, total_tokens), jnp.float32),
            table,
            table,
        ),
        in_specs=[vmem] * (data_count + 3),
        out_specs=(vmem, vmem, vmem),
        scratch_shapes=[
            rows_scratch,
            pltpu.VMEM((total_tokens, extra), jnp.bfloat16),
        ],
        compiler_params=scoped(3 * row_bytes),
        cost_estimate=cost(1, 1),
        name="scores",
    )(*packed_pieces, hidden_0, hidden_1, down)

    score_blocks = lax.all_to_all(partial, ("dp", "expert"), split_axis=0, concat_axis=0, tiled=True)

    logit_grad, router_grad = pl.pallas_call(
        functools.partial(gradient_kernel, data_count),
        out_shape=(
            jax.ShapeDtypeStruct((tok_dev, experts_all), jnp.float32),
            jax.ShapeDtypeStruct((experts_all, model_width // data_count), jnp.float32),
        ),
        in_specs=[vmem] * 4,
        out_specs=(hbm, hbm),
        scratch_shapes=[
            pltpu.VMEM((total_tokens, experts_all), jnp.float32),
            pltpu.VMEM((experts_all, model_width // data_count), jnp.float32),
            pltpu.SemaphoreType.DMA((3,)),
        ],
        compiler_params=scoped(4 << 20),
        name="gradient",
    )(score_blocks, probs, chosen, mine)
    return logit_grad, router_grad.T


def solution(mesh):
    placed = (
        P("dp", None),
        P("dp", None),
        P("dp", None),
        P("dp", None),
        P("expert", "dp", None),
        P("expert", "dp", None),
        P("expert", "dp", None),
    )
    mapped = jax.shard_map(
        per_device,
        mesh=mesh,
        in_specs=placed,
        out_specs=(P("dp", None), P("dp", None)),
        check_vma=False,
    )

    def run(*args):
        with jax.sharding.use_abstract_mesh(mesh.abstract_mesh):
            return mapped(*args)

    return run
```

```python
import functools

import jax
import jax.numpy as jnp
from jax import lax
from jax.experimental import pallas as pl
from jax.experimental.pallas import tpu as pltpu
from jax.sharding import PartitionSpec as P

CORES = 2


def dot_rows(a, b):
    return lax.dot_general(a, b, (((1,), (1,)), ((), ())), preferred_element_type=jnp.float32)


def stream_dots(pieces, rows, lanes, size, accs, ready, finish, meanwhile=lambda: None):
    count = len(lanes[0])
    groups = [range(first, min(first + size, count)) for first in range(0, count, size)]

    def dots_of(number, place):
        if not accs:
            return [dot_rows(lane[place][...], rows[...]) for lane in lanes]
        at = number % 2 * size + place % size
        return [pltpu.matmul_pop(acc[at])[:, : rows.shape[0]] for acc in accs]

    def read(number):
        for place in groups[number]:
            finish(place, dots_of(number, place))

    if not accs:
        meanwhile()
        held = pieces[0].shape[0]
        for number, piece in enumerate(pieces):
            rows[number * held : (number + 1) * held, :] = piece[...]
        for number in range(len(groups)):
            ready(number)
            read(number)
        return
    edge = accs[0][0].shape[1]
    steps = rows.shape[1] // edge

    def push(turn):
        first = turn % steps * edge
        parts = [piece[:, first : first + edge] for piece in pieces]
        both = jnp.concatenate(parts * (edge // rows.shape[0]), axis=0)
        for unit in range(len(lanes)):
            pltpu.matmul_push_rhs(both, turn % 2, unit, transpose=True)

    push(0)
    for turn in range(len(groups) * steps):
        number, step = divmod(turn, steps)
        if step == 0:
            ready(number)
        for place in groups[number]:
            for lane, acc in zip(lanes, accs):
                part = lane[place][:, step * edge : (step + 1) * edge]
                staged = turn % 2 if place == groups[number][0] else None
                pltpu.matmul_acc_lhs(acc[number % 2 * size + place % size], part, load_staged_rhs=staged)
            if place == groups[number][0] and turn + 1 < len(groups) * steps:
                push(turn + 1)
        if step == 0 and number > 0:
            read(number - 1)
        if turn == 1:
            meanwhile()
    read(len(groups) - 1)


def with_accs(kernel, shapes):
    if not shapes:
        return kernel
    half = len(shapes) // 2

    def body(*refs):
        pl.run_scoped(lambda *accs: kernel(*refs, accs=(accs[:half], accs[half:])), *shapes)

    return body


def place_rows(pieces, distances, rows):
    me = lax.axis_index("dp")
    tok_dev = pieces[0].shape[0]
    for piece, distance in zip(pieces, distances):
        start = pl.multiple_of(jnp.bitwise_xor(me, distance) * tok_dev, tok_dev)
        rows[pl.ds(start, tok_dev), :] = piece[...]


def start_loads(plan, sources, nears, sems):
    copies, number = [], 0
    for (first, last), source, near in zip(plan, sources, nears):
        for chunk in range(first, last):
            copies.append(pltpu.make_async_copy(source.at[chunk], near.at[chunk - first], sems.at[number]))
            number += 1
    for copy in copies:
        copy.start()
    return copies


def load_pack_kernel(plan, logits, routes, cotangent, gate, up, packed, gate_near, up_near, *scratch):
    logits_near, routes_near, columns, sems, load_sems = scratch
    model_width = cotangent.shape[1]
    copies = [
        pltpu.make_async_copy(logits, logits_near, sems.at[0]),
        pltpu.make_async_copy(routes, routes_near, sems.at[1]),
        pltpu.make_async_copy(cotangent, packed.at[:, :model_width], sems.at[2]),
    ]
    for copy in copies:
        copy.start()
    loads = start_loads(plan, [gate, up], [gate_near, up_near], load_sems)
    columns[...] = jnp.zeros(columns.shape, jnp.float32)
    copies[0].wait()
    left = logits_near[...]
    experts_all = left.shape[1]
    for term in range(3):
        rounded = left.astype(jnp.bfloat16).astype(jnp.float32)
        columns[:, term * experts_all : (term + 1) * experts_all] = rounded
        left = left - rounded
    copies[1].wait()
    columns[:, 3 * experts_all : 3 * experts_all + routes.shape[0]] = routes_near[...].astype(jnp.float32).T
    packed[:, model_width:] = columns[...].astype(jnp.bfloat16)
    copies[2].wait()
    for copy in loads:
        copy.wait()


def blocks_of(buffers, unit):
    return [
        buffer.at[chunk, first : first + unit]
        for buffer in buffers
        for chunk in range(buffer.shape[0])
        for first in range(0, buffer.shape[1], unit)
    ]


def gated(dots):
    gate_pre, up_pre = dots
    return gate_pre / (1.0 + jnp.exp(-gate_pre)) * up_pre


def stream_hidden(pieces, rows, lanes, size, accs, ready, hidden):
    def finish(place, dots):
        gate_pre, up_pre = dots
        hidden[place] = gate_pre / (1.0 + jnp.exp(-gate_pre)) * up_pre

    stream_dots(pieces, rows, lanes, size, accs, ready, finish)


def first_hidden_kernel(distances, plan, size, *refs, accs=()):
    count = len(distances)
    pieces, refs = refs[:count], refs[count:]
    gate, up, gate_far, up_far, hidden, mine, gate_last, up_last, rows, gate_mid, up_mid, sems, mine_sems = refs
    loads = start_loads(
        plan, [gate_far, up_far, gate_far, up_far], [gate_mid, up_mid, gate_last, up_last], sems
    )
    me = lax.axis_index("dp")
    width, held = mine.shape[1], pieces[0].shape[0]
    columns = pl.ds(pl.multiple_of(me * width, width), width)
    own = []
    for number, piece in enumerate(pieces):
        start = pl.multiple_of(jnp.bitwise_xor(me, distances[number]) * held, held)
        own.append(pltpu.make_async_copy(piece.at[:, columns], mine.at[pl.ds(start, held)], mine_sems.at[number]))
        own[number].start()
    unit = hidden.shape[1]
    lanes = [blocks_of([gate, gate_mid], unit), blocks_of([up, up_mid], unit)]
    there = gate.shape[0] * gate.shape[1] // unit
    waited = [0]

    def ready(group):
        if (group + 1) * size > there and waited[0] == 0:
            waited[0] = gate_mid.shape[0] + up_mid.shape[0]
            for copy in loads[: waited[0]]:
                copy.wait()

    stream_hidden(pieces, rows, lanes, size, accs, ready, hidden)
    for copy in own + loads[waited[0] :]:
        copy.wait()


def second_hidden_kernel(count, size, *refs, accs=()):
    pieces, (gate, up, after, hidden, rows) = refs[:count], refs[count:]
    unit = hidden.shape[1]
    lanes = [blocks_of([gate], unit), blocks_of([up], unit)]
    stream_hidden(pieces, rows, lanes, size, accs, lambda group: None, hidden)


def token_order(lines, count):
    me = lax.axis_index("dp")
    tokens = lines.shape[1]
    lane = lax.broadcasted_iota(jnp.int32, lines.shape, 1)
    distance = 1
    while distance < count:
        step = distance * (tokens // count)
        above, below = pltpu.roll(lines, tokens - step, 1), pltpu.roll(lines, step, 1)
        swapped = jnp.where(jnp.bitwise_and(lane, step) == 0, above, below)
        lines = jnp.where(jnp.bitwise_and(me, distance) != 0, swapped, lines)
        distance *= 2
    return lines


def score_kernel(distances, top, *refs, accs=()):
    count = len(distances)
    pieces, refs = refs[:count], refs[count:]
    hidden_0, hidden_1, down, partial, probs, chosen, rows, routing_rows = refs
    model_width = down.shape[2]
    experts_all = probs.shape[0]
    place_rows([piece.at[:, model_width:] for piece in pieces], distances, routing_rows)
    local_experts = partial.shape[1]
    blocks = blocks_of([down], hidden_0.shape[1])
    hidden = [held.at[place] for held in (hidden_0, hidden_1) for place in range(held.shape[0])]
    per_expert = len(blocks) // local_experts
    size = len(blocks) // 4
    order = [
        [group * 2 * size + lane * size + place for group in range(2) for place in range(size)] for lane in range(2)
    ]
    sums = [None] * local_experts

    def routing():
        packed = routing_rows[...].astype(jnp.float32).T
        terms = [packed[term * experts_all : (term + 1) * experts_all] for term in range(3)]
        logits = terms[0] + terms[1] + terms[2]
        raised = jnp.exp(logits - jnp.max(logits, axis=0, keepdims=True))
        probs[...] = raised / jnp.sum(raised, axis=0, keepdims=True)
        number = lax.broadcasted_iota(jnp.int32, logits.shape, 0).astype(jnp.float32)
        named = jnp.zeros(logits.shape, jnp.float32)
        for slot in range(3 * experts_all, 3 * experts_all + top):
            named = named + (packed[slot : slot + 1] == number).astype(jnp.float32)
        chosen[...] = named

    def finish(place, dots):
        for lane, paired in zip(order, dots):
            block = lane[place]
            product = hidden[block][...] * paired
            expert = block // per_expert
            sums[expert] = product if sums[expert] is None else sums[expert] + product

    lanes = [[blocks[block] for block in lane] for lane in order]
    stream_dots([piece.at[:, :model_width] for piece in pieces], rows, lanes, 2 * size, accs, lambda group: None, finish, routing)
    lines = [jnp.sum(term, axis=0, keepdims=True) for term in sums]
    scores = token_order(jnp.concatenate(lines, axis=0), count)
    partial[...] = jnp.broadcast_to(scores[None], partial.shape)


def gradient_kernel(data_count, blocks, probs_ref, chosen_ref, mine, logit_grad, router_grad, grads, held, sems):
    experts_all, total_tokens = probs_ref.shape
    scores = jnp.sum(blocks[...].reshape((data_count, experts_all, total_tokens)), axis=0)
    probs, chosen = probs_ref[...], chosen_ref[...]
    mass = jnp.sum(probs * chosen, axis=0, keepdims=True)
    weighted = jnp.sum(probs * chosen * scores, axis=0, keepdims=True)
    total = jnp.sum(probs * scores, axis=0, keepdims=True) / mass - mass * weighted / (mass * mass)
    prob_grad = scores / mass - chosen * weighted / (mass * mass)
    grad = probs * (prob_grad - total)
    half = mine.shape[1] // 2
    copies = []
    for number in range(2):
        part = pl.ds(number * half, half)
        held[:, part] = jnp.dot(grad.astype(jnp.bfloat16), mine[:, part], preferred_element_type=jnp.float32)
        copies.append(pltpu.make_async_copy(held.at[:, part], router_grad.at[:, part], sems.at[number]))
        copies[number].start()
    grads[...] = grad.T
    tok_dev = logit_grad.shape[0]
    start = pl.multiple_of(lax.axis_index("dp") * tok_dev, tok_dev)
    copies.append(pltpu.make_async_copy(grads.at[pl.ds(start, tok_dev)], logit_grad, sems.at[2]))
    copies[2].start()
    for copy in copies:
        copy.wait()


def swap(value, axis, distance):
    return lax.ppermute(value, axis, [(index, index ^ distance) for index in range(lax.axis_size(axis))])


def per_device(tokens, cotangent, logits, routes, gate_weight, up_weight, down_weight):
    data_count = lax.axis_size("dp")
    expert_count = lax.axis_size("expert")
    tok_dev, model_width = tokens.shape
    local_experts, ff_dev = gate_weight.shape[:2]
    total_tokens = tok_dev * data_count
    experts_all = local_experts * expert_count
    top = routes.shape[1]
    unit = 128 if ff_dev % 128 == 0 else ff_dev
    units = local_experts * ff_dev // unit
    chunk_rows = unit * (2 if unit == 128 and units % 2 == 0 else 1)
    chunks = local_experts * ff_dev // chunk_rows
    extra = -(-(3 * experts_all + top) // 128) * 128
    chips = data_count // CORES
    distances = [chip * CORES + core for chip in range(chips) for core in range(CORES)]
    first = 2 * chunks // 3

    vmem = pl.BlockSpec(memory_space=pltpu.VMEM)
    hbm = pl.BlockSpec(memory_space=pltpu.HBM)
    anywhere = pl.BlockSpec(memory_space=pl.ANY)
    row_bytes = total_tokens * model_width * 2

    def keep_far(value):
        return pltpu.with_memory_space_constraint(value, pltpu.HBM)

    def near(first, last):
        return pltpu.VMEM((last - first, chunk_rows, model_width), jnp.bfloat16)

    def cost(loads, dots):
        return pl.CostEstimate(flops=dots, bytes_accessed=loads, transcendentals=0)

    def scoped(size):
        return pltpu.CompilerParams(vmem_limit_bytes=size + (2 << 20))

    edge = pltpu.get_tpu_info().mxu_column_size
    accs = []
    size = units // 3 if units % 3 == 0 else 1

    def accs(count):
        if edge != 2 * total_tokens or model_width % edge != 0 or 2 * count * unit > 1024 or units % 12 != 0:
            return []
        return [pltpu.ACC(number)((unit, edge), jnp.float32) for number in range(2) for _ in range(2 * count)]

    cut = (chunks, chunk_rows, model_width)
    gate, up = (keep_far(weight.reshape(cut)) for weight in (gate_weight, up_weight))
    down = pltpu.with_memory_space_constraint(down_weight.reshape(cut), pltpu.VMEM)

    tokens_beside = swap(tokens, "dp", 1)
    tokens_far = [swap(tokens, "dp", chip * CORES) for chip in range(1, chips)]
    plan = [(0, first), (0, first)]
    packed, gate_near, up_near = pl.pallas_call(
        functools.partial(load_pack_kernel, plan),
        out_shape=(
            jax.ShapeDtypeStruct((tok_dev, model_width + extra), jnp.bfloat16),
            near(*plan[0]),
            near(*plan[1]),
        ),
        in_specs=[hbm] * 5,
        out_specs=(vmem,) * 3,
        scratch_shapes=[
            pltpu.VMEM((tok_dev, experts_all), jnp.float32),
            pltpu.VMEM((top, tok_dev), jnp.int32),
            pltpu.VMEM((tok_dev, extra), jnp.float32),
            pltpu.SemaphoreType.DMA((3,)),
            pltpu.SemaphoreType.DMA((2 * first,)),
        ],
        compiler_params=scoped(0),
        cost_estimate=cost(2 * first, 0),
        name="load_pack",
    )(keep_far(logits), keep_far(routes.T), keep_far(cotangent), gate, up)
    packed_far = [swap(packed, "dp", chip * CORES) for chip in range(1, chips)]
    packed_beside = swap(packed, "dp", 1)
    tokens_far, gate_near, up_near = lax.optimization_barrier((tokens_far, gate_near, up_near))
    token_pieces = [tokens, tokens_beside]
    for far in tokens_far:
        token_pieces += [far, swap(far, "dp", 1)]
    plan = [(first, chunks - 1), (first, chunks - 1), (chunks - 1, chunks), (chunks - 1, chunks)]
    loads = 2 * (chunks - first)
    places = units // chunks
    rows_scratch = pltpu.VMEM((total_tokens, model_width), jnp.bfloat16)
    hidden_0, mine, gate_last, up_last = pl.pallas_call(
        with_accs(functools.partial(first_hidden_kernel, distances, plan, size), accs(size)),
        out_shape=(
            jax.ShapeDtypeStruct((units - places, unit, total_tokens), jnp.float32),
            jax.ShapeDtypeStruct((total_tokens, model_width // data_count), jnp.bfloat16),
            near(*plan[2]),
            near(*plan[3]),
        ),
        in_specs=[vmem] * (data_count + 2) + [hbm] * 2,
        out_specs=(vmem,) * 4,
        scratch_shapes=[
            rows_scratch,
            near(*plan[0]),
            near(*plan[1]),
            pltpu.SemaphoreType.DMA((loads,)),
            pltpu.SemaphoreType.DMA((data_count,)),
        ],
        compiler_params=scoped(loads * cut[1] * cut[2] * 2 + (1 if accs(size) else 3) * row_bytes),
        cost_estimate=cost(loads, 2 * chunks),
        name="hidden_first",
    )(*token_pieces, gate_near, up_near, gate, up)

    packed_far, hidden_0 = lax.optimization_barrier((packed_far, hidden_0))
    hidden_1 = pl.pallas_call(
        with_accs(functools.partial(second_hidden_kernel, data_count, size), accs(size)),
        out_shape=jax.ShapeDtypeStruct((places, unit, total_tokens), jnp.float32),
        in_specs=[vmem] * (data_count + 2) + [anywhere],
        out_specs=vmem,
        scratch_shapes=[rows_scratch],
        compiler_params=scoped((1 if accs(size) else 3) * row_bytes),
        cost_estimate=cost(1, 2),
        name="hidden_second",
    )(*token_pieces, gate_last, up_last, packed_far[0])

    packed_pieces = [packed, packed_beside]
    for far in packed_far:
        packed_pieces += [far, swap(far, "dp", 1)]
    table = jax.ShapeDtypeStruct((experts_all, total_tokens), jnp.float32)
    partial, probs, chosen = pl.pallas_call(
        with_accs(functools.partial(score_kernel, distances, top), accs(units // 4)),
        out_shape=(
            jax.ShapeDtypeStruct((data_count * expert_count, local_experts, total_tokens), jnp.float32),
            table,
            table,
        ),
        in_specs=[vmem] * (data_count + 3),
        out_specs=(vmem, vmem, vmem),
        scratch_shapes=[
            rows_scratch,
            pltpu.VMEM((total_tokens, extra), jnp.bfloat16),
        ],
        compiler_params=scoped(3 * row_bytes),
        cost_estimate=cost(1, 1),
        name="scores",
    )(*packed_pieces, hidden_0, hidden_1, down)

    score_blocks = lax.all_to_all(partial, ("dp", "expert"), split_axis=0, concat_axis=0, tiled=True)

    logit_grad, router_grad = pl.pallas_call(
        functools.partial(gradient_kernel, data_count),
        out_shape=(
            jax.ShapeDtypeStruct((tok_dev, experts_all), jnp.float32),
            jax.ShapeDtypeStruct((experts_all, model_width // data_count), jnp.float32),
        ),
        in_specs=[vmem] * 4,
        out_specs=(hbm, hbm),
        scratch_shapes=[
            pltpu.VMEM((total_tokens, experts_all), jnp.float32),
            pltpu.VMEM((experts_all, model_width // data_count), jnp.float32),
            pltpu.SemaphoreType.DMA((3,)),
        ],
        compiler_params=scoped(4 << 20),
        name="gradient",
    )(score_blocks, probs, chosen, mine)
    return logit_grad, router_grad.T


def solution(mesh):
    placed = (
        P("dp", None),
        P("dp", None),
        P("dp", None),
        P("dp", None),
        P("expert", "dp", None),
        P("expert", "dp", None),
        P("expert", "dp", None),
    )
    mapped = jax.shard_map(
        per_device,
        mesh=mesh,
        in_specs=placed,
        out_specs=(P("dp", None), P("dp", None)),
        check_vma=False,
    )

    def run(*args):
        with jax.sharding.use_abstract_mesh(mesh.abstract_mesh):
            return mapped(*args)

    return run
```

```python
import functools

import jax
import jax.numpy as jnp
from jax import lax
from jax.experimental import pallas as pl
from jax.experimental.pallas import tpu as pltpu
from jax.sharding import PartitionSpec as P

CORES = 2


def dot_rows(a, b):
    return lax.dot_general(a, b, (((1,), (1,)), ((), ())), preferred_element_type=jnp.float32)


def stream_dots(pieces, rows, lanes, size, accs, ready, finish):
    count = len(lanes[0])
    groups = [range(first, min(first + size, count)) for first in range(0, count, size)]

    def dots_of(number, place):
        if not accs:
            return [dot_rows(lane[place][...], rows[...]) for lane in lanes]
        at = number % 2 * size + place % size
        return [pltpu.matmul_pop(acc[at])[:, : rows.shape[0]] for acc in accs]

    def read(number):
        for place in groups[number]:
            finish(place, dots_of(number, place))

    if not accs:
        held = pieces[0].shape[0]
        for number, piece in enumerate(pieces):
            rows[number * held : (number + 1) * held, :] = piece[...]
        for number in range(len(groups)):
            ready(number)
            read(number)
        return
    edge = accs[0][0].shape[1]
    steps = rows.shape[1] // edge

    def push(turn):
        first = turn % steps * edge
        parts = [piece[:, first : first + edge] for piece in pieces]
        both = jnp.concatenate(parts * (edge // rows.shape[0]), axis=0)
        for unit in range(len(lanes)):
            pltpu.matmul_push_rhs(both, turn % 2, unit, transpose=True)

    push(0)
    for turn in range(len(groups) * steps):
        number, step = divmod(turn, steps)
        if step == 0:
            ready(number)
        for place in groups[number]:
            for lane, acc in zip(lanes, accs):
                part = lane[place][:, step * edge : (step + 1) * edge]
                staged = turn % 2 if place == groups[number][0] else None
                pltpu.matmul_acc_lhs(acc[number % 2 * size + place % size], part, load_staged_rhs=staged)
            if place == groups[number][0] and turn + 1 < len(groups) * steps:
                push(turn + 1)
        if step == 0 and number > 0:
            read(number - 1)
    read(len(groups) - 1)


def with_accs(kernel, shapes):
    if not shapes:
        return kernel
    half = len(shapes) // 2

    def body(*refs):
        pl.run_scoped(lambda *accs: kernel(*refs, accs=(accs[:half], accs[half:])), *shapes)

    return body


def place_rows(pieces, distances, rows):
    me = lax.axis_index("dp")
    tok_dev = pieces[0].shape[0]
    for piece, distance in zip(pieces, distances):
        start = pl.multiple_of(jnp.bitwise_xor(me, distance) * tok_dev, tok_dev)
        rows[pl.ds(start, tok_dev), :] = piece[...]


def start_loads(plan, sources, nears, sems, most=None):
    copies, number = [], 0
    for (first, last), source, near in zip(plan, sources, nears):
        for chunk in range(first, last):
            copies.append(pltpu.make_async_copy(source.at[chunk], near.at[chunk - first], sems.at[number]))
            number += 1
    for copy in copies[:most]:
        copy.start()
    return copies


def load_pack_kernel(plan, logits, routes, cotangent, gate, up, packed, gate_near, up_near, *scratch):
    logits_near, routes_near, columns, sems, load_sems = scratch
    model_width = cotangent.shape[1]
    copies = [
        pltpu.make_async_copy(logits, logits_near, sems.at[0]),
        pltpu.make_async_copy(routes, routes_near, sems.at[1]),
        pltpu.make_async_copy(cotangent, packed.at[:, :model_width], sems.at[2]),
    ]
    for copy in copies:
        copy.start()
    most = 3
    loads = start_loads(plan, [gate, up], [gate_near, up_near], load_sems, most)
    columns[...] = jnp.zeros(columns.shape, jnp.float32)
    copies[0].wait()
    left = logits_near[...]
    experts_all = left.shape[1]
    for term in range(3):
        rounded = left.astype(jnp.bfloat16).astype(jnp.float32)
        columns[:, term * experts_all : (term + 1) * experts_all] = rounded
        left = left - rounded
    copies[1].wait()
    columns[:, 3 * experts_all : 3 * experts_all + routes.shape[0]] = routes_near[...].astype(jnp.float32).T
    packed[:, model_width:] = columns[...].astype(jnp.bfloat16)
    copies[2].wait()
    for number, copy in enumerate(loads):
        copy.wait()
        if number + most < len(loads):
            loads[number + most].start()


def blocks_of(buffers, unit):
    return [
        buffer.at[chunk, first : first + unit]
        for buffer in buffers
        for chunk in range(buffer.shape[0])
        for first in range(0, buffer.shape[1], unit)
    ]


def gated(dots):
    gate_pre, up_pre = dots
    return gate_pre / (1.0 + jnp.exp(-gate_pre)) * up_pre


def stream_hidden(pieces, rows, lanes, size, accs, ready, hidden):
    def finish(place, dots):
        gate_pre, up_pre = dots
        hidden[place] = gate_pre / (1.0 + jnp.exp(-gate_pre)) * up_pre

    stream_dots(pieces, rows, lanes, size, accs, ready, finish)


def first_hidden_kernel(distances, plan, size, *refs, accs=()):
    count = len(distances)
    pieces, refs = refs[:count], refs[count:]
    gate, up, gate_far, up_far, hidden, mine, gate_last, up_last, rows, gate_mid, up_mid, sems, mine_sems = refs
    loads = start_loads(
        plan, [gate_far, up_far, gate_far, up_far], [gate_mid, up_mid, gate_last, up_last], sems
    )
    me = lax.axis_index("dp")
    width, held = mine.shape[1], pieces[0].shape[0]
    columns = pl.ds(pl.multiple_of(me * width, width), width)
    own = []
    for number, piece in enumerate(pieces):
        start = pl.multiple_of(jnp.bitwise_xor(me, distances[number]) * held, held)
        own.append(pltpu.make_async_copy(piece.at[:, columns], mine.at[pl.ds(start, held)], mine_sems.at[number]))
        own[number].start()
    unit = hidden.shape[1]
    lanes = [blocks_of([gate, gate_mid], unit), blocks_of([up, up_mid], unit)]
    there = gate.shape[0] * gate.shape[1] // unit
    waited = [0]

    def ready(group):
        if (group + 1) * size > there and waited[0] == 0:
            waited[0] = gate_mid.shape[0] + up_mid.shape[0]
            for copy in loads[: waited[0]]:
                copy.wait()

    stream_hidden(pieces, rows, lanes, size, accs, ready, hidden)
    for copy in own + loads[waited[0] :]:
        copy.wait()


def second_hidden_kernel(count, size, *refs, accs=()):
    pieces, (gate, up, after, hidden, rows) = refs[:count], refs[count:]
    unit = hidden.shape[1]
    lanes = [blocks_of([gate], unit), blocks_of([up], unit)]
    stream_hidden(pieces, rows, lanes, size, accs, lambda group: None, hidden)


def token_order(lines, count):
    me = lax.axis_index("dp")
    tokens = lines.shape[1]
    lane = lax.broadcasted_iota(jnp.int32, lines.shape, 1)
    distance = 1
    while distance < count:
        step = distance * (tokens // count)
        above, below = pltpu.roll(lines, tokens - step, 1), pltpu.roll(lines, step, 1)
        swapped = jnp.where(jnp.bitwise_and(lane, step) == 0, above, below)
        lines = jnp.where(jnp.bitwise_and(me, distance) != 0, swapped, lines)
        distance *= 2
    return lines


def score_kernel(distances, top, *refs, accs=()):
    count = len(distances)
    pieces, refs = refs[:count], refs[count:]
    hidden_0, hidden_1, down, partial, probs, chosen, rows, routing_rows = refs
    model_width = down.shape[2]
    experts_all = probs.shape[0]
    place_rows([piece.at[:, model_width:] for piece in pieces], distances, routing_rows)
    local_experts = partial.shape[1]
    blocks = blocks_of([down], hidden_0.shape[1])
    hidden = [held.at[place] for held in (hidden_0, hidden_1) for place in range(held.shape[0])]
    per_expert = len(blocks) // local_experts
    size = len(blocks) // 4
    order = [
        [group * 2 * size + lane * size + place for group in range(2) for place in range(size)] for lane in range(2)
    ]
    sums = [None] * local_experts

    def routing():
        packed = routing_rows[...].astype(jnp.float32).T
        terms = [packed[term * experts_all : (term + 1) * experts_all] for term in range(3)]
        logits = terms[0] + terms[1] + terms[2]
        raised = jnp.exp(logits - jnp.max(logits, axis=0, keepdims=True))
        probs[...] = raised / jnp.sum(raised, axis=0, keepdims=True)
        number = lax.broadcasted_iota(jnp.int32, logits.shape, 0).astype(jnp.float32)
        named = jnp.zeros(logits.shape, jnp.float32)
        for slot in range(3 * experts_all, 3 * experts_all + top):
            named = named + (packed[slot : slot + 1] == number).astype(jnp.float32)
        chosen[...] = named

    def finish(place, dots):
        if place == 0:
            routing()
        for lane, paired in zip(order, dots):
            block = lane[place]
            product = hidden[block][...] * paired
            expert = block // per_expert
            sums[expert] = product if sums[expert] is None else sums[expert] + product

    lanes = [[blocks[block] for block in lane] for lane in order]
    stream_dots([piece.at[:, :model_width] for piece in pieces], rows, lanes, size, accs, lambda group: None, finish)
    lines = [jnp.sum(term, axis=0, keepdims=True) for term in sums]
    scores = token_order(jnp.concatenate(lines, axis=0), count)
    partial[...] = jnp.broadcast_to(scores[None], partial.shape)


def gradient_kernel(data_count, blocks, probs_ref, chosen_ref, mine, logit_grad, router_grad, grads, held, sems):
    experts_all, total_tokens = probs_ref.shape
    scores = jnp.sum(blocks[...].reshape((data_count, experts_all, total_tokens)), axis=0)
    probs, chosen = probs_ref[...], chosen_ref[...]
    mass = jnp.sum(probs * chosen, axis=0, keepdims=True)
    weighted = jnp.sum(probs * chosen * scores, axis=0, keepdims=True)
    prob_grad = scores / mass - chosen * weighted / (mass * mass)
    grad = probs * (prob_grad - jnp.sum(probs * prob_grad, axis=0, keepdims=True))
    half = mine.shape[1] // 2
    copies = []
    for number in range(2):
        part = pl.ds(number * half, half)
        held[:, part] = jnp.dot(grad.astype(jnp.bfloat16), mine[:, part], preferred_element_type=jnp.float32)
        copies.append(pltpu.make_async_copy(held.at[:, part], router_grad.at[:, part], sems.at[number]))
        copies[number].start()
    grads[...] = grad.T
    tok_dev = logit_grad.shape[0]
    start = pl.multiple_of(lax.axis_index("dp") * tok_dev, tok_dev)
    copies.append(pltpu.make_async_copy(grads.at[pl.ds(start, tok_dev)], logit_grad, sems.at[2]))
    copies[2].start()
    for copy in copies:
        copy.wait()


def swap(value, axis, distance):
    return lax.ppermute(value, axis, [(index, index ^ distance) for index in range(lax.axis_size(axis))])


def per_device(tokens, cotangent, logits, routes, gate_weight, up_weight, down_weight):
    data_count = lax.axis_size("dp")
    expert_count = lax.axis_size("expert")
    tok_dev, model_width = tokens.shape
    local_experts, ff_dev = gate_weight.shape[:2]
    total_tokens = tok_dev * data_count
    experts_all = local_experts * expert_count
    top = routes.shape[1]
    unit = 128 if ff_dev % 128 == 0 else ff_dev
    units = local_experts * ff_dev // unit
    chunk_rows = unit * (2 if unit == 128 and units % 2 == 0 else 1)
    chunks = local_experts * ff_dev // chunk_rows
    extra = -(-(3 * experts_all + top) // 128) * 128
    chips = data_count // CORES
    distances = [chip * CORES + core for chip in range(chips) for core in range(CORES)]
    first = 2 * chunks // 3

    vmem = pl.BlockSpec(memory_space=pltpu.VMEM)
    hbm = pl.BlockSpec(memory_space=pltpu.HBM)
    anywhere = pl.BlockSpec(memory_space=pl.ANY)
    row_bytes = total_tokens * model_width * 2

    def keep_far(value):
        return pltpu.with_memory_space_constraint(value, pltpu.HBM)

    def near(first, last):
        return pltpu.VMEM((last - first, chunk_rows, model_width), jnp.bfloat16)

    def cost(loads, dots):
        return pl.CostEstimate(flops=dots, bytes_accessed=loads, transcendentals=0)

    def scoped(size):
        return pltpu.CompilerParams(vmem_limit_bytes=size + (2 << 20))

    edge = pltpu.get_tpu_info().mxu_column_size
    accs = []
    size = units // 3 if units % 3 == 0 else 1

    def accs(count):
        if edge != 2 * total_tokens or model_width % edge != 0 or 2 * count * unit > 1024 or units % 12 != 0:
            return []
        return [pltpu.ACC(number)((unit, edge), jnp.float32) for number in range(2) for _ in range(2 * count)]

    cut = (chunks, chunk_rows, model_width)
    gate, up = (keep_far(weight.reshape(cut)) for weight in (gate_weight, up_weight))
    down = pltpu.with_memory_space_constraint(down_weight.reshape(cut), pltpu.VMEM)

    tokens_beside = swap(tokens, "dp", 1)
    tokens_far = [swap(tokens, "dp", chip * CORES) for chip in range(1, chips)]
    plan = [(0, first), (0, first)]
    packed, gate_near, up_near = pl.pallas_call(
        functools.partial(load_pack_kernel, plan),
        out_shape=(
            jax.ShapeDtypeStruct((tok_dev, model_width + extra), jnp.bfloat16),
            near(*plan[0]),
            near(*plan[1]),
        ),
        in_specs=[hbm] * 5,
        out_specs=(vmem,) * 3,
        scratch_shapes=[
            pltpu.VMEM((tok_dev, experts_all), jnp.float32),
            pltpu.VMEM((top, tok_dev), jnp.int32),
            pltpu.VMEM((tok_dev, extra), jnp.float32),
            pltpu.SemaphoreType.DMA((3,)),
            pltpu.SemaphoreType.DMA((2 * first,)),
        ],
        compiler_params=scoped(0),
        cost_estimate=cost(2 * first, 0),
        name="load_pack",
    )(keep_far(logits), keep_far(routes.T), keep_far(cotangent), gate, up)
    packed_far = [swap(packed, "dp", chip * CORES) for chip in range(1, chips)]
    packed_beside = swap(packed, "dp", 1)
    tokens_far, gate_near, up_near = lax.optimization_barrier((tokens_far, gate_near, up_near))
    token_pieces = [tokens, tokens_beside]
    for far in tokens_far:
        token_pieces += [far, swap(far, "dp", 1)]
    plan = [(first, chunks - 1), (first, chunks - 1), (chunks - 1, chunks), (chunks - 1, chunks)]
    loads = 2 * (chunks - first)
    places = units // chunks
    rows_scratch = pltpu.VMEM((total_tokens, model_width), jnp.bfloat16)
    hidden_0, mine, gate_last, up_last = pl.pallas_call(
        with_accs(functools.partial(first_hidden_kernel, distances, plan, size), accs(size)),
        out_shape=(
            jax.ShapeDtypeStruct((units - places, unit, total_tokens), jnp.float32),
            jax.ShapeDtypeStruct((total_tokens, model_width // data_count), jnp.bfloat16),
            near(*plan[2]),
            near(*plan[3]),
        ),
        in_specs=[vmem] * (data_count + 2) + [hbm] * 2,
        out_specs=(vmem,) * 4,
        scratch_shapes=[
            rows_scratch,
            near(*plan[0]),
            near(*plan[1]),
            pltpu.SemaphoreType.DMA((loads,)),
            pltpu.SemaphoreType.DMA((data_count,)),
        ],
        compiler_params=scoped(loads * cut[1] * cut[2] * 2 + (1 if accs(size) else 3) * row_bytes),
        cost_estimate=cost(loads, 2 * chunks),
        name="hidden_first",
    )(*token_pieces, gate_near, up_near, gate, up)

    packed_far, hidden_0 = lax.optimization_barrier((packed_far, hidden_0))
    hidden_1 = pl.pallas_call(
        with_accs(functools.partial(second_hidden_kernel, data_count, size), accs(size)),
        out_shape=jax.ShapeDtypeStruct((places, unit, total_tokens), jnp.float32),
        in_specs=[vmem] * (data_count + 2) + [anywhere],
        out_specs=vmem,
        scratch_shapes=[rows_scratch],
        compiler_params=scoped((1 if accs(size) else 3) * row_bytes),
        cost_estimate=cost(1, 2),
        name="hidden_second",
    )(*token_pieces, gate_last, up_last, packed_far[0])

    packed_pieces = [packed, packed_beside]
    for far in packed_far:
        packed_pieces += [far, swap(far, "dp", 1)]
    table = jax.ShapeDtypeStruct((experts_all, total_tokens), jnp.float32)
    partial, probs, chosen = pl.pallas_call(
        with_accs(functools.partial(score_kernel, distances, top), accs(units // 4)),
        out_shape=(
            jax.ShapeDtypeStruct((data_count * expert_count, local_experts, total_tokens), jnp.float32),
            table,
            table,
        ),
        in_specs=[vmem] * (data_count + 3),
        out_specs=(vmem, vmem, vmem),
        scratch_shapes=[
            rows_scratch,
            pltpu.VMEM((total_tokens, extra), jnp.bfloat16),
        ],
        compiler_params=scoped(3 * row_bytes),
        cost_estimate=cost(1, 1),
        name="scores",
    )(*packed_pieces, hidden_0, hidden_1, down)

    score_blocks = lax.all_to_all(partial, ("dp", "expert"), split_axis=0, concat_axis=0, tiled=True)

    logit_grad, router_grad = pl.pallas_call(
        functools.partial(gradient_kernel, data_count),
        out_shape=(
            jax.ShapeDtypeStruct((tok_dev, experts_all), jnp.float32),
            jax.ShapeDtypeStruct((experts_all, model_width // data_count), jnp.float32),
        ),
        in_specs=[vmem] * 4,
        out_specs=(hbm, hbm),
        scratch_shapes=[
            pltpu.VMEM((total_tokens, experts_all), jnp.float32),
            pltpu.VMEM((experts_all, model_width // data_count), jnp.float32),
            pltpu.SemaphoreType.DMA((3,)),
        ],
        compiler_params=scoped(4 << 20),
        name="gradient",
    )(score_blocks, probs, chosen, mine)
    return logit_grad, router_grad.T


def solution(mesh):
    placed = (
        P("dp", None),
        P("dp", None),
        P("dp", None),
        P("dp", None),
        P("expert", "dp", None),
        P("expert", "dp", None),
        P("expert", "dp", None),
    )
    mapped = jax.shard_map(
        per_device,
        mesh=mesh,
        in_specs=placed,
        out_specs=(P("dp", None), P("dp", None)),
        check_vma=False,
    )

    def run(*args):
        with jax.sharding.use_abstract_mesh(mesh.abstract_mesh):
            return mapped(*args)

    return run
```

```python
import functools

import jax
import jax.numpy as jnp
from jax import lax
from jax.experimental import pallas as pl
from jax.experimental.pallas import tpu as pltpu
from jax.sharding import PartitionSpec as P

CORES = 2


def dot_rows(a, b):
    return lax.dot_general(a, b, (((1,), (1,)), ((), ())), preferred_element_type=jnp.float32)


def stream_dots(pieces, rows, lanes, size, accs, ready, finish):
    count = len(lanes[0])
    groups = [range(first, min(first + size, count)) for first in range(0, count, size)]

    def dots_of(number, place):
        if not accs:
            return [dot_rows(lane[place][...], rows[...]) for lane in lanes]
        at = number % 2 * size + place % size
        return [pltpu.matmul_pop(acc[at])[:, : rows.shape[0]] for acc in accs]

    def read(number):
        for place in groups[number]:
            finish(place, dots_of(number, place))

    if not accs:
        held = pieces[0].shape[0]
        for number, piece in enumerate(pieces):
            rows[number * held : (number + 1) * held, :] = piece[...]
        for number in range(len(groups)):
            ready(number)
            read(number)
        return
    edge = accs[0][0].shape[1]
    steps = rows.shape[1] // edge

    def push(turn):
        first = turn % steps * edge
        parts = [piece[:, first : first + edge] for piece in pieces]
        both = jnp.concatenate(parts * (edge // rows.shape[0]), axis=0)
        for unit in range(len(lanes)):
            pltpu.matmul_push_rhs(both, turn % 2, unit, transpose=True)

    push(0)
    for turn in range(len(groups) * steps):
        number, step = divmod(turn, steps)
        if step == 0:
            ready(number)
        for place in groups[number]:
            for lane, acc in zip(lanes, accs):
                part = lane[place][:, step * edge : (step + 1) * edge]
                staged = turn % 2 if place == groups[number][0] else None
                pltpu.matmul_acc_lhs(acc[number % 2 * size + place % size], part, load_staged_rhs=staged)
            if place == groups[number][0] and turn + 1 < len(groups) * steps:
                push(turn + 1)
        if step == 0 and number > 0:
            read(number - 1)
    read(len(groups) - 1)


def with_accs(kernel, shapes):
    if not shapes:
        return kernel
    half = len(shapes) // 2

    def body(*refs):
        pl.run_scoped(lambda *accs: kernel(*refs, accs=(accs[:half], accs[half:])), *shapes)

    return body


def place_rows(pieces, distances, rows):
    me = lax.axis_index("dp")
    tok_dev = pieces[0].shape[0]
    for piece, distance in zip(pieces, distances):
        start = pl.multiple_of(jnp.bitwise_xor(me, distance) * tok_dev, tok_dev)
        rows[pl.ds(start, tok_dev), :] = piece[...]


def start_loads(plan, sources, nears, sems):
    copies, number = [], 0
    for (first, last), source, near in zip(plan, sources, nears):
        for chunk in range(first, last):
            copies.append(pltpu.make_async_copy(source.at[chunk], near.at[chunk - first], sems.at[number]))
            number += 1
    for copy in copies:
        copy.start()
    return copies


def load_pack_kernel(plan, logits, routes, cotangent, gate, up, packed, gate_near, up_near, *scratch):
    logits_near, routes_near, columns, sems, load_sems = scratch
    model_width = cotangent.shape[1]
    copies = [
        pltpu.make_async_copy(logits, logits_near, sems.at[0]),
        pltpu.make_async_copy(routes, routes_near, sems.at[1]),
        pltpu.make_async_copy(cotangent, packed.at[:, :model_width], sems.at[2]),
    ]
    for copy in copies:
        copy.start()
    loads = start_loads(plan, [gate, up], [gate_near, up_near], load_sems)
    columns[...] = jnp.zeros(columns.shape, jnp.float32)
    copies[0].wait()
    left = logits_near[...]
    experts_all = left.shape[1]
    for term in range(3):
        rounded = left.astype(jnp.bfloat16).astype(jnp.float32)
        columns[:, term * experts_all : (term + 1) * experts_all] = rounded
        left = left - rounded
    copies[1].wait()
    columns[:, 3 * experts_all : 3 * experts_all + routes.shape[0]] = routes_near[...].astype(jnp.float32).T
    packed[:, model_width:] = columns[...].astype(jnp.bfloat16)
    copies[2].wait()
    for copy in loads:
        copy.wait()


def blocks_of(buffers, unit):
    return [
        buffer.at[chunk, first : first + unit]
        for buffer in buffers
        for chunk in range(buffer.shape[0])
        for first in range(0, buffer.shape[1], unit)
    ]


def gated(dots):
    gate_pre, up_pre = dots
    return gate_pre / (1.0 + jnp.exp(-gate_pre)) * up_pre


def stream_hidden(pieces, rows, lanes, size, accs, ready, hidden):
    def finish(place, dots):
        gate_pre, up_pre = dots
        hidden[place] = gate_pre / (1.0 + jnp.exp(-gate_pre)) * up_pre

    stream_dots(pieces, rows, lanes, size, accs, ready, finish)


def first_hidden_kernel(distances, plan, size, *refs, accs=()):
    count = len(distances)
    pieces, refs = refs[:count], refs[count:]
    gate, up, gate_far, up_far, hidden, mine, gate_last, up_last, rows, gate_mid, up_mid, sems, mine_sems = refs
    loads = start_loads(
        plan, [gate_far, up_far, gate_far, up_far], [gate_mid, up_mid, gate_last, up_last], sems
    )
    me = lax.axis_index("dp")
    width, held = mine.shape[1], pieces[0].shape[0]
    columns = pl.ds(pl.multiple_of(me * width, width), width)
    own = []
    for number, piece in enumerate(pieces):
        start = pl.multiple_of(jnp.bitwise_xor(me, distances[number]) * held, held)
        own.append(pltpu.make_async_copy(piece.at[:, columns], mine.at[pl.ds(start, held)], mine_sems.at[number]))
        own[number].start()
    unit = hidden.shape[1]
    lanes = [blocks_of([gate, gate_mid], unit), blocks_of([up, up_mid], unit)]
    there = gate.shape[0] * gate.shape[1] // unit
    waited = [0]

    def ready(group):
        if (group + 1) * size > there and waited[0] == 0:
            waited[0] = gate_mid.shape[0] + up_mid.shape[0]
            for copy in loads[: waited[0]]:
                copy.wait()

    stream_hidden(pieces, rows, lanes, size, accs, ready, hidden)
    for copy in own + loads[waited[0] :]:
        copy.wait()


def second_hidden_kernel(count, size, *refs, accs=()):
    pieces, (gate, up, after, hidden, rows) = refs[:count], refs[count:]
    unit = hidden.shape[1]
    lanes = [blocks_of([gate], unit), blocks_of([up], unit)]
    stream_hidden(pieces, rows, lanes, size, accs, lambda group: None, hidden)


def token_order(lines, count):
    me = lax.axis_index("dp")
    tokens = lines.shape[1]
    lane = lax.broadcasted_iota(jnp.int32, lines.shape, 1)
    distance = 1
    while distance < count:
        step = distance * (tokens // count)
        above, below = pltpu.roll(lines, tokens - step, 1), pltpu.roll(lines, step, 1)
        swapped = jnp.where(jnp.bitwise_and(lane, step) == 0, above, below)
        lines = jnp.where(jnp.bitwise_and(me, distance) != 0, swapped, lines)
        distance *= 2
    return lines


def score_kernel(distances, top, *refs, accs=()):
    count = len(distances)
    pieces, refs = refs[:count], refs[count:]
    hidden_0, hidden_1, down, partial, probs, chosen, rows, routing_rows = refs
    model_width = down.shape[2]
    experts_all = probs.shape[0]
    place_rows([piece.at[:, model_width:] for piece in pieces], distances, routing_rows)
    local_experts = partial.shape[1]
    blocks = blocks_of([down], hidden_0.shape[1])
    hidden = [held.at[place] for held in (hidden_0, hidden_1) for place in range(held.shape[0])]
    per_expert = len(blocks) // local_experts
    size = len(blocks) // 4
    order = [
        [group * 2 * size + lane * size + place for group in range(2) for place in range(size)] for lane in range(2)
    ]
    sums = [None] * local_experts

    def routing():
        packed = routing_rows[...].astype(jnp.float32).T
        terms = [packed[term * experts_all : (term + 1) * experts_all] for term in range(3)]
        logits = terms[0] + terms[1] + terms[2]
        raised = jnp.exp(logits - jnp.max(logits, axis=0, keepdims=True))
        probs[...] = raised / jnp.sum(raised, axis=0, keepdims=True)
        number = lax.broadcasted_iota(jnp.int32, logits.shape, 0).astype(jnp.float32)
        named = jnp.zeros(logits.shape, jnp.float32)
        for slot in range(3 * experts_all, 3 * experts_all + top):
            named = named + (packed[slot : slot + 1] == number).astype(jnp.float32)
        chosen[...] = named

    def finish(place, dots):
        if place == 0:
            routing()
        for lane, paired in zip(order, dots):
            block = lane[place]
            product = hidden[block][...] * paired
            expert = block // per_expert
            sums[expert] = product if sums[expert] is None else sums[expert] + product

    lanes = [[blocks[block] for block in lane] for lane in order]
    stream_dots([piece.at[:, :model_width] for piece in pieces], rows, lanes, size, accs, lambda group: None, finish)
    lines = [jnp.sum(term, axis=0, keepdims=True) for term in sums]
    scores = token_order(jnp.concatenate(lines, axis=0), count)
    partial[...] = jnp.broadcast_to(scores[None], partial.shape)


def gradient_kernel(data_count, blocks, probs_ref, chosen_ref, mine, logit_grad, router_grad, grads, held, sems):
    experts_all, total_tokens = probs_ref.shape
    scores = jnp.sum(blocks[...].reshape((data_count, experts_all, total_tokens)), axis=0)
    probs, chosen = probs_ref[...], chosen_ref[...]
    mass = jnp.sum(probs * chosen, axis=0, keepdims=True)
    weighted = jnp.sum(probs * chosen * scores, axis=0, keepdims=True)
    prob_grad = scores / mass - chosen * weighted / (mass * mass)
    grad = probs * (prob_grad - jnp.sum(probs * prob_grad, axis=0, keepdims=True))
    half = mine.shape[1] // 2
    copies = []
    for number in range(2):
        part = pl.ds(number * half, half)
        held[:, part] = jnp.dot(grad.astype(jnp.bfloat16), mine[:, part], preferred_element_type=jnp.float32)
        copies.append(pltpu.make_async_copy(held.at[:, part], router_grad.at[:, part], sems.at[number]))
        copies[number].start()
    grads[...] = grad.T
    tok_dev = logit_grad.shape[0]
    start = pl.multiple_of(lax.axis_index("dp") * tok_dev, tok_dev)
    copies.append(pltpu.make_async_copy(grads.at[pl.ds(start, tok_dev)], logit_grad, sems.at[2]))
    copies[2].start()
    for copy in copies:
        copy.wait()


def swap(value, axis, distance):
    return lax.ppermute(value, axis, [(index, index ^ distance) for index in range(lax.axis_size(axis))])


def per_device(tokens, cotangent, logits, routes, gate_weight, up_weight, down_weight):
    data_count = lax.axis_size("dp")
    expert_count = lax.axis_size("expert")
    tok_dev, model_width = tokens.shape
    local_experts, ff_dev = gate_weight.shape[:2]
    total_tokens = tok_dev * data_count
    experts_all = local_experts * expert_count
    top = routes.shape[1]
    unit = 128 if ff_dev % 128 == 0 else ff_dev
    units = local_experts * ff_dev // unit
    chunk_rows = unit * (2 if unit == 128 and units % 2 == 0 else 1)
    chunks = local_experts * ff_dev // chunk_rows
    extra = -(-(3 * experts_all + top) // 128) * 128
    chips = data_count // CORES
    distances = [chip * CORES + core for chip in range(chips) for core in range(CORES)]
    first = 2 * chunks // 3

    vmem = pl.BlockSpec(memory_space=pltpu.VMEM)
    hbm = pl.BlockSpec(memory_space=pltpu.HBM)
    anywhere = pl.BlockSpec(memory_space=pl.ANY)
    row_bytes = total_tokens * model_width * 2

    def keep_far(value):
        return pltpu.with_memory_space_constraint(value, pltpu.HBM)

    def near(first, last):
        return pltpu.VMEM((last - first, chunk_rows, model_width), jnp.bfloat16)

    def cost(loads, dots):
        return pl.CostEstimate(flops=dots, bytes_accessed=loads, transcendentals=0)

    def scoped(size):
        return pltpu.CompilerParams(vmem_limit_bytes=size + (2 << 20))

    edge = pltpu.get_tpu_info().mxu_column_size
    accs = []
    size = units // 3 if units % 3 == 0 else 1

    def accs(count):
        if edge != 2 * total_tokens or model_width % edge != 0 or 2 * count * unit > 1024 or units % 12 != 0:
            return []
        return [pltpu.ACC(number)((unit, edge), jnp.float32) for number in range(2) for _ in range(2 * count)]

    cut = (chunks, chunk_rows, model_width)
    gate, up = (keep_far(weight.reshape(cut)) for weight in (gate_weight, up_weight))
    down = pltpu.with_memory_space_constraint(down_weight.reshape(cut), pltpu.VMEM)

    tokens_beside = swap(tokens, "dp", 1)
    tokens_far = [swap(tokens, "dp", chip * CORES) for chip in range(1, chips)]
    plan = [(0, first), (0, first)]
    packed, gate_near, up_near = pl.pallas_call(
        functools.partial(load_pack_kernel, plan),
        out_shape=(
            jax.ShapeDtypeStruct((tok_dev, model_width + extra), jnp.bfloat16),
            near(*plan[0]),
            near(*plan[1]),
        ),
        in_specs=[hbm] * 5,
        out_specs=(vmem,) * 3,
        scratch_shapes=[
            pltpu.VMEM((tok_dev, experts_all), jnp.float32),
            pltpu.VMEM((top, tok_dev), jnp.int32),
            pltpu.VMEM((tok_dev, extra), jnp.float32),
            pltpu.SemaphoreType.DMA((3,)),
            pltpu.SemaphoreType.DMA((2 * first,)),
        ],
        compiler_params=scoped(0),
        cost_estimate=cost(2 * first, 0),
        name="load_pack",
    )(keep_far(logits), keep_far(routes.T), keep_far(cotangent), gate, up)
    packed_far = [swap(packed, "dp", chip * CORES) for chip in range(1, chips)]
    tokens_far, gate_near, up_near = lax.optimization_barrier((tokens_far, gate_near, up_near))
    token_pieces = [tokens, tokens_beside]
    for far in tokens_far:
        token_pieces += [far, swap(far, "dp", 1)]
    plan = [(first, chunks - 1), (first, chunks - 1), (chunks - 1, chunks), (chunks - 1, chunks)]
    loads = 2 * (chunks - first)
    places = units // chunks
    rows_scratch = pltpu.VMEM((total_tokens, model_width), jnp.bfloat16)
    hidden_0, mine, gate_last, up_last = pl.pallas_call(
        with_accs(functools.partial(first_hidden_kernel, distances, plan, size), accs(size)),
        out_shape=(
            jax.ShapeDtypeStruct((units - places, unit, total_tokens), jnp.float32),
            jax.ShapeDtypeStruct((total_tokens, model_width // data_count), jnp.bfloat16),
            near(*plan[2]),
            near(*plan[3]),
        ),
        in_specs=[vmem] * (data_count + 2) + [hbm] * 2,
        out_specs=(vmem,) * 4,
        scratch_shapes=[
            rows_scratch,
            near(*plan[0]),
            near(*plan[1]),
            pltpu.SemaphoreType.DMA((loads,)),
            pltpu.SemaphoreType.DMA((data_count,)),
        ],
        compiler_params=scoped(loads * cut[1] * cut[2] * 2 + (1 if accs(size) else 3) * row_bytes),
        cost_estimate=cost(loads, 2 * chunks),
        name="hidden_first",
    )(*token_pieces, gate_near, up_near, gate, up)

    packed_far, packed_own, hidden_0 = lax.optimization_barrier((packed_far, packed, hidden_0))
    packed_beside = swap(packed_own, "dp", 1)
    hidden_1 = pl.pallas_call(
        with_accs(functools.partial(second_hidden_kernel, data_count, size), accs(size)),
        out_shape=jax.ShapeDtypeStruct((places, unit, total_tokens), jnp.float32),
        in_specs=[vmem] * (data_count + 2) + [anywhere],
        out_specs=vmem,
        scratch_shapes=[rows_scratch],
        compiler_params=scoped((1 if accs(size) else 3) * row_bytes),
        cost_estimate=cost(1, 2),
        name="hidden_second",
    )(*token_pieces, gate_last, up_last, packed_far[0])

    packed_pieces = [packed, packed_beside]
    for far in packed_far:
        packed_pieces += [far, swap(far, "dp", 1)]
    table = jax.ShapeDtypeStruct((experts_all, total_tokens), jnp.float32)
    partial, probs, chosen = pl.pallas_call(
        with_accs(functools.partial(score_kernel, distances, top), accs(units // 4)),
        out_shape=(
            jax.ShapeDtypeStruct((data_count * expert_count, local_experts, total_tokens), jnp.float32),
            table,
            table,
        ),
        in_specs=[vmem] * (data_count + 3),
        out_specs=(vmem, vmem, vmem),
        scratch_shapes=[
            rows_scratch,
            pltpu.VMEM((total_tokens, extra), jnp.bfloat16),
        ],
        compiler_params=scoped(3 * row_bytes),
        cost_estimate=cost(1, 1),
        name="scores",
    )(*packed_pieces, hidden_0, hidden_1, down)

    score_blocks = lax.all_to_all(partial, ("dp", "expert"), split_axis=0, concat_axis=0, tiled=True)

    logit_grad, router_grad = pl.pallas_call(
        functools.partial(gradient_kernel, data_count),
        out_shape=(
            jax.ShapeDtypeStruct((tok_dev, experts_all), jnp.float32),
            jax.ShapeDtypeStruct((experts_all, model_width // data_count), jnp.float32),
        ),
        in_specs=[vmem] * 4,
        out_specs=(hbm, hbm),
        scratch_shapes=[
            pltpu.VMEM((total_tokens, experts_all), jnp.float32),
            pltpu.VMEM((experts_all, model_width // data_count), jnp.float32),
            pltpu.SemaphoreType.DMA((3,)),
        ],
        compiler_params=scoped(4 << 20),
        name="gradient",
    )(score_blocks, probs, chosen, mine)
    return logit_grad, router_grad.T


def solution(mesh):
    placed = (
        P("dp", None),
        P("dp", None),
        P("dp", None),
        P("dp", None),
        P("expert", "dp", None),
        P("expert", "dp", None),
        P("expert", "dp", None),
    )
    mapped = jax.shard_map(
        per_device,
        mesh=mesh,
        in_specs=placed,
        out_specs=(P("dp", None), P("dp", None)),
        check_vma=False,
    )

    def run(*args):
        with jax.sharding.use_abstract_mesh(mesh.abstract_mesh):
            return mapped(*args)

    return run
```
